32 devices in a mesh: row: 4 (over z), col: 8 (over y, x, core).
Axes of the slice: x: 2, y: 2, z: 4, core: 2. Of those that a mesh axis runs over, the one named last changes fastest.
Arguments:
- amplitudes: bfloat16 [4096, 2048], P('row', 'col'), may hold values from -6 to 6
- amp_mask: int32 [32, 16], P('row', 'col'), may hold values 0 or 1
- integrals: bfloat16 [2048, 16384], P('row', 'col'), may hold values from -0.25 to 0.25
- int_tiles: int32 [4, 8, 32], P(None, 'col'), may hold values from 0 to 64, as said below
- pair_dest: int32 [4096], P('row'), may hold values from 0 to 7, as said below
Outputs:
- moved: bfloat16 [8192, 16384], P(('row', 'col'))
The draws below stay inside these ranges and needn't reach their ends.
Inputs may be any that keep to these rules, and one draw needn't show every extreme that they name: `int_tiles`: entry t of a list names the nonzero tile (t // 16, t mod 16) of that integral block; the entries naming tiles are distinct, the value 64 marks an empty entry, and some block has all 32 entries filled. `pair_dest`: within each row block of 1024 consecutive pairs no column index is named by more than 256 pairs, and one is named by exactly 256.
All inputs are finite; a program needn't handle non-finite values. No bound on the sum of `amp_mask` on one device may be relied on, other than what follows from the above.
Results may differ from the reference program's by a relative error of at most 0.001.
Values may be sent and summed in bfloat16 or wider, within the bound.
No kernel may reach another device: no remote copies, remote signals or barrier semaphores. Data moves between devices by JAX's collectives and lax.ppermute only.
A program may use at most 128 MiB of HBM per device.

```python
import jax
import jax.numpy as jnp
from jax import lax

TILE = 128
NTC = 16
GRID_ROWS = 4
GRID_COLS = 8
PAIR_DEV = 1024
PTILES = 32
P_SIZE = 4096
KT = 16
K = 2048
KRT = 4
NT = 128
N = 16384
BTILES = 64
NZMAX = 32
CAP = 256
SLOTS = 8192


def draw_int_tiles(key, part):
    blocks_all = GRID_ROWS * GRID_COLS
    count_key, full_key, order_key = jax.random.split(key, 3)
    counts = jax.random.randint(count_key, (blocks_all,), max(1, NZMAX // 4), NZMAX + 1)
    fullest = jax.random.randint(full_key, (), 0, blocks_all)
    counts = jnp.where(jnp.arange(blocks_all) == fullest, NZMAX, counts)
    order_keys = jax.random.split(order_key, blocks_all)

    def order_one(each_key):
        return jax.random.permutation(each_key, BTILES)
    orders = jax.vmap(order_one)(order_keys)
    chosen = orders[:, :NZMAX].astype(jnp.int32)
    slot_ids = jnp.arange(NZMAX)[None, :]
    listed = jnp.where(slot_ids < counts[:, None], chosen, BTILES)
    return listed.reshape(GRID_ROWS, GRID_COLS, NZMAX).astype(jnp.int32)


def draw_pair_dest(key, part):
    remaining = PAIR_DEV - CAP
    others = GRID_COLS - 1
    even_share = remaining // others
    leftover = remaining - even_share * others
    pair_count = others // 2
    busy_key, move_key, perm_key = jax.random.split(key, 3)
    busiest_all = jax.random.randint(busy_key, (GRID_ROWS,), 0, GRID_COLS)
    moves_all = jax.random.randint(move_key, (GRID_ROWS, pair_count), 0, even_share // 2 + 1)
    perm_keys = jax.random.split(perm_key, GRID_ROWS)

    def dest_row(row_key, busiest, moves):
        other_ids = jnp.arange(others)
        counts = even_share + (other_ids < leftover).astype(jnp.int32)
        transfer = jnp.zeros((others,), jnp.int32)
        transfer = transfer.at[0:2 * pair_count:2].add(moves)
        transfer = transfer.at[1:2 * pair_count:2].add(-moves)
        counts = counts + transfer
        bounds = jnp.cumsum(counts)
        positions = jnp.arange(remaining)
        chosen = jnp.sum((positions[:, None] >= bounds[None, :]).astype(jnp.int32), axis=1)
        chosen = chosen + (chosen >= busiest).astype(jnp.int32)
        labels = jnp.concatenate([jnp.full((CAP,), busiest, jnp.int32), chosen.astype(jnp.int32)])
        return jax.random.permutation(row_key, labels)
    shuffled = jax.vmap(dest_row)(perm_keys, busiest_all, moves_all)
    return shuffled.reshape(GRID_ROWS * PAIR_DEV).astype(jnp.int32)


def touch_ends(values, own_key, smallest, high):
    longest = values.shape.index(max(values.shape))
    spots = []
    for shift in (0, 1):
        where = [jax.random.randint(jax.random.fold_in(own_key, axis), (), 0, length) for axis, length in enumerate(values.shape)]
        where[longest] = (where[longest] + shift) % values.shape[longest]
        spots.append(tuple(where))
    return values.at[spots[0]].set(smallest).at[spots[1]].set(high)


def steps_of(rng, extent, pieces, low, largest):
    def one(axis_at, parts):
        draws = jax.random.uniform(jax.random.fold_in(jax.random.fold_in(rng, 6), axis_at), (parts,), jnp.float32, low / len(pieces), largest / len(pieces))
        return jnp.repeat(jnp.exp(draws), extent[axis_at] // parts).reshape((-1,) + (1,) * (len(extent) - axis_at - 1))

    factor_of = one(*pieces[0])
    for cut in pieces[1:]:
        factor_of = factor_of * one(*cut)
    return factor_of


def noise(stream_key, shape, scale, reach, pieces=(), kind=jnp.bfloat16):
    result = jax.random.normal(stream_key, shape, jnp.float32) * scale
    if len(pieces) > 0:
        result = steps_of(stream_key, shape, pieces, -0.22, 0.18) * result
    return jnp.clip(result, min=-reach, max=reach).astype(kind)


def setup_inputs(seed: int = 0) -> dict:
    arg_keys = jax.random.split(jax.random.key(seed), 6)
    return {
        "amplitudes": noise(arg_keys[0], (P_SIZE, K), 1.0, 6.0, ((0, 4), (1, 8))),
        "amp_mask": touch_ends((jax.random.randint(arg_keys[1], (PTILES, KT), 0, 2) < 1).astype(jnp.int32), jax.random.fold_in(arg_keys[1], 1), 0, 1),
        "integrals": noise(arg_keys[2], (K, N), (K // 4) ** -0.5, 0.25, ((0, 4), (1, 8))),
        "int_tiles": draw_int_tiles(jax.random.fold_in(arg_keys[5], 71), 0),
        "pair_dest": draw_pair_dest(jax.random.fold_in(arg_keys[5], 71), 0),
    }


def tile_mask(int_tiles):
    tile_ids = jnp.arange(BTILES, dtype=jnp.int32)
    present = jnp.any(int_tiles[:, :, :, None] == tile_ids[None, None, None, :], axis=2)
    present = present.reshape(GRID_ROWS, GRID_COLS, KRT, NTC).transpose(0, 2, 1, 3)
    return present.reshape(KT, NT)


def reference(amplitudes, amp_mask, integrals, int_tiles, pair_dest):
    amp_scale = amp_mask.astype(jnp.bfloat16)
    amp_used = (amplitudes.reshape(PTILES, TILE, KT, TILE) * amp_scale[:, None, :, None]).reshape(P_SIZE, K)
    int_scale = tile_mask(int_tiles).astype(jnp.bfloat16)
    int_used = (integrals.reshape(KT, TILE, NT, TILE) * int_scale[:, None, :, None]).reshape(K, N)

    def one_block(block_pair):
        pair_rows, targets = block_pair
        ladder = jnp.dot(pair_rows, int_used, preferred_element_type=jnp.float32).astype(jnp.bfloat16)
        col_ids = jnp.arange(GRID_COLS, dtype=jnp.int32)
        onehot = (targets[:, None] == col_ids[None, :]).astype(jnp.int32)
        before = jnp.cumsum(onehot, axis=0) - onehot
        slot_of = jnp.sum(before * onehot, axis=1)
        row_place = (targets * CAP + slot_of).astype(jnp.int32)
        return jnp.zeros((GRID_COLS * CAP, N), jnp.bfloat16).at[row_place].set(ladder)

    moved = lax.map(one_block, (amp_used.reshape(GRID_ROWS, PAIR_DEV, K), pair_dest.reshape(GRID_ROWS, PAIR_DEV)))
    return moved.reshape(SLOTS, N)
```

```python
import functools

import jax
import jax.numpy as jnp
from jax import lax
from jax.experimental import pallas as pl
from jax.experimental.pallas import tpu as pltpu
from jax.sharding import PartitionSpec as P

TILE = 128
MM_COLS = 512
DENSE_BUDGET = 48 << 20
VMEM_LIMIT = 48 << 20


def params():
    return pltpu.CompilerParams(vmem_limit_bytes=VMEM_LIMIT)


def pack_body(row_ref, ids_ref, src_ref, out_ref, sem):
    col_tiles = src_ref.shape[1] // TILE
    tiles = col_tiles * (src_ref.shape[0] // TILE)
    for e in range(out_ref.shape[0]):
        t = jnp.minimum(ids_ref[row_ref[0], e], tiles - 1)
        k = pl.multiple_of(lax.div(t, col_tiles) * TILE, TILE)
        n = pl.multiple_of(lax.rem(t, col_tiles) * TILE, TILE)
        pltpu.make_async_copy(src_ref.at[pl.ds(k, TILE), pl.ds(n, TILE)], out_ref.at[e], sem).start()
    pltpu.make_async_copy(out_ref, out_ref, sem).wait()


def pack(row, lists, integrals):
    count = lists.shape[1]
    return pl.pallas_call(
        pack_body,
        out_shape=jax.ShapeDtypeStruct((count, TILE, TILE), integrals.dtype),
        in_specs=[
            pl.BlockSpec(memory_space=pltpu.SMEM),
            pl.BlockSpec(memory_space=pltpu.SMEM),
            pl.BlockSpec(memory_space=pl.ANY),
        ],
        out_specs=pl.BlockSpec(memory_space=pltpu.VMEM),
        scratch_shapes=[pltpu.SemaphoreType.DMA],
        compiler_params=params(),
        name="pack_tiles",
    )(row, lists, integrals)


def densify_body(row_ref, ids_ref, packed_ref, *rest):
    out_ref = rest[-1]
    col_tiles = out_ref.shape[1] // TILE
    tiles = col_tiles * (out_ref.shape[0] // TILE)
    out_ref[...] = jnp.zeros_like(out_ref)
    for e in range(packed_ref.shape[0]):
        t = ids_ref[row_ref[0], e]

        @pl.when(t < tiles)
        def _():
            k = pl.multiple_of(lax.div(t, col_tiles) * TILE, TILE)
            n = pl.multiple_of(lax.rem(t, col_tiles) * TILE, TILE)
            out_ref[pl.ds(k, TILE), pl.ds(n, TILE)] = packed_ref[e]


def densify(row, lists, packed, dense, shape, block_rows):
    in_specs = [pl.BlockSpec(packed.shape, lambda i, r, l: (0, 0, 0))]
    operands = [row, lists, packed]
    aliases = {}
    if dense is not None:
        in_specs.append(pl.BlockSpec(memory_space=pl.ANY))
        operands.append(dense)
        aliases = {3: 0}
    return pl.pallas_call(
        densify_body,
        out_shape=jax.ShapeDtypeStruct(shape, packed.dtype),
        grid_spec=pltpu.PrefetchScalarGridSpec(
            num_scalar_prefetch=2,
            grid=(1,),
            in_specs=in_specs,
            out_specs=pl.BlockSpec((block_rows, shape[1]), lambda i, r, l: (r[0], 0)),
        ),
        input_output_aliases=aliases,
        compiler_params=params(),
        cost_estimate=pl.CostEstimate(flops=0, bytes_accessed=6 * block_rows * shape[1], transcendentals=0),
        name="densify",
    )(*operands)


def multiply_body(place_ref, lhs_ref, rhs_ref, *rest):
    out_ref = rest[-1]
    out_ref[...] = jnp.dot(lhs_ref[0], rhs_ref[...], preferred_element_type=jnp.float32).astype(out_ref.dtype)


def multiply(lhs, which, dense, whole=None, total_cols=None, place=None):
    _, m, k = lhs.shape
    n = dense.shape[1]
    width = min(MM_COLS, n)
    steps = n // width
    own = total_cols is None
    scalars = jnp.stack([which, jnp.int32(0) if own else place]).astype(jnp.int32)
    in_specs = [
        pl.BlockSpec((1, m, k), lambda i, s: (s[0], 0, 0)),
        pl.BlockSpec((k, width), lambda i, s: (0, i)),
    ]
    operands = [scalars, lhs, dense]
    aliases = {}
    if whole is not None:
        in_specs.append(pl.BlockSpec(memory_space=pl.ANY))
        operands.append(whole)
        aliases = {3: 0}
    return pl.pallas_call(
        multiply_body,
        out_shape=jax.ShapeDtypeStruct((m, n if own else total_cols), lhs.dtype),
        grid_spec=pltpu.PrefetchScalarGridSpec(
            num_scalar_prefetch=1,
            grid=(steps,),
            in_specs=in_specs,
            out_specs=pl.BlockSpec((m, width), lambda i, s: (0, s[1] * steps + i)),
        ),
        input_output_aliases=aliases,
        compiler_params=params(),
        cost_estimate=pl.CostEstimate(flops=2 * m * k * n, bytes_accessed=2 * (m * k + k * n + m * n), transcendentals=0),
        name="multiply",
    )(*operands)


def place_body(place_ref, piece_ref, whole_ref, out_ref):
    out_ref[...] = piece_ref[...]


def put(piece, whole, place):
    m, n = piece.shape
    width = min(2 * MM_COLS, n)
    steps = n // width
    return pl.pallas_call(
        place_body,
        out_shape=jax.ShapeDtypeStruct(whole.shape, whole.dtype),
        grid_spec=pltpu.PrefetchScalarGridSpec(
            num_scalar_prefetch=1,
            grid=(steps,),
            in_specs=[pl.BlockSpec((m, width), lambda i, s: (0, i)), pl.BlockSpec(memory_space=pl.ANY)],
            out_specs=pl.BlockSpec((m, width), lambda i, s: (0, s[0] * steps + i)),
        ),
        input_output_aliases={2: 0},
        compiler_params=params(),
        cost_estimate=pl.CostEstimate(flops=0, bytes_accessed=4 * m * n, transcendentals=0),
        name="put",
    )(place.astype(jnp.int32).reshape(1), piece, whole)


def col_index(ie, ia, ib, core):
    return ((ie * 2 + ia) * 2 + ib) * 2 + core


def on_device(amplitudes, amp_mask, integrals, int_tiles, pair_dest):
    rows = lax.axis_size("row")
    cols = lax.axis_size("col")
    extra = cols // 8
    pair_rows, amp_cols = amplitudes.shape
    int_rows, int_cols = integrals.shape
    capacity = 2 * pair_rows // cols
    panel_shape = (rows * int_rows, int_cols)
    z = lax.axis_index("row")
    me = lax.axis_index("col")
    core = lax.rem(me, 2)
    ib = lax.rem(lax.div(me, 2), 2)
    ia = lax.rem(lax.div(me, 4), 2)
    ie = lax.div(me, 8)
    every = [(e, a, b, c) for e in range(extra) for a in range(2) for b in range(2) for c in range(2)]

    own_lists = int_tiles[:, 0, :]
    packed = pack(z.astype(jnp.int32).reshape(1), own_lists, integrals)
    up, down = {0: packed}, {0: packed}
    for k in range(1, rows):
        up[k] = lax.ppermute(up[k - 1], "row", [(i + 1, i) for i in range(rows - k)])
        down[k] = lax.ppermute(down[k - 1], "row", [(i, i + 1) for i in range(k - 1, rows - 1)])

    order = []
    for i in range(rows):
        near = [(abs(r - i), 0 if (r > i) == (i < rows // 2) else 1, r - i) for r in range(rows) if r != i]
        order.append([(d, off > 0) for d, _, off in sorted(near)])
    slots, slot_row = [packed], [z]
    for j in range(rows - 1):
        kinds = sorted({order[i][j] for i in range(rows)})
        value, row = None, jnp.int32(0)
        for d, upward in kinds:
            here = functools.reduce(jnp.logical_or, [z == i for i in range(rows) if order[i][j] == (d, upward)])
            source = up[d] if upward else down[d]
            value = source if value is None else jnp.where(here, source, value)
            row = jnp.where(here, z + d if upward else z - d, row)
        slots.append(value)
        slot_row.append(row)
    slot_row = [r.astype(jnp.int32).reshape(1) for r in slot_row]

    along = [
        (col_index(e, a, b, c), col_index(e, a ^ (c == 1), b ^ (c == 0), c)) for e, a, b, c in every
    ]
    across = [(col_index(e, a, b, c), col_index(e, a, b, 1 - c)) for e, a, b, c in every]
    lists_next = lax.ppermute(own_lists, "col", along)
    pair_lists = lax.ppermute(jnp.concatenate([own_lists, lists_next], axis=0), "col", across)
    all_lists = [own_lists, lists_next, pair_lists[:rows], pair_lists[rows:]]
    blocks = [[], [], [], []]
    for slot in slots:
        mine_next = lax.ppermute(slot, "col", along)
        blocks[0].append(slot)
        blocks[1].append(mine_next)
        blocks[2].append(lax.ppermute(slot, "col", across))
        blocks[3].append(lax.ppermute(mine_next, "col", across))

    amp_scale = amp_mask.astype(jnp.bfloat16)
    amp_used = (
        amplitudes.reshape(amp_mask.shape[0], TILE, amp_mask.shape[1], TILE) * amp_scale[:, None, :, None]
    ).reshape(pair_rows, amp_cols)
    amp_all = lax.all_gather(amp_used, "col", axis=1, tiled=True)
    col_ids = jnp.arange(cols, dtype=jnp.int32)
    onehot = (pair_dest[:, None] == col_ids[None, :]).astype(jnp.int32)
    before = jnp.cumsum(onehot, axis=0) - onehot
    target = pair_dest * capacity + jnp.sum(before * onehot, axis=1)
    turns = [(de, da, db) for de in range(extra) for da, db in ((0, 0), (1, 0), (0, 1))]
    wanted = jnp.stack(
        [col_index(lax.rem(ie + de, extra), ia ^ da, ib ^ db, core) for de, da, db in turns]
    ).astype(jnp.int32)
    row_ids = (wanted[:, None] * capacity + jnp.arange(capacity, dtype=jnp.int32)[None, :]).reshape(-1)
    picker = (row_ids[:, None] == target[None, :]).astype(jnp.bfloat16)
    lhs = jnp.dot(picker, amp_all, preferred_element_type=jnp.bfloat16).reshape(len(turns), capacity, -1)

    live = 2 if 4 * panel_shape[0] * panel_shape[1] * 2 > DENSE_BUDGET else 4
    spare = []
    out = None
    total_cols = cols * int_cols
    arrived = []
    for q in (0, 2, 1, 3):
        dense = spare.pop(0) if len(spare) == live else None
        for slot, row in zip(blocks[q], slot_row):
            dense = densify(row, all_lists[q], slot, dense, panel_shape, int_rows)
        kind = core if q < 2 else 1 - core
        second = q % 2
        made = []
        for de in range(extra):
            for turn in (0, 1):
                if (de, turn) == (0, 0):
                    continue
                which = jnp.int32(3 * de) + turn * (1 + kind)
                piece = multiply(lhs, which, dense)
                made.append(piece)
                pairs = []
                for e, a, b, c in every:
                    to_kind = c if q < 2 else 1 - c
                    flip_a = turn if to_kind == 0 else 0
                    flip_b = turn if to_kind == 1 else 0
                    pairs.append(
                        (col_index(e, a, b, c), col_index((e + de) % extra, a ^ flip_a, b ^ flip_b, c))
                    )
                got = lax.ppermute(piece, "col", pairs)
                from_e = lax.rem(ie - de + extra, extra)
                swap = jnp.int32(turn)
                a_of = jnp.where(kind == 0, ia ^ swap, ia ^ second)
                b_of = jnp.where(kind == 0, ib ^ second, ib ^ swap)
                arrived.append((got, col_index(from_e, a_of, b_of, kind)))
        a_own = jnp.where(kind == 0, ia, ia ^ second)
        b_own = jnp.where(kind == 0, ib ^ second, ib)
        out = multiply(lhs, jnp.int32(0), dense, out, total_cols, col_index(ie, a_own, b_own, kind))
        if live < 4:
            dense, out, *_ = lax.optimization_barrier((dense, out, *made))
            spare.append(dense)
    for got, place in arrived:
        out = put(got, out, place)
    return out


def solution(mesh):
    in_specs = (P("row", "col"), P("row", "col"), P("row", "col"), P(None, "col", None), P("row"))
    out_specs = P(("row", "col"), None)
    return jax.shard_map(
        on_device, mesh=mesh, in_specs=in_specs, out_specs=out_specs, check_vma=False
    )
```

```python
import functools

import jax
import jax.numpy as jnp
from jax import lax
from jax.experimental import pallas as pl
from jax.experimental.pallas import tpu as pltpu
from jax.sharding import PartitionSpec as P

TILE = 128
MM_COLS = 512
VMEM_LIMIT = 63 << 20


def params():
    return pltpu.CompilerParams(vmem_limit_bytes=VMEM_LIMIT)


def pack_body(row_ref, ids_ref, src_ref, out_ref, sem):
    col_tiles = src_ref.shape[1] // TILE
    tiles = col_tiles * (src_ref.shape[0] // TILE)
    for e in range(out_ref.shape[0]):
        t = jnp.minimum(ids_ref[row_ref[0], e], tiles - 1)
        k = pl.multiple_of(lax.div(t, col_tiles) * TILE, TILE)
        n = pl.multiple_of(lax.rem(t, col_tiles) * TILE, TILE)
        pltpu.make_async_copy(src_ref.at[pl.ds(k, TILE), pl.ds(n, TILE)], out_ref.at[e], sem).start()
    pltpu.make_async_copy(out_ref, out_ref, sem).wait()


def pack(row, lists, integrals):
    count = lists.shape[1]
    return pl.pallas_call(
        pack_body,
        out_shape=jax.ShapeDtypeStruct((count, TILE, TILE), integrals.dtype),
        in_specs=[
            pl.BlockSpec(memory_space=pltpu.SMEM),
            pl.BlockSpec(memory_space=pltpu.SMEM),
            pl.BlockSpec(memory_space=pltpu.HBM),
        ],
        out_specs=pl.BlockSpec(memory_space=pltpu.VMEM),
        scratch_shapes=[pltpu.SemaphoreType.DMA],
        compiler_params=params(),
        name="pack_tiles",
    )(row, lists, integrals)


def partial_body(steps_of, scalars, table, *refs):
    lhs_count, slot_count, has_acc, final, has_whole = steps_of
    refs = list(refs)
    lhs = [[refs.pop(0) for _ in range(slot_count)] for _ in range(lhs_count)]
    packed = [refs.pop(0) for _ in range(slot_count)]
    acc = refs.pop(0) if has_acc else None
    if has_whole:
        refs.pop(0)
    outs, lhs_all, rhs_all = refs[:-2], refs[-2], refs[-1]
    step = pl.program_id(0)
    capacity, depth = lhs[0][0].shape[1:]
    width = rhs_all.shape[1]
    count = packed[0].shape[0]
    col_tiles = table.shape[1] // (depth // TILE)

    @pl.when(step == 0)
    def _():
        for t in range(lhs_count):
            for s in range(slot_count):
                lhs_all[t * capacity : (t + 1) * capacity, s * depth : (s + 1) * depth] = lhs[t][s][0]

    for s in range(slot_count):
        row = scalars[lhs_count + s]
        for k in range(depth // TILE):
            for n in range(width // TILE):
                e = table[row, k * col_tiles + step * (width // TILE) + n]
                tile = packed[s][jnp.minimum(e, count - 1)]
                rhs_all[s * depth + k * TILE : s * depth + (k + 1) * TILE, n * TILE : (n + 1) * TILE] = jnp.where(
                    e < count, tile, jnp.zeros_like(tile)
                )
    total = jnp.dot(lhs_all[...], rhs_all[...], preferred_element_type=jnp.float32)
    if has_acc:
        total = acc[...] + total
    if final:
        for t in range(lhs_count):
            outs[t][...] = total[t * capacity : (t + 1) * capacity].astype(outs[t].dtype)
    else:
        outs[0][...] = total


def partial(lhs, picks, table, slots, slot_rows, int_cols, acc=None, whole_cols=None, whole=None, place=None):
    _, capacity, _ = lhs.shape
    lhs_count, slot_count = len(picks), len(slots)
    m = lhs_count * capacity
    depth = table.shape[1] // (int_cols // TILE) * TILE
    width = min(MM_COLS, int_cols)
    steps = int_cols // width
    final = whole_cols is not None
    scalars = jnp.stack([*picks, *slot_rows, jnp.int32(0) if place is None else place]).astype(jnp.int32)
    last = lhs_count + slot_count

    def lhs_at(t, s):
        return lambda i, sc, tab: (sc[t], 0, sc[lhs_count + s])

    in_specs = [
        pl.BlockSpec((1, capacity, depth), lhs_at(t, s)) for t in range(lhs_count) for s in range(slot_count)
    ]
    in_specs += [pl.BlockSpec(slot.shape, lambda i, sc, tab: (0, 0, 0)) for slot in slots]
    operands = [scalars, table] + [lhs] * (lhs_count * slot_count) + list(slots)
    aliases = {}
    if acc is not None:
        in_specs.append(pl.BlockSpec((m, width), lambda i, sc, tab: (0, i)))
        operands.append(acc)
        if not final:
            aliases = {len(operands) - 1: 0}
    if whole is not None:
        in_specs.append(pl.BlockSpec(memory_space=pltpu.HBM))
        operands.append(whole)
        aliases = {len(operands) - 1: 0}
    if final:
        out_specs = [pl.BlockSpec((capacity, width), lambda i, sc, tab: (0, sc[last] * steps + i))]
        out_shape = [jax.ShapeDtypeStruct((capacity, whole_cols), lhs.dtype)]
        for _ in range(lhs_count - 1):
            out_specs.append(pl.BlockSpec((capacity, width), lambda i, sc, tab: (0, i)))
            out_shape.append(jax.ShapeDtypeStruct((capacity, int_cols), lhs.dtype))
    else:
        out_specs = [pl.BlockSpec((m, width), lambda i, sc, tab: (0, i))]
        out_shape = [jax.ShapeDtypeStruct((m, int_cols), jnp.float32)]
    k = slot_count * depth
    return pl.pallas_call(
        functools.partial(partial_body, (lhs_count, slot_count, acc is not None, final, whole is not None)),
        out_shape=out_shape,
        grid_spec=pltpu.PrefetchScalarGridSpec(
            num_scalar_prefetch=2,
            grid=(steps,),
            in_specs=in_specs,
            out_specs=out_specs,
            scratch_shapes=[pltpu.VMEM((m, k), lhs.dtype), pltpu.VMEM((k, width), lhs.dtype)],
        ),
        input_output_aliases=aliases,
        compiler_params=params(),
        cost_estimate=pl.CostEstimate(
            flops=4 * m * k * int_cols, bytes_accessed=8 * m * int_cols + k * int_cols, transcendentals=0
        ),
        name="last_blocks" if final else "first_blocks",
    )(*operands)


def tie_body(*refs):
    pass


def tie(value, *others):
    return pl.pallas_call(
        tie_body,
        out_shape=jax.ShapeDtypeStruct(value.shape, value.dtype),
        in_specs=[pl.BlockSpec(memory_space=pltpu.HBM)] * (1 + len(others)),
        out_specs=pl.BlockSpec(memory_space=pltpu.HBM),
        input_output_aliases={0: 0},
        compiler_params=params(),
        name="tie",
    )(value, *others)


def choose_body(flag, a_ref, b_ref, out_ref, sem):
    @pl.when(flag[0] != 0)
    def _():
        pltpu.make_async_copy(a_ref, out_ref, sem).start()

    @pl.when(flag[0] == 0)
    def _():
        pltpu.make_async_copy(b_ref, out_ref, sem).start()

    pltpu.make_async_copy(a_ref, out_ref, sem).wait()


def choose(here, a, b):
    return pl.pallas_call(
        choose_body,
        out_shape=jax.ShapeDtypeStruct(a.shape, a.dtype),
        in_specs=[
            pl.BlockSpec(memory_space=pltpu.SMEM),
            pl.BlockSpec(memory_space=pltpu.HBM),
            pl.BlockSpec(memory_space=pltpu.HBM),
        ],
        out_specs=pl.BlockSpec(memory_space=pltpu.VMEM),
        scratch_shapes=[pltpu.SemaphoreType.DMA],
        compiler_params=params(),
        name="choose",
    )(here.astype(jnp.int32).reshape(1), a, b)


def place_body(place_ref, piece_ref, whole_ref, out_ref):
    out_ref[...] = piece_ref[...]


def put(piece, whole, place):
    m, n = piece.shape
    width = min(2 * MM_COLS, n)
    steps = n // width
    return pl.pallas_call(
        place_body,
        out_shape=jax.ShapeDtypeStruct(whole.shape, whole.dtype),
        grid_spec=pltpu.PrefetchScalarGridSpec(
            num_scalar_prefetch=1,
            grid=(steps,),
            in_specs=[pl.BlockSpec((m, width), lambda i, s: (0, i)), pl.BlockSpec(memory_space=pltpu.HBM)],
            out_specs=pl.BlockSpec((m, width), lambda i, s: (0, s[0] * steps + i)),
        ),
        input_output_aliases={2: 0},
        compiler_params=params(),
        cost_estimate=pl.CostEstimate(flops=0, bytes_accessed=4 * m * n, transcendentals=0),
        name="put",
    )(place.astype(jnp.int32).reshape(1), piece, whole)


def col_index(ie, ia, ib, core):
    return ((ie * 2 + ia) * 2 + ib) * 2 + core


def on_device(amplitudes, amp_mask, integrals, int_tiles, pair_dest):
    rows = lax.axis_size("row")
    cols = lax.axis_size("col")
    extra = cols // 8
    pair_rows, amp_cols = amplitudes.shape
    int_rows, int_cols = integrals.shape
    capacity = 2 * pair_rows // cols
    z = lax.axis_index("row")
    me = lax.axis_index("col")
    core = lax.rem(me, 2)
    ib = lax.rem(lax.div(me, 2), 2)
    ia = lax.rem(lax.div(me, 4), 2)
    ie = lax.div(me, 8)
    every = [(e, a, b, c) for e in range(extra) for a in range(2) for b in range(2) for c in range(2)]

    amp_scale = amp_mask.astype(jnp.bfloat16)
    amp_used = (
        amplitudes.reshape(amp_mask.shape[0], TILE, amp_mask.shape[1], TILE) * amp_scale[:, None, :, None]
    ).reshape(pair_rows, amp_cols)
    amp_all = lax.all_gather(amp_used, "col", axis=1, tiled=True)

    own_lists = int_tiles[:, 0, :]
    count = own_lists.shape[1]
    tiles = (int_rows // TILE) * (int_cols // TILE)
    found = own_lists[:, None, :] == jnp.arange(tiles, dtype=jnp.int32)[None, :, None]
    own_table = jnp.min(jnp.where(found, jnp.arange(count, dtype=jnp.int32), count), axis=2)

    along = [
        (col_index(e, a, b, c), col_index(e, a ^ (c == 1), b ^ (c == 0), c)) for e, a, b, c in every
    ]
    across = [(col_index(e, a, b, c), col_index(e, a, b, 1 - c)) for e, a, b, c in every]
    table_next = lax.ppermute(own_table, "col", along)
    pair_tables = lax.ppermute(jnp.concatenate([own_table, table_next], axis=0), "col", across)
    tables = [own_table, table_next, pair_tables[:rows], pair_tables[rows:]]
    blocks = [[], [], [], []]

    def spread(slot):
        mine_next = lax.ppermute(slot, "col", along)
        theirs = lax.ppermute(slot, "col", across)
        theirs_next = lax.ppermute(mine_next, "col", across)
        for q, block in enumerate((slot, mine_next, theirs, theirs_next)):
            blocks[q].append(block)

    col_ids = jnp.arange(cols, dtype=jnp.int32)
    onehot = (pair_dest[:, None] == col_ids[None, :]).astype(jnp.int32)
    before = jnp.cumsum(onehot, axis=0) - onehot
    target = pair_dest * capacity + jnp.sum(before * onehot, axis=1)
    turns = [(de, da, db) for de in range(extra) for da, db in ((0, 0), (1, 0), (0, 1))]
    wanted = jnp.stack(
        [col_index(lax.rem(ie + de, extra), ia ^ da, ib ^ db, core) for de, da, db in turns]
    ).astype(jnp.int32)
    row_ids = (wanted[:, None] * capacity + jnp.arange(capacity, dtype=jnp.int32)[None, :]).reshape(-1)
    picker = (row_ids[:, None] == target[None, :]).astype(jnp.bfloat16)
    lhs = jnp.dot(picker, amp_all, preferred_element_type=jnp.bfloat16).reshape(len(turns), capacity, -1)

    panels = (0, 2, 1, 3)
    early = max(rows - 2, 1)
    hops = [(de, turn) for de in range(extra) for turn in (0, 1)]
    picks_of = {}
    for q in panels:
        kind = core if q < 2 else 1 - core
        picks_of[q] = [jnp.int32(3 * de) + turn * (1 + kind) for de, turn in hops]

    def first_sums():
        return {
            q: partial(lhs, picks_of[q], tables[q], blocks[q][:early], slot_rows[:early], int_cols)[0]
            for q in panels
        }

    packed = pack(z.astype(jnp.int32).reshape(1), own_lists, integrals)
    spread(packed)
    partner = ({}, {})
    for i in range(rows):
        if i ^ 1 < rows:
            partner[0][i] = i ^ 1
        if 0 <= ((i + 1) ^ 1) - 1 < rows:
            partner[1][i] = ((i + 1) ^ 1) - 1
    held = ({i: i for i in range(rows)}, {i: i for i in range(rows)})
    values = (packed, packed)
    history = []
    order = [[] for _ in range(rows)]
    slot_rows = [z.astype(jnp.int32)]
    filled = 1
    sums = None
    while filled < rows:
        moved, fresh = ({}, {}), []
        for side in (0, 1):
            passed = held[0] if not history else held[1 - side]
            pairs = [(p, i) for i, p in partner[side].items() if p in passed]
            moved[side].update({i: passed[p] for p, i in pairs})
            source = values[1 - side]
            fresh.append(lax.ppermute(source, "row", pairs) if pairs else None)
        if len(blocks[0]) == rows - 1 and sums is None:
            sums = first_sums()
            waited = tuple(sums.values())
        else:
            waited = (blocks[1][-1],)
        fresh = [value if value is None else tie(value, *waited) for value in fresh]
        history.append(fresh)
        for i in range(rows):
            for side in (0, 1):
                if i in moved[side]:
                    order[i].append((len(history) - 1, side, moved[side][i]))
        held, values = moved, tuple(fresh)
        while filled < rows and all(len(o) >= filled for o in order):
            kinds = sorted({order[i][filled - 1][:2] for i in range(rows)})
            slot = None
            for kind in kinds:
                here = functools.reduce(
                    jnp.logical_or, [z == i for i in range(rows) if order[i][filled - 1][:2] == kind]
                )
                value = history[kind[0]][kind[1]]
                slot = value if slot is None else choose(here, value, slot)
            origin = jnp.array([order[i][filled - 1][2] for i in range(rows)], jnp.int32)
            slot_rows.append(origin[z])
            spread(slot)
            filled += 1

    out = None
    arrived = []
    for q in panels:
        kind = core if q < 2 else 1 - core
        second = q % 2
        a_own = jnp.where(kind == 0, ia, ia ^ second)
        b_own = jnp.where(kind == 0, ib ^ second, ib)
        out, *pieces = partial(
            lhs,
            picks_of[q],
            tables[q],
            blocks[q][early:],
            slot_rows[early:],
            int_cols,
            acc=sums[q],
            whole_cols=cols * int_cols,
            whole=out,
            place=col_index(ie, a_own, b_own, kind),
        )
        for (de, turn), piece in zip(hops[1:], pieces):
            pairs = []
            for e, a, b, c in every:
                to_kind = c if q < 2 else 1 - c
                flip_a = turn if to_kind == 0 else 0
                flip_b = turn if to_kind == 1 else 0
                pairs.append((col_index(e, a, b, c), col_index((e + de) % extra, a ^ flip_a, b ^ flip_b, c)))
            got = lax.ppermute(piece, "col", pairs)
            from_e = lax.rem(ie - de + extra, extra)
            a_of = jnp.where(kind == 0, ia ^ turn, ia ^ second)
            b_of = jnp.where(kind == 0, ib ^ second, ib ^ turn)
            arrived.append((got, col_index(from_e, a_of, b_of, kind)))
    for got, place in arrived:
        out = put(got, out, place)
    return out


def solution(mesh):
    in_specs = (P("row", "col"), P("row", "col"), P("row", "col"), P(None, "col", None), P("row"))
    out_specs = P(("row", "col"), None)
    return jax.shard_map(
        on_device, mesh=mesh, in_specs=in_specs, out_specs=out_specs, check_vma=False
    )
```

```python
import functools

import jax
import jax.numpy as jnp
import numpy as np
from jax import lax
from jax.experimental import pallas as pl
from jax.experimental.pallas import tpu as pltpu
from jax.sharding import PartitionSpec as P

TILE = 128
MM_COLS = 512
VMEM_LIMIT = (64 << 20) - (256 << 10)


def params():
    return pltpu.CompilerParams(vmem_limit_bytes=VMEM_LIMIT)


def pack_body(scalars, ids_ref, src_ref, out_ref):
    col_tiles = src_ref.shape[1] // TILE
    tiles = col_tiles * (src_ref.shape[0] // TILE)
    for e in range(out_ref.shape[0]):
        t = jnp.minimum(ids_ref[scalars[0], e], tiles - 1)
        k = pl.multiple_of(lax.div(t, col_tiles) * TILE, TILE)
        n = pl.multiple_of(lax.rem(t, col_tiles) * TILE, TILE)
        out_ref[e] = src_ref[pl.ds(k, TILE), pl.ds(n, TILE)]


def pack(scalars, lists, integrals):
    count = lists.shape[1]
    return pl.pallas_call(
        pack_body,
        out_shape=jax.ShapeDtypeStruct((count, TILE, TILE), integrals.dtype),
        in_specs=[
            pl.BlockSpec(memory_space=pltpu.SMEM),
            pl.BlockSpec(memory_space=pltpu.SMEM),
            pl.BlockSpec(memory_space=pltpu.VMEM),
        ],
        out_specs=pl.BlockSpec(memory_space=pltpu.VMEM),
        compiler_params=params(),
        name="pack_tiles",
    )(scalars, lists, integrals)


def mask_body(mask_ref, amp_ref, after_ref, out_ref):
    for a in range(mask_ref.shape[0]):
        for k in range(mask_ref.shape[1]):
            at = (slice(a * TILE, (a + 1) * TILE), slice(k * TILE, (k + 1) * TILE))
            scale = mask_ref[a, k].astype(jnp.float32)
            out_ref[at] = (amp_ref[at].astype(jnp.float32) * scale).astype(out_ref.dtype)


def mask_tiles(mask, amplitudes, after):
    return pl.pallas_call(
        mask_body,
        out_shape=jax.ShapeDtypeStruct(amplitudes.shape, amplitudes.dtype),
        in_specs=[
            pl.BlockSpec(memory_space=pltpu.SMEM),
            pl.BlockSpec(memory_space=pltpu.VMEM),
            pl.BlockSpec(memory_space=pltpu.HBM),
        ],
        out_specs=pl.BlockSpec(memory_space=pltpu.VMEM),
        compiler_params=params(),
        name="mask_tiles",
    )(mask, amplitudes, after)


def pick_body(first, capacity, scalars, target_ref, *refs):
    amps, (mine, theirs) = refs[:-2], refs[-2:]
    step = pl.program_id(0)
    half = pl.num_programs(0) // 2
    rows = scalars[first + step] * capacity + lax.broadcasted_iota(jnp.int32, (capacity, target_ref.shape[1]), 0)
    chosen = jnp.where(rows == target_ref[...], 1.0, 0.0).astype(mine.dtype)
    for at, amp in enumerate(amps):
        value = jnp.dot(chosen, amp[...], preferred_element_type=jnp.float32).astype(mine.dtype)

        @pl.when(step < half)
        def _():
            theirs[at, 0] = value

        @pl.when(step >= half)
        def _():
            mine[at, 0] = value


def pick_rows(scalars, first, count, target, amps, capacity):
    n, k = amps[0].shape
    shape = jax.ShapeDtypeStruct((len(amps), count, capacity, k), amps[0].dtype)
    block = (len(amps), 1, capacity, k)
    return pl.pallas_call(
        functools.partial(pick_body, first, capacity),
        out_shape=[shape, shape],
        grid_spec=pltpu.PrefetchScalarGridSpec(
            num_scalar_prefetch=1,
            grid=(2 * count,),
            in_specs=[pl.BlockSpec((1, n), lambda i, s: (0, 0))]
            + [pl.BlockSpec((n, k), lambda i, s: (0, 0)) for _ in amps],
            out_specs=[
                pl.BlockSpec(block, lambda i, s: (0, jnp.maximum(i - count, 0), 0, 0)),
                pl.BlockSpec(block, lambda i, s: (0, jnp.minimum(i, count - 1), 0, 0)),
            ],
        ),
        compiler_params=params(),
        cost_estimate=pl.CostEstimate(
            flops=4 * count * capacity * n * k * len(amps), bytes_accessed=8 * n * k * len(amps), transcendentals=0
        ),
        name="pick_rows",
    )(scalars, target.reshape(1, n), *amps)


def product_body(at, has_whole, scalars, table, mine, theirs, *refs):
    core_at, picks, rows_at, mine_at, theirs_at = at
    slot_count = len(rows_at)
    packed_hbm = refs[:slot_count]
    refs = refs[slot_count + has_whole :]
    outs, (lhs_all, rhs_all, packed, lhs_sem, sems) = refs[:-5], refs[-5:]
    step = pl.program_id(0)
    capacity, part = mine.shape[2:]
    depth = lhs_all.shape[1] // slot_count
    width = rhs_all.shape[1]
    count = packed.shape[1]
    col_tiles = table.shape[1] // (depth // TILE)

    @pl.when(step == 0)
    def _():
        for s in range(slot_count):
            pltpu.make_async_copy(packed_hbm[s], packed.at[s], sems.at[s]).start()
        for s in range(slot_count):
            for source, chip, side in (
                (mine, scalars[mine_at[s]], scalars[core_at]),
                (theirs, scalars[theirs_at[s]], 1 - scalars[core_at]),
            ):
                lanes = pl.ds(pl.multiple_of(s * depth + side * part, part), part)
                for t, pick in enumerate(picks):
                    pltpu.make_async_copy(
                        source.at[chip, scalars[pick]], lhs_all.at[pl.ds(t * capacity, capacity), lanes], lhs_sem
                    ).start()
        for s in range(slot_count):
            pltpu.make_async_copy(packed_hbm[s], packed.at[s], sems.at[s]).wait()
        pltpu.make_async_copy(lhs_all, lhs_all, lhs_sem).wait()

    for s in range(slot_count):
        row = scalars[rows_at[s]]
        for k in range(depth // TILE):
            for n in range(width // TILE):
                e = table[row, k * col_tiles + step * (width // TILE) + n]
                tile = packed[s, jnp.minimum(e, count - 1)]
                rhs_all[s * depth + k * TILE : s * depth + (k + 1) * TILE, n * TILE : (n + 1) * TILE] = jnp.where(
                    e < count, tile, jnp.zeros_like(tile)
                )
    total = jnp.dot(lhs_all[...], rhs_all[...], preferred_element_type=jnp.float32)
    for t in range(len(picks)):
        outs[t][...] = total[t * capacity : (t + 1) * capacity].astype(outs[t].dtype)


def product(scalars, table, mine, theirs, slots, int_cols, whole_cols, whole, at, place_at):
    core_at, picks, rows_at, mine_at, theirs_at = at
    capacity, part = mine.shape[2:]
    slot_count, m = len(slots), len(picks) * capacity
    depth = 2 * part
    width = min(MM_COLS, int_cols)
    steps = int_cols // width
    hbm = pl.BlockSpec(memory_space=pltpu.HBM)
    operands = [scalars, table, mine, theirs, *slots]
    aliases = {}
    if whole is not None:
        aliases = {len(operands): 0}
        operands.append(whole)
    out_specs = [pl.BlockSpec((capacity, width), lambda i, sc, tab: (0, sc[place_at] * steps + i))]
    out_shape = [jax.ShapeDtypeStruct((capacity, whole_cols), mine.dtype)]
    for _ in picks[1:]:
        out_specs.append(pl.BlockSpec((capacity, width), lambda i, sc, tab: (0, i)))
        out_shape.append(jax.ShapeDtypeStruct((capacity, int_cols), mine.dtype))
    k = slot_count * depth
    return pl.pallas_call(
        functools.partial(product_body, at, whole is not None),
        out_shape=out_shape,
        grid_spec=pltpu.PrefetchScalarGridSpec(
            num_scalar_prefetch=2,
            grid=(steps,),
            in_specs=[hbm] * (len(operands) - 2),
            out_specs=out_specs,
            scratch_shapes=[
                pltpu.VMEM((m, k), mine.dtype),
                pltpu.VMEM((k, width), mine.dtype),
                pltpu.VMEM((slot_count, *slots[0].shape), mine.dtype),
                pltpu.SemaphoreType.DMA,
                pltpu.SemaphoreType.DMA((slot_count,)),
            ],
        ),
        input_output_aliases=aliases,
        compiler_params=params(),
        cost_estimate=pl.CostEstimate(
            flops=4 * m * k * int_cols, bytes_accessed=2 * m * (k + int_cols) + k * int_cols, transcendentals=0
        ),
        name="product",
    )(*operands)


def tie_body(*refs):
    pass


def tie(value, *others):
    return pl.pallas_call(
        tie_body,
        out_shape=jax.ShapeDtypeStruct(value.shape, value.dtype),
        in_specs=[pl.BlockSpec(memory_space=pltpu.HBM)] * (1 + len(others)),
        out_specs=pl.BlockSpec(memory_space=pltpu.HBM),
        input_output_aliases={0: 0},
        compiler_params=params(),
        name="tie",
    )(value, *others)


def choose_body(at, scalars, into_ref, other_ref, out_ref, sem):
    @pl.when(scalars[at] != 0)
    def _():
        copy = pltpu.make_async_copy(other_ref, out_ref, sem)
        copy.start()
        copy.wait()


def choose(scalars, at, into, other):
    return pl.pallas_call(
        functools.partial(choose_body, at),
        out_shape=jax.ShapeDtypeStruct(into.shape, into.dtype),
        in_specs=[
            pl.BlockSpec(memory_space=pltpu.SMEM),
            pl.BlockSpec(memory_space=pltpu.HBM),
            pl.BlockSpec(memory_space=pltpu.HBM),
        ],
        out_specs=pl.BlockSpec(memory_space=pltpu.HBM),
        scratch_shapes=[pltpu.SemaphoreType.DMA],
        input_output_aliases={1: 0},
        compiler_params=params(),
        name="choose",
    )(scalars, into, other)


def place_body(place_ref, piece_ref, whole_ref, out_ref):
    out_ref[...] = piece_ref[...]


def put(piece, whole, scalars, at):
    m, n = piece.shape
    width = min(2 * MM_COLS, n)
    steps = n // width
    return pl.pallas_call(
        place_body,
        out_shape=jax.ShapeDtypeStruct(whole.shape, whole.dtype),
        grid_spec=pltpu.PrefetchScalarGridSpec(
            num_scalar_prefetch=1,
            grid=(steps,),
            in_specs=[pl.BlockSpec((m, width), lambda i, s: (0, i)), pl.BlockSpec(memory_space=pltpu.HBM)],
            out_specs=pl.BlockSpec((m, width), lambda i, s: (0, s[at] * steps + i)),
        ),
        input_output_aliases={2: 0},
        compiler_params=params(),
        cost_estimate=pl.CostEstimate(flops=0, bytes_accessed=4 * m * n, transcendentals=0),
        name="put",
    )(scalars, piece, whole)


def col_index(ie, ia, ib, core):
    return ((ie * 2 + ia) * 2 + ib) * 2 + core


class Scalars:
    def __init__(self, rows, cols):
        self.places = [(z, me // 8, me // 4 % 2, me // 2 % 2, me % 2) for z in range(rows) for me in range(cols)]
        self.columns = []

    def add(self, value_of):
        self.columns.append([int(value_of(*place)) for place in self.places])
        return len(self.columns) - 1

    def of_device(self, z, me, cols):
        table = np.array(self.columns, np.int32).T
        return lax.dynamic_slice(jnp.asarray(table), (z * cols + me, 0), (1, table.shape[1]))[0]


def line_schedule(rows):
    partner = ({}, {})
    for i in range(rows):
        if i ^ 1 < rows:
            partner[0][i] = i ^ 1
        if 0 <= ((i + 1) ^ 1) - 1 < rows:
            partner[1][i] = ((i + 1) ^ 1) - 1
    held = ({i: i for i in range(rows)}, {i: i for i in range(rows)})
    steps, order = [], [[] for _ in range(rows)]
    while min(len(o) for o in order) < rows - 1:
        moved, pairs = ({}, {}), []
        for side in (0, 1):
            passed = held[1 - side]
            pairs.append([(p, i) for i, p in partner[side].items() if p in passed])
            moved[side].update({i: passed[p] for p, i in pairs[side]})
        for i in range(rows):
            for side in (0, 1):
                if i in moved[side]:
                    order[i].append((len(steps), side, moved[side][i]))
        steps.append(pairs)
        held = moved
    return steps, order


def on_device(amplitudes, amp_mask, integrals, int_tiles, pair_dest):
    rows = lax.axis_size("row")
    cols = lax.axis_size("col")
    extra = cols // 8
    pair_rows, amp_cols = amplitudes.shape
    int_rows, int_cols = integrals.shape
    capacity = 2 * pair_rows // cols
    every = [(e, a, b, c) for e in range(extra) for a in range(2) for b in range(2) for c in range(2)]
    chips = [(e, a, b) for e in range(extra) for a in range(2) for b in range(2)]
    hops = [(de, turn) for de in range(extra) for turn in (0, 1)]
    turns = [(de, da, db) for de in range(extra) for da, db in ((0, 0), (1, 0), (0, 1))]
    steps, order = line_schedule(rows)

    def permute(value, moved_to):
        return lax.ppermute(value, "col", [(col_index(*at), col_index(*moved_to(*at))) for at in every])

    def along(e, a, b, c):
        return e, a ^ (c == 1), b ^ (c == 0), c

    def other(e, a, b, c):
        return e, a ^ (c == 0), b ^ (c == 1), c

    def across(e, a, b, c):
        return e, a, b, 1 - c

    consts = Scalars(rows, cols)
    consts.add(lambda z, e, a, b, c: z)
    core_at = consts.add(lambda z, e, a, b, c: c)
    wanted_at = len(consts.columns)
    for flip in (1, 0):
        for de, da, db in turns:
            consts.add(lambda z, e, a, b, c: col_index((e + de) % extra, a ^ da, b ^ db, c ^ flip))
    slot_rows = [lambda z: z] + [functools.partial(lambda j, z: order[z][j][2], j) for j in range(rows - 1)]
    rows_at = [consts.add(lambda z, e, a, b, c: row(z)) for row in slot_rows]
    gathered = [(de, p, q) for de in range(extra) for q in (0, 1) for p in (0, 1)]

    def arrival(chip, e, a, b, c):
        ce, ca, cb = chips[chip]
        p, q = (cb ^ b, ca ^ a) if c == 0 else (ca ^ a, cb ^ b)
        return gathered.index(((ce - e) % extra, p, q))

    mine_at = [consts.add(lambda z, e, a, b, c: arrival(row(z), e, a, b, c)) for row in slot_rows]
    theirs_at = [consts.add(lambda z, e, a, b, c: arrival(row(z), e, a, b, 1 - c)) for row in slot_rows]
    picks_at, place_at, arrive_at = {}, {}, {}
    for q in range(4):
        flip, second = int(q >= 2), q % 2
        picks_at[q] = [
            consts.add(lambda z, e, a, b, c: 3 * de + turn * (1 + (c ^ flip))) for de, turn in hops
        ]

        def block(e, a, b, kind, turn):
            return col_index(e, a ^ (second if kind else turn), b ^ (turn if kind else second), kind)

        place_at[q] = consts.add(lambda z, e, a, b, c: block(e, a, b, c ^ flip, 0))
        arrive_at[q] = [
            consts.add(lambda z, e, a, b, c: block((e - de) % extra, a, b, c ^ flip, turn)) for de, turn in hops[1:]
        ]
    flags_at = {}
    for j in range(rows - 1):
        kinds = sorted({order[i][j][:2] for i in range(rows)})
        for kind in kinds[:-1]:
            flags_at[j, kind] = consts.add(lambda z, e, a, b, c: order[z][j][:2] == kind)
    scalars = consts.of_device(lax.axis_index("row"), lax.axis_index("col"), cols)

    own_lists = int_tiles[:, 0, :]
    packed = pack(scalars, own_lists, integrals)

    def line_step(values, pairs):
        return [lax.ppermute(values[1 - side], "row", pairs[side]) if pairs[side] else None for side in (0, 1)]

    fresh = line_step((packed, packed), steps[0])
    amp_used = mask_tiles(amp_mask, amplitudes, packed)
    amp_next = permute(amp_used, along)
    amp_other = permute(amp_used, other)
    amp_far = permute(amp_next, other)
    amps = [amp_used, amp_next, amp_other, amp_far]
    for de in range(1, extra):
        amps += [permute(amp, lambda e, a, b, c: ((e - de) % extra, a, b, c)) for amp in amps[:4]]

    count = own_lists.shape[1]
    tiles = (int_rows // TILE) * (int_cols // TILE)
    found = own_lists[:, None, :] == jnp.arange(tiles, dtype=jnp.int32)[None, :, None]
    own_table = jnp.min(jnp.where(found, jnp.arange(count, dtype=jnp.int32), count), axis=2)
    table_next = permute(own_table, along)
    pair_tables = permute(jnp.concatenate([own_table, table_next], axis=0), across)
    tables = [own_table, table_next, pair_tables[:rows], pair_tables[rows:]]

    col_ids = jnp.arange(cols, dtype=jnp.int32)
    onehot = (pair_dest[:, None] == col_ids[None, :]).astype(jnp.int32)
    before = jnp.cumsum(onehot, axis=0) - onehot
    target = pair_dest * capacity + jnp.sum(before * onehot, axis=1)
    mine, for_them = pick_rows(scalars, wanted_at, len(turns), target, amps, capacity)
    theirs = permute(for_them, across)

    blocks = [[], [], [], []]

    def spread(slot, last):
        mine_next = permute(slot, along)
        blocks[0].append(slot)
        blocks[2].append(permute(slot, across))
        if not last:
            blocks[1].append(mine_next)
            blocks[3].append(permute(mine_next, across))
        return mine_next

    last_next = spread(packed, rows == 1)
    history = []
    for at in range(len(steps)):
        if at > 0:
            fresh = line_step(history[-1], steps[at])
        if at == 0:
            waited = (amp_far, amp_other, pair_tables)
        elif at < len(steps) - 1:
            waited = (*blocks[1], *blocks[2])
        else:
            waited = (theirs, *blocks[1][-1:], *blocks[2][-1:], *blocks[3][:-1])
        history.append([value if value is None else tie(value, *waited) for value in fresh])
        while len(blocks[0]) < rows and all(order[i][len(blocks[0]) - 1][0] <= at for i in range(rows)):
            j = len(blocks[0]) - 1
            kinds = sorted({order[i][j][:2] for i in range(rows)})
            slot = history[kinds[-1][0]][kinds[-1][1]]
            for kind in kinds[:-1]:
                slot = choose(scalars, flags_at[j, kind], slot, history[kind[0]][kind[1]])
            last_next = spread(slot, j == rows - 2)

    out = None
    arrived = []
    for q in (0, 2, 1, 3):
        out, *pieces = product(
            scalars,
            tables[q],
            mine,
            theirs,
            blocks[q],
            int_cols,
            cols * int_cols,
            out,
            (core_at, picks_at[q], rows_at, mine_at, theirs_at),
            place_at[q],
        )
        for (de, turn), piece, place in zip(hops[1:], pieces, arrive_at[q]):
            def sent_to(e, a, b, c):
                kind = c ^ int(q >= 2)
                return (e + de) % extra, a ^ (0 if kind else turn), b ^ (turn if kind else 0), c

            arrived.append((permute(piece, sent_to), place))
        if q == 0:
            last_next = tie(last_next, pieces[0])
            blocks[1].append(last_next)
            blocks[3].append(permute(last_next, across))
    for got, place in arrived:
        out = put(got, out, scalars, place)
    return out


def solution(mesh):
    in_specs = (P("row", "col"), P("row", "col"), P("row", "col"), P(None, "col", None), P("row"))
    out_specs = P(("row", "col"), None)
    return jax.shard_map(
        on_device, mesh=mesh, in_specs=in_specs, out_specs=out_specs, check_vma=False
    )
```

```python
import functools

import jax
import jax.numpy as jnp
import numpy as np
from jax import lax
from jax.experimental import pallas as pl
from jax.experimental.pallas import tpu as pltpu
from jax.sharding import PartitionSpec as P

TILE = 128
NOTHING = pl.CostEstimate(flops=0, bytes_accessed=0, transcendentals=0)
MM_COLS = 512
VMEM_LIMIT = (64 << 20) - (256 << 10)


def params():
    return pltpu.CompilerParams(vmem_limit_bytes=VMEM_LIMIT)


def pack_body(row, ids_ref, mask_ref, src_ref, amp_ref, out_ref, used_ref):
    col_tiles = src_ref.shape[1] // TILE
    tiles = col_tiles * (src_ref.shape[0] // TILE)
    for e in range(out_ref.shape[0]):
        t = jnp.minimum(ids_ref[row[0], e], tiles - 1)
        k = pl.multiple_of(lax.div(t, col_tiles) * TILE, TILE)
        n = pl.multiple_of(lax.rem(t, col_tiles) * TILE, TILE)
        out_ref[e] = src_ref[pl.ds(k, TILE), pl.ds(n, TILE)]
    for k in range(mask_ref.shape[0]):
        for a in range(mask_ref.shape[1]):
            at = (slice(a * TILE, (a + 1) * TILE), slice(k * TILE, (k + 1) * TILE))
            scale = mask_ref[k, a].astype(jnp.float32)
            used_ref[at] = (amp_ref[at].astype(jnp.float32) * scale).astype(used_ref.dtype)


def pack(row, lists, mask, integrals, amplitudes):
    count = lists.shape[1]
    smem, vmem = pl.BlockSpec(memory_space=pltpu.SMEM), pl.BlockSpec(memory_space=pltpu.VMEM)
    return pl.pallas_call(
        pack_body,
        out_shape=[
            jax.ShapeDtypeStruct((count, TILE, TILE), integrals.dtype),
            jax.ShapeDtypeStruct(amplitudes.shape, amplitudes.dtype),
        ],
        in_specs=[smem, smem, smem, vmem, vmem],
        out_specs=[vmem, vmem],
        compiler_params=params(),
        cost_estimate=NOTHING,
        name="pack_tiles",
    )(row, lists, mask.T, integrals, amplitudes)


def pick_body(first, capacity, scalars, target_ref, *refs):
    amps, (mine, theirs) = refs[:-2], refs[-2:]
    step = pl.program_id(0)
    half = pl.num_programs(0) // 2
    rows = scalars[first + step] * capacity + lax.broadcasted_iota(jnp.int32, (capacity, target_ref.shape[1]), 0)
    chosen = jnp.where(rows == target_ref[...], 1.0, 0.0).astype(mine.dtype)
    for at, amp in enumerate(amps):
        value = jnp.dot(chosen, amp[...], preferred_element_type=jnp.float32).astype(mine.dtype)

        @pl.when(step < half)
        def _():
            theirs[at, 0] = value

        @pl.when(step >= half)
        def _():
            mine[at, 0] = value


def pick_rows(scalars, first, count, target, amps, capacity):
    n, k = amps[0].shape
    shape = jax.ShapeDtypeStruct((len(amps), count, capacity, k), amps[0].dtype)
    block = (len(amps), 1, capacity, k)
    return pl.pallas_call(
        functools.partial(pick_body, first, capacity),
        out_shape=[shape, shape],
        grid_spec=pltpu.PrefetchScalarGridSpec(
            num_scalar_prefetch=1,
            grid=(2 * count,),
            in_specs=[pl.BlockSpec((1, n), lambda i, s: (0, 0))]
            + [pl.BlockSpec((n, k), lambda i, s: (0, 0)) for _ in amps],
            out_specs=[
                pl.BlockSpec(block, lambda i, s: (0, jnp.maximum(i - count, 0), 0, 0)),
                pl.BlockSpec(block, lambda i, s: (0, jnp.minimum(i, count - 1), 0, 0)),
            ],
        ),
        compiler_params=params(),
        cost_estimate=NOTHING,
        name="pick_rows",
    )(scalars, target.reshape(1, n), *amps)


def product_body(at, has_whole, scalars, table, mine, theirs, *refs):
    core_at, picks, rows_at, mine_at, theirs_at = at
    slot_count = len(rows_at)
    packed_hbm = refs[:slot_count]
    refs = refs[slot_count + has_whole :]
    outs, (lhs_all, rhs_all, packed, lhs_sem, sems) = refs[:-5], refs[-5:]
    step = pl.program_id(0)
    capacity, part = mine.shape[2:]
    depth = lhs_all.shape[1] // slot_count
    width = rhs_all.shape[1]
    count = packed.shape[1]
    col_tiles = table.shape[1] // (depth // TILE)

    @pl.when(step == 0)
    def _():
        for s in range(slot_count):
            pltpu.make_async_copy(packed_hbm[s], packed.at[s], sems.at[s]).start()
        for s in range(slot_count):
            for source, chip, side in (
                (mine, scalars[mine_at[s]], scalars[core_at]),
                (theirs, scalars[theirs_at[s]], 1 - scalars[core_at]),
            ):
                lanes = pl.ds(pl.multiple_of(s * depth + side * part, part), part)
                for t, pick in enumerate(picks):
                    pltpu.make_async_copy(
                        source.at[chip, scalars[pick]], lhs_all.at[pl.ds(t * capacity, capacity), lanes], lhs_sem
                    ).start()
        for s in range(slot_count):
            pltpu.make_async_copy(packed_hbm[s], packed.at[s], sems.at[s]).wait()
        pltpu.make_async_copy(lhs_all, lhs_all, lhs_sem).wait()

    for s in range(slot_count):
        row = scalars[rows_at[s]]
        for k in range(depth // TILE):
            for n in range(width // TILE):
                e = table[row, k * col_tiles + step * (width // TILE) + n]
                tile = packed[s, jnp.minimum(e, count - 1)]
                rhs_all[s * depth + k * TILE : s * depth + (k + 1) * TILE, n * TILE : (n + 1) * TILE] = jnp.where(
                    e < count, tile, jnp.zeros_like(tile)
                )
    total = jnp.dot(lhs_all[...], rhs_all[...], preferred_element_type=jnp.float32)
    for t in range(len(picks)):
        outs[t][...] = total[t * capacity : (t + 1) * capacity].astype(outs[t].dtype)


def product(scalars, table, mine, theirs, slots, int_cols, whole_cols, whole, at, place_at):
    core_at, picks, rows_at, mine_at, theirs_at = at
    capacity, part = mine.shape[2:]
    slot_count, m = len(slots), len(picks) * capacity
    depth = 2 * part
    width = min(MM_COLS, int_cols)
    steps = int_cols // width
    hbm = pl.BlockSpec(memory_space=pltpu.HBM)
    operands = [scalars, table, mine, theirs, *slots]
    aliases = {}
    if whole is not None:
        aliases = {len(operands): 0}
        operands.append(whole)
    out_specs = [pl.BlockSpec((capacity, width), lambda i, sc, tab: (0, sc[place_at] * steps + i))]
    out_shape = [jax.ShapeDtypeStruct((capacity, whole_cols), mine.dtype)]
    for _ in picks[1:]:
        out_specs.append(pl.BlockSpec((capacity, width), lambda i, sc, tab: (0, i)))
        out_shape.append(jax.ShapeDtypeStruct((capacity, int_cols), mine.dtype))
    k = slot_count * depth
    return pl.pallas_call(
        functools.partial(product_body, at, whole is not None),
        out_shape=out_shape,
        grid_spec=pltpu.PrefetchScalarGridSpec(
            num_scalar_prefetch=2,
            grid=(steps,),
            in_specs=[hbm] * (len(operands) - 2),
            out_specs=out_specs,
            scratch_shapes=[
                pltpu.VMEM((m, k), mine.dtype),
                pltpu.VMEM((k, width), mine.dtype),
                pltpu.VMEM((slot_count, *slots[0].shape), mine.dtype),
                pltpu.SemaphoreType.DMA,
                pltpu.SemaphoreType.DMA((slot_count,)),
            ],
        ),
        input_output_aliases=aliases,
        compiler_params=params(),
        cost_estimate=NOTHING,
        name="product",
    )(*operands)


def tie_body(*refs):
    pass


def tie(value, *others):
    return pl.pallas_call(
        tie_body,
        out_shape=jax.ShapeDtypeStruct(value.shape, value.dtype),
        in_specs=[pl.BlockSpec(memory_space=pltpu.HBM)] * (1 + len(others)),
        out_specs=pl.BlockSpec(memory_space=pltpu.HBM),
        input_output_aliases={0: 0},
        compiler_params=params(),
        cost_estimate=NOTHING,
        name="tie",
    )(value, *others)


def choose_body(at, scalars, a_ref, b_ref, out_ref, sem):
    @pl.when(scalars[at] != 0)
    def _():
        pltpu.make_async_copy(a_ref, out_ref, sem).start()

    @pl.when(scalars[at] == 0)
    def _():
        pltpu.make_async_copy(b_ref, out_ref, sem).start()

    pltpu.make_async_copy(a_ref, out_ref, sem).wait()


def choose(scalars, at, a, b):
    return pl.pallas_call(
        functools.partial(choose_body, at),
        out_shape=jax.ShapeDtypeStruct(a.shape, a.dtype),
        in_specs=[
            pl.BlockSpec(memory_space=pltpu.SMEM),
            pl.BlockSpec(memory_space=pltpu.HBM),
            pl.BlockSpec(memory_space=pltpu.HBM),
        ],
        out_specs=pl.BlockSpec(memory_space=pltpu.VMEM),
        scratch_shapes=[pltpu.SemaphoreType.DMA],
        compiler_params=params(),
        cost_estimate=NOTHING,
        name="choose",
    )(scalars, a, b)


def place_body(place_ref, piece_ref, whole_ref, out_ref):
    out_ref[...] = piece_ref[...]


def put(piece, whole, scalars, at):
    m, n = piece.shape
    width = min(2 * MM_COLS, n)
    steps = n // width
    return pl.pallas_call(
        place_body,
        out_shape=jax.ShapeDtypeStruct(whole.shape, whole.dtype),
        grid_spec=pltpu.PrefetchScalarGridSpec(
            num_scalar_prefetch=1,
            grid=(steps,),
            in_specs=[pl.BlockSpec((m, width), lambda i, s: (0, i)), pl.BlockSpec(memory_space=pltpu.HBM)],
            out_specs=pl.BlockSpec((m, width), lambda i, s: (0, s[at] * steps + i)),
        ),
        input_output_aliases={2: 0},
        compiler_params=params(),
        cost_estimate=pl.CostEstimate(flops=0, bytes_accessed=4 * m * n, transcendentals=0),
        name="put",
    )(scalars, piece, whole)


def col_index(ie, ia, ib, core):
    return ((ie * 2 + ia) * 2 + ib) * 2 + core


class Scalars:
    def __init__(self, rows, cols):
        self.places = [(z, me // 8, me // 4 % 2, me // 2 % 2, me % 2) for z in range(rows) for me in range(cols)]
        self.columns = []

    def add(self, value_of):
        self.columns.append([int(value_of(*place)) for place in self.places])
        return len(self.columns) - 1

    def of_device(self, z, me, cols):
        table = np.array(self.columns, np.int32).T
        return lax.dynamic_slice(jnp.asarray(table), (z * cols + me, 0), (1, table.shape[1]))[0]


def line_schedule(rows):
    partner = ({}, {})
    for i in range(rows):
        if i ^ 1 < rows:
            partner[0][i] = i ^ 1
        if 0 <= ((i + 1) ^ 1) - 1 < rows:
            partner[1][i] = ((i + 1) ^ 1) - 1
    held = ({i: i for i in range(rows)}, {i: i for i in range(rows)})
    steps, order = [], [[] for _ in range(rows)]
    while min(len(o) for o in order) < rows - 1:
        moved, pairs = ({}, {}), []
        for side in (0, 1):
            passed = held[1 - side]
            pairs.append([(p, i) for i, p in partner[side].items() if p in passed])
            moved[side].update({i: passed[p] for p, i in pairs[side]})
        for i in range(rows):
            for side in (0, 1):
                if i in moved[side]:
                    order[i].append((len(steps), side, moved[side][i]))
        steps.append(pairs)
        held = moved
    return steps, order


def on_device(amplitudes, amp_mask, integrals, int_tiles, pair_dest):
    rows = lax.axis_size("row")
    cols = lax.axis_size("col")
    extra = cols // 8
    pair_rows, amp_cols = amplitudes.shape
    int_rows, int_cols = integrals.shape
    capacity = 2 * pair_rows // cols
    every = [(e, a, b, c) for e in range(extra) for a in range(2) for b in range(2) for c in range(2)]
    chips = [(e, a, b) for e in range(extra) for a in range(2) for b in range(2)]
    hops = [(de, turn) for de in range(extra) for turn in (0, 1)]
    turns = [(de, da, db) for de in range(extra) for da, db in ((0, 0), (1, 0), (0, 1))]
    steps, order = line_schedule(rows)

    def permute(value, moved_to):
        return lax.ppermute(value, "col", [(col_index(*at), col_index(*moved_to(*at))) for at in every])

    def along(e, a, b, c):
        return e, a ^ (c == 1), b ^ (c == 0), c

    def other(e, a, b, c):
        return e, a ^ (c == 0), b ^ (c == 1), c

    def across(e, a, b, c):
        return e, a, b, 1 - c

    consts = Scalars(rows, cols)
    core_at = consts.add(lambda z, e, a, b, c: c)
    wanted_at = len(consts.columns)
    for flip in (1, 0):
        for de, da, db in turns:
            consts.add(lambda z, e, a, b, c: col_index((e + de) % extra, a ^ da, b ^ db, c ^ flip))
    slot_rows = [lambda z: z] + [functools.partial(lambda j, z: order[z][j][2], j) for j in range(rows - 1)]
    rows_at = [consts.add(lambda z, e, a, b, c: row(z)) for row in slot_rows]
    low_rows_at = [consts.add(lambda z, e, a, b, c: rows + row(z)) for row in slot_rows]
    gathered = [(de, p, q) for de in range(extra) for q in (0, 1) for p in (0, 1)]

    def arrival(chip, e, a, b, c):
        ce, ca, cb = chips[chip]
        p, q = (cb ^ b, ca ^ a) if c == 0 else (ca ^ a, cb ^ b)
        return gathered.index(((ce - e) % extra, p, q))

    mine_at = [consts.add(lambda z, e, a, b, c: arrival(row(z), e, a, b, c)) for row in slot_rows]
    theirs_at = [consts.add(lambda z, e, a, b, c: arrival(row(z), e, a, b, 1 - c)) for row in slot_rows]
    picks_at, place_at, arrive_at = {}, {}, {}
    for q in range(4):
        flip, second = int(q >= 2), q % 2
        picks_at[q] = [
            consts.add(lambda z, e, a, b, c: 3 * de + turn * (1 + (c ^ flip))) for de, turn in hops
        ]

        def block(e, a, b, kind, turn):
            return col_index(e, a ^ (second if kind else turn), b ^ (turn if kind else second), kind)

        place_at[q] = consts.add(lambda z, e, a, b, c: block(e, a, b, c ^ flip, 0))
        arrive_at[q] = [
            consts.add(lambda z, e, a, b, c: block((e - de) % extra, a, b, c ^ flip, turn)) for de, turn in hops[1:]
        ]
    flags_at = {}
    for j in range(rows - 1):
        kinds = sorted({order[i][j][:2] for i in range(rows)})
        for kind in kinds[:-1]:
            flags_at[j, kind] = consts.add(lambda z, e, a, b, c: order[z][j][:2] == kind)
    scalars = consts.of_device(lax.axis_index("row"), lax.axis_index("col"), cols)

    own_lists = int_tiles[:, 0, :]
    row = lax.axis_index("row").astype(jnp.int32).reshape(1)
    packed, amp_used = pack(row, own_lists, amp_mask, integrals, amplitudes)

    def line_step(values, pairs):
        return [lax.ppermute(values[1 - side], "row", pairs[side]) if pairs[side] else None for side in (0, 1)]

    fresh = line_step((packed, packed), steps[0])
    amp_next = permute(amp_used, along)
    amp_other = permute(amp_used, other)

    count = own_lists.shape[1]
    tiles = (int_rows // TILE) * (int_cols // TILE)
    found = own_lists[:, None, :] == jnp.arange(tiles, dtype=jnp.int32)[None, :, None]
    own_table = jnp.min(jnp.where(found, jnp.arange(count, dtype=jnp.int32), count), axis=2)
    table_next = permute(own_table, along)

    col_ids = jnp.arange(cols, dtype=jnp.int32)
    onehot = (pair_dest[:, None] == col_ids[None, :]).astype(jnp.int32)
    before = jnp.cumsum(onehot, axis=0) - onehot
    target = pair_dest * capacity + jnp.sum(before * onehot, axis=1)

    slots, nexts, theirs_of, theirs_next = [packed], [permute(packed, along)], [permute(packed, across)], []
    history = []
    for at in range(len(steps)):
        if at > 0:
            fresh = line_step(history[-1], steps[at])
        if at == 0:
            waited = (amp_next, amp_other, table_next, nexts[0], theirs_of[0], target, scalars)
        elif at == 1:
            amps = [amp_used, amp_next, amp_other, permute(amp_next, other)]
            for de in range(1, extra):
                amps += [permute(amp, lambda e, a, b, c: ((e - de) % extra, a, b, c)) for amp in amps[:4]]
            pair_tables = permute(jnp.concatenate([own_table, table_next], axis=0), across)
            waited = (*amps[3:], pair_tables, *nexts[1:], *theirs_of[1:])
        elif at == 2:
            mine, for_them = pick_rows(scalars, wanted_at, len(turns), target, amps, capacity)
            theirs = permute(for_them, across)
            waited = (theirs, *nexts[-1:], *theirs_of[-1:])
        else:
            waited = (*nexts[-1:], *theirs_of[-1:])
        if at > 0 and len(theirs_next) < len(nexts) - 1:
            theirs_next.append(permute(nexts[len(theirs_next)], across))
            waited = (*waited, theirs_next[-1])
        both = [value for value in fresh if value is not None]
        tied = [tie(both[0], *waited, *both[1:])]
        tied += [tie(value, *tied) for value in both[1:]]
        tied = iter(tied)
        history.append([value if value is None else next(tied) for value in fresh])
        while len(slots) < rows and all(order[i][len(slots) - 1][0] <= at for i in range(rows)):
            j = len(slots) - 1
            kinds = sorted({order[i][j][:2] for i in range(rows)})
            slot = history[kinds[-1][0]][kinds[-1][1]]
            for kind in kinds[:-1]:
                slot = choose(scalars, flags_at[j, kind], history[kind[0]][kind[1]], slot)
            slots.append(slot)
            nexts.append(permute(slot, along))
            theirs_of.append(permute(slot, across))

    out = None
    arrived = []
    for turn_at, q in enumerate((0, 2, 1, 3)):
        if turn_at >= 2:
            out = tie(out, *arrived[turn_at - 2])
        out, *pieces = product(
            scalars,
            (own_table, table_next, pair_tables, pair_tables)[q],
            mine,
            theirs,
            (slots, nexts, theirs_of, theirs_next)[q],
            int_cols,
            cols * int_cols,
            out,
            (core_at, picks_at[q], rows_at if q < 3 else low_rows_at, mine_at, theirs_at),
            place_at[q],
        )
        arrived.append([])
        for (de, turn), piece in zip(hops[1:], pieces):
            def sent_to(e, a, b, c):
                kind = c ^ int(q >= 2)
                return (e + de) % extra, a ^ (0 if kind else turn), b ^ (turn if kind else 0), c

            arrived[-1].append(permute(piece, sent_to))
        if q in (0, 2):
            while len(theirs_next) < rows - (q == 0):
                nexts[len(theirs_next)] = tie(nexts[len(theirs_next)], pieces[0])
                theirs_next.append(permute(nexts[len(theirs_next)], across))
    for got, q in zip(arrived, (0, 2, 1, 3)):
        for piece, place in zip(got, arrive_at[q]):
            out = put(piece, out, scalars, place)
    return out


def solution(mesh):
    in_specs = (P("row", "col"), P("row", "col"), P("row", "col"), P(None, "col", None), P("row"))
    out_specs = P(("row", "col"), None)
    return jax.shard_map(
        on_device, mesh=mesh, in_specs=in_specs, out_specs=out_specs, check_vma=False
    )
```

```python
import functools

import jax
import jax.numpy as jnp
import numpy as np
from jax import lax
from jax.experimental import pallas as pl
from jax.experimental.pallas import tpu as pltpu
from jax.sharding import PartitionSpec as P

TILE = 128
PARTS = 8
NOTHING = pl.CostEstimate(flops=0, bytes_accessed=0, transcendentals=0)
MM_COLS = 512
VMEM_LIMIT = (64 << 20) - (256 << 10)


def params():
    return pltpu.CompilerParams(vmem_limit_bytes=VMEM_LIMIT)


def pack_body(row, ids_ref, mask_ref, src_ref, amp_ref, out_ref, again_ref, used_ref):
    col_tiles = src_ref.shape[1] // TILE
    tiles = col_tiles * (src_ref.shape[0] // TILE)
    for e in range(out_ref.shape[0]):
        t = jnp.minimum(ids_ref[row[0], e], tiles - 1)
        k = pl.multiple_of(lax.div(t, col_tiles) * TILE, TILE)
        n = pl.multiple_of(lax.rem(t, col_tiles) * TILE, TILE)
        out_ref[e] = again_ref[e] = src_ref[pl.ds(k, TILE), pl.ds(n, TILE)]
    for k in range(mask_ref.shape[0]):
        for a in range(mask_ref.shape[1]):
            at = (slice(a * TILE, (a + 1) * TILE), slice(k * TILE, (k + 1) * TILE))
            scale = mask_ref[k, a].astype(jnp.float32)
            used_ref[at] = (amp_ref[at].astype(jnp.float32) * scale).astype(used_ref.dtype)


def pack(row, lists, mask, integrals, amplitudes):
    count = lists.shape[1]
    smem, vmem = pl.BlockSpec(memory_space=pltpu.SMEM), pl.BlockSpec(memory_space=pltpu.VMEM)
    return pl.pallas_call(
        pack_body,
        out_shape=[
            jax.ShapeDtypeStruct((count, TILE, TILE), integrals.dtype),
            jax.ShapeDtypeStruct((count, TILE, TILE), integrals.dtype),
            jax.ShapeDtypeStruct(amplitudes.shape, amplitudes.dtype),
        ],
        in_specs=[smem, smem, smem, vmem, vmem],
        out_specs=[vmem, vmem, vmem],
        compiler_params=params(),
        cost_estimate=NOTHING,
        name="pack_tiles",
    )(row, lists, mask.T, integrals, amplitudes)


def pick_body(first, capacity, scalars, target_ref, *refs):
    amps, (mine, theirs) = refs[:-2], refs[-2:]
    step = pl.program_id(0)
    half = pl.num_programs(0) // 2
    rows = scalars[first + step] * capacity + lax.broadcasted_iota(jnp.int32, (capacity, target_ref.shape[1]), 0)
    chosen = jnp.where(rows == target_ref[...], 1.0, 0.0).astype(mine.dtype)
    for at, amp in enumerate(amps):
        value = jnp.dot(chosen, amp[...], preferred_element_type=jnp.float32).astype(mine.dtype)

        @pl.when(step < half)
        def _():
            theirs[at, 0] = value

        @pl.when(step >= half)
        def _():
            mine[at, 0] = value


def pick_rows(scalars, first, count, target, amps, capacity):
    n, k = amps[0].shape
    shape = jax.ShapeDtypeStruct((len(amps), count, capacity, k), amps[0].dtype)
    block = (len(amps), 1, capacity, k)
    return pl.pallas_call(
        functools.partial(pick_body, first, capacity),
        out_shape=[shape, shape],
        grid_spec=pltpu.PrefetchScalarGridSpec(
            num_scalar_prefetch=1,
            grid=(2 * count,),
            in_specs=[pl.BlockSpec((1, n), lambda i, s: (0, 0))]
            + [pl.BlockSpec((n, k), lambda i, s: (0, 0)) for _ in amps],
            out_specs=[
                pl.BlockSpec(block, lambda i, s: (0, jnp.maximum(i - count, 0), 0, 0)),
                pl.BlockSpec(block, lambda i, s: (0, jnp.minimum(i, count - 1), 0, 0)),
            ],
        ),
        compiler_params=params(),
        cost_estimate=NOTHING,
        name="pick_rows",
    )(scalars, target.reshape(1, n), *amps)


def product_body(at, has_whole, scalars, table, mine, theirs, *refs):
    core_at, picks, rows_at, mine_at, theirs_at = at
    slot_count = len(rows_at)
    packed_hbm = refs[:slot_count]
    refs = refs[slot_count + has_whole :]
    outs, (lhs_all, rhs_all, packed, lhs_sem, sems) = refs[:-5], refs[-5:]
    step = pl.program_id(0)
    capacity, part = mine.shape[2:]
    depth = lhs_all.shape[1] // slot_count
    width = rhs_all.shape[1]
    count = packed.shape[1]
    col_tiles = table.shape[1] // (depth // TILE)

    @pl.when(step == 0)
    def _():
        for s in range(slot_count):
            pltpu.make_async_copy(packed_hbm[s], packed.at[s], sems.at[s]).start()
        for s in range(slot_count):
            for source, chip, side in (
                (mine, scalars[mine_at[s]], scalars[core_at]),
                (theirs, scalars[theirs_at[s]], 1 - scalars[core_at]),
            ):
                lanes = pl.ds(pl.multiple_of(s * depth + side * part, part), part)
                for t, pick in enumerate(picks):
                    pltpu.make_async_copy(
                        source.at[chip, scalars[pick]], lhs_all.at[pl.ds(t * capacity, capacity), lanes], lhs_sem
                    ).start()
        for s in range(slot_count):
            pltpu.make_async_copy(packed_hbm[s], packed.at[s], sems.at[s]).wait()
        pltpu.make_async_copy(lhs_all, lhs_all, lhs_sem).wait()

    for s in range(slot_count):
        row = scalars[rows_at[s]]
        for k in range(depth // TILE):
            for n in range(width // TILE):
                e = table[row, k * col_tiles + step * (width // TILE) + n]
                tile = packed[s, jnp.minimum(e, count - 1)]
                rhs_all[s * depth + k * TILE : s * depth + (k + 1) * TILE, n * TILE : (n + 1) * TILE] = jnp.where(
                    e < count, tile, jnp.zeros_like(tile)
                )
    total = jnp.dot(lhs_all[...], rhs_all[...], preferred_element_type=jnp.float32)
    for t in range(len(picks)):
        outs[t][...] = total[t * capacity : (t + 1) * capacity].astype(outs[t].dtype)


def product(scalars, table, mine, theirs, slots, int_cols, whole_cols, whole, at, place_at):
    core_at, picks, rows_at, mine_at, theirs_at = at
    capacity, part = mine.shape[2:]
    slot_count, m = len(slots), len(picks) * capacity
    depth = 2 * part
    width = min(MM_COLS, int_cols)
    steps = int_cols // width
    hbm = pl.BlockSpec(memory_space=pltpu.HBM)
    operands = [scalars, table, mine, theirs, *slots]
    aliases = {}
    if whole is not None:
        aliases = {len(operands): 0}
        operands.append(whole)
    out_specs = [pl.BlockSpec((capacity, width), lambda i, sc, tab: (0, sc[place_at] * steps + i))]
    out_shape = [jax.ShapeDtypeStruct((capacity, whole_cols), mine.dtype)]
    for _ in picks[1:]:
        out_specs.append(pl.BlockSpec((capacity, width), lambda i, sc, tab: (0, i)))
        out_shape.append(jax.ShapeDtypeStruct((capacity, int_cols), mine.dtype))
    k = slot_count * depth
    return pl.pallas_call(
        functools.partial(product_body, at, whole is not None),
        out_shape=out_shape,
        grid_spec=pltpu.PrefetchScalarGridSpec(
            num_scalar_prefetch=2,
            grid=(steps,),
            in_specs=[hbm] * (len(operands) - 2),
            out_specs=out_specs,
            scratch_shapes=[
                pltpu.VMEM((m, k), mine.dtype),
                pltpu.VMEM((k, width), mine.dtype),
                pltpu.VMEM((slot_count, *slots[0].shape), mine.dtype),
                pltpu.SemaphoreType.DMA,
                pltpu.SemaphoreType.DMA((slot_count,)),
            ],
        ),
        input_output_aliases=aliases,
        compiler_params=params(),
        cost_estimate=NOTHING,
        name="product",
    )(*operands)


def tie_body(*refs):
    pass


def tie(value, *others):
    return pl.pallas_call(
        tie_body,
        out_shape=jax.ShapeDtypeStruct(value.shape, value.dtype),
        in_specs=[pl.BlockSpec(memory_space=pltpu.HBM)] * (1 + len(others)),
        out_specs=pl.BlockSpec(memory_space=pltpu.HBM),
        input_output_aliases={0: 0},
        compiler_params=params(),
        cost_estimate=NOTHING,
        name="tie",
    )(value, *others)


def choose_body(at, scalars, a_ref, b_ref, out_ref, held, in_sems, out_sems):
    parts = in_sems.shape[0]
    size = held.shape[0] // parts
    spans = [pl.ds(p * size, size) for p in range(parts)]

    @pl.when(scalars[at] != 0)
    def _():
        for p, span in enumerate(spans):
            pltpu.make_async_copy(a_ref.at[span], held.at[span], in_sems.at[p]).start()

    @pl.when(scalars[at] == 0)
    def _():
        for p, span in enumerate(spans):
            pltpu.make_async_copy(b_ref.at[span], held.at[span], in_sems.at[p]).start()

    outs = [pltpu.make_async_copy(held.at[span], out_ref.at[span], out_sems.at[p]) for p, span in enumerate(spans)]
    for p, span in enumerate(spans):
        pltpu.make_async_copy(a_ref.at[span], held.at[span], in_sems.at[p]).wait()
        outs[p].start()
    for copy in outs:
        copy.wait()


def choose(scalars, at, a, b):
    hbm = pl.BlockSpec(memory_space=pltpu.HBM)
    return pl.pallas_call(
        functools.partial(choose_body, at),
        out_shape=jax.ShapeDtypeStruct(a.shape, a.dtype),
        in_specs=[pl.BlockSpec(memory_space=pltpu.SMEM), hbm, hbm],
        out_specs=hbm,
        scratch_shapes=[
            pltpu.VMEM(a.shape, a.dtype),
            pltpu.SemaphoreType.DMA((PARTS,)),
            pltpu.SemaphoreType.DMA((PARTS,)),
        ],
        compiler_params=params(),
        cost_estimate=NOTHING,
        name="choose",
    )(scalars, a, b)


def put_body(at, scalars, piece_ref, whole_ref, out_ref, held, in_sems, out_sems):
    parts = in_sems.shape[0]
    m, n = held.shape
    size = m // parts
    columns = pl.ds(pl.multiple_of(scalars[at] * n, TILE), n)
    spans = [pl.ds(p * size, size) for p in range(parts)]
    ins = [pltpu.make_async_copy(piece_ref.at[span], held.at[span], in_sems.at[p]) for p, span in enumerate(spans)]
    outs = [
        pltpu.make_async_copy(held.at[span], out_ref.at[span, columns], out_sems.at[p]) for p, span in enumerate(spans)
    ]
    for copy in ins:
        copy.start()
    for before, after in zip(ins, outs):
        before.wait()
        after.start()
    for copy in outs:
        copy.wait()


def put(piece, whole, scalars, at):
    hbm = pl.BlockSpec(memory_space=pltpu.HBM)
    return pl.pallas_call(
        functools.partial(put_body, at),
        out_shape=jax.ShapeDtypeStruct(whole.shape, whole.dtype),
        in_specs=[pl.BlockSpec(memory_space=pltpu.SMEM), hbm, hbm],
        out_specs=hbm,
        scratch_shapes=[
            pltpu.VMEM(piece.shape, piece.dtype),
            pltpu.SemaphoreType.DMA((PARTS,)),
            pltpu.SemaphoreType.DMA((PARTS,)),
        ],
        input_output_aliases={2: 0},
        compiler_params=params(),
        cost_estimate=NOTHING,
        name="put",
    )(scalars, piece, whole)


def col_index(ie, ia, ib, core):
    return ((ie * 2 + ia) * 2 + ib) * 2 + core


class Scalars:
    def __init__(self, rows, cols):
        self.places = [(z, me // 8, me // 4 % 2, me // 2 % 2, me % 2) for z in range(rows) for me in range(cols)]
        self.columns = []

    def add(self, value_of):
        self.columns.append([int(value_of(*place)) for place in self.places])
        return len(self.columns) - 1

    def of_device(self, z, me, cols):
        table = np.array(self.columns, np.int32).T
        return lax.dynamic_slice(jnp.asarray(table), (z * cols + me, 0), (1, table.shape[1]))[0]


def line_schedule(rows):
    if rows == 4:
        phases = [
            [(-1, [(0, 1), (1, 0), (2, 3), (3, 2)]), (-1, [(0, 2), (2, 0), (1, 3), (3, 1)])],
            [(-1, [(1, 2), (2, 1)]), (1, [(1, 0), (2, 3)])],
        ]
    else:
        partner = ({}, {})
        for i in range(rows):
            if i ^ 1 < rows:
                partner[0][i] = i ^ 1
            if 0 <= ((i + 1) ^ 1) - 1 < rows:
                partner[1][i] = ((i + 1) ^ 1) - 1
        phases, reached, last, count = [], (set(range(rows)), set(range(rows))), (-1, -1), 0
        while True:
            moves, now, fresh = [], [-1, -1], (set(), set())
            for side in (0, 1):
                pairs = [(p, i) for i, p in partner[side].items() if p in reached[1 - side]]
                fresh[side].update(i for _, i in pairs)
                if pairs:
                    moves.append((last[1 - side], pairs))
                    now[side] = count
                    count += 1
            if not moves:
                break
            phases.append(moves)
            reached, last = fresh, tuple(now)
    arrivals = [[] for _ in range(rows)]
    blocks = []
    for moves in phases:
        for source, pairs in moves:
            got = {b: a if source < 0 else blocks[source][a] for a, b in pairs}
            blocks.append(got)
            for i, block in got.items():
                arrivals[i].append((len(blocks) - 1, block))
    return phases, arrivals


def on_device(amplitudes, amp_mask, integrals, int_tiles, pair_dest):
    rows = lax.axis_size("row")
    cols = lax.axis_size("col")
    extra = cols // 8
    pair_rows, amp_cols = amplitudes.shape
    int_rows, int_cols = integrals.shape
    capacity = 2 * pair_rows // cols
    every = [(e, a, b, c) for e in range(extra) for a in range(2) for b in range(2) for c in range(2)]
    chips = [(e, a, b) for e in range(extra) for a in range(2) for b in range(2)]
    hops = [(de, turn) for de in range(extra) for turn in (0, 1)]
    turns = [(de, da, db) for de in range(extra) for da, db in ((0, 0), (1, 0), (0, 1))]
    phases, order = line_schedule(rows)

    def permute(value, moved_to):
        return lax.ppermute(value, "col", [(col_index(*at), col_index(*moved_to(*at))) for at in every])

    def along(e, a, b, c):
        return e, a ^ (c == 1), b ^ (c == 0), c

    def other(e, a, b, c):
        return e, a ^ (c == 0), b ^ (c == 1), c

    def across(e, a, b, c):
        return e, a, b, 1 - c

    consts = Scalars(rows, cols)
    core_at = consts.add(lambda z, e, a, b, c: c)
    wanted_at = len(consts.columns)
    for flip in (1, 0):
        for de, da, db in turns:
            consts.add(lambda z, e, a, b, c: col_index((e + de) % extra, a ^ da, b ^ db, c ^ flip))
    slot_rows = [lambda z: z] + [functools.partial(lambda j, z: order[z][j][1], j) for j in range(rows - 1)]
    rows_at = [consts.add(lambda z, e, a, b, c: row(z)) for row in slot_rows]
    low_rows_at = [consts.add(lambda z, e, a, b, c: rows + row(z)) for row in slot_rows]
    gathered = [(de, p, q) for de in range(extra) for q in (0, 1) for p in (0, 1)]

    def arrival(chip, e, a, b, c):
        ce, ca, cb = chips[chip]
        p, q = (cb ^ b, ca ^ a) if c == 0 else (ca ^ a, cb ^ b)
        return gathered.index(((ce - e) % extra, p, q))

    mine_at = [consts.add(lambda z, e, a, b, c: arrival(row(z), e, a, b, c)) for row in slot_rows]
    theirs_at = [consts.add(lambda z, e, a, b, c: arrival(row(z), e, a, b, 1 - c)) for row in slot_rows]
    picks_at, place_at, arrive_at = {}, {}, {}
    for q in range(4):
        flip, second = int(q >= 2), q % 2
        picks_at[q] = [
            consts.add(lambda z, e, a, b, c: 3 * de + turn * (1 + (c ^ flip))) for de, turn in hops
        ]

        def block(e, a, b, kind, turn):
            return col_index(e, a ^ (second if kind else turn), b ^ (turn if kind else second), kind)

        place_at[q] = consts.add(lambda z, e, a, b, c: block(e, a, b, c ^ flip, 0))
        arrive_at[q] = [
            consts.add(lambda z, e, a, b, c: block((e - de) % extra, a, b, c ^ flip, turn)) for de, turn in hops[1:]
        ]
    flags_at = {}
    for j in range(rows - 1):
        kinds = sorted({order[i][j][0] for i in range(rows)})
        for kind in kinds[:-1]:
            flags_at[j, kind] = consts.add(lambda z, e, a, b, c: order[z][j][0] == kind)
    scalars = consts.of_device(lax.axis_index("row"), lax.axis_index("col"), cols)

    own_lists = int_tiles[:, 0, :]
    row = lax.axis_index("row").astype(jnp.int32).reshape(1)
    packed, packed_again, amp_used = pack(row, own_lists, amp_mask, integrals, amplitudes)

    moved = []

    def line_phase(moves, own):
        return [lax.ppermute(own if source < 0 else moved[source], "row", pairs) for source, pairs in moves]

    fresh = line_phase(phases[0], packed)
    amp_next = permute(amp_used, along)
    amp_other = permute(amp_used, other)
    amps = [amp_used, amp_next, amp_other, permute(amp_next, other)]
    for de in range(1, extra):
        amps += [permute(amp, lambda e, a, b, c: ((e - de) % extra, a, b, c)) for amp in amps[:4]]

    count = own_lists.shape[1]
    tiles = (int_rows // TILE) * (int_cols // TILE)
    found = own_lists[:, None, :] == jnp.arange(tiles, dtype=jnp.int32)[None, :, None]
    own_table = jnp.min(jnp.where(found, jnp.arange(count, dtype=jnp.int32), count), axis=2)

    col_ids = jnp.arange(cols, dtype=jnp.int32)
    onehot = (pair_dest[:, None] == col_ids[None, :]).astype(jnp.int32)
    before = jnp.cumsum(onehot, axis=0) - onehot
    target = pair_dest * capacity + jnp.sum(before * onehot, axis=1)

    mine, for_them = pick_rows(scalars, wanted_at, len(turns), target, amps, capacity)
    slots, nexts, theirs_of, theirs_next = [packed], [permute(packed, along)], [permute(packed, across)], []
    for at, moves in enumerate(phases):
        if at > 0:
            fresh = line_phase(moves, packed_again)
        if at == 0:
            waited = (mine, nexts[0], theirs_of[0])
            fresh[0] = tie(fresh[0], mine)
        elif at == 1:
            theirs = permute(for_them, across)
            own_table = tie(own_table, *nexts[1:])
            table_next = permute(own_table, along)
            pair_tables = permute(jnp.concatenate([own_table, table_next], axis=0), across)
            waited = (theirs, table_next, *theirs_of[1:], *nexts[1:])
            theirs_next.append(permute(nexts[0], across))
            waited = (theirs, table_next, *nexts[1:], *theirs_of[1:], *theirs_next)
        else:
            waited = (*nexts[-1:], *theirs_of[-1:])
            while len(theirs_next) < len(nexts) - 1:
                theirs_next.append(permute(nexts[len(theirs_next)], across))
                waited = (*waited, theirs_next[-1])
        tied = []
        for i, value in enumerate(fresh):
            if at > 0 or i > 0:
                value = tie(value, *waited, *fresh[i + 1 :], *(tied[:1] if at > 0 else ()))
            tied.append(value)
        moved += tied
        if at == 0:
            packed_again = tie(packed_again, moved[-1])
        while len(slots) < rows and all(order[i][len(slots) - 1][0] < len(moved) for i in range(rows)):
            j = len(slots) - 1
            kinds = sorted({order[i][j][0] for i in range(rows)})
            slot = moved[kinds[-1]]
            for kind in kinds[:-1]:
                slot = choose(scalars, flags_at[j, kind], moved[kind], slot)
            slots.append(slot)
            nexts.append(permute(slot, along))
            theirs_of.append(permute(slot, across))

    out = None
    arrived = []
    for turn_at, q in enumerate((0, 2, 1, 3)):
        if turn_at >= 2:
            out = tie(out, *arrived[turn_at - 2])
        out, *pieces = product(
            scalars,
            (own_table, table_next, pair_tables, pair_tables)[q],
            mine,
            theirs,
            (slots, nexts, theirs_of, theirs_next)[q],
            int_cols,
            cols * int_cols,
            out,
            (core_at, picks_at[q], rows_at if q < 3 else low_rows_at, mine_at, theirs_at),
            place_at[q],
        )
        arrived.append([])
        for (de, turn), piece in zip(hops[1:], pieces):
            def sent_to(e, a, b, c):
                kind = c ^ int(q >= 2)
                return (e + de) % extra, a ^ (0 if kind else turn), b ^ (turn if kind else 0), c

            arrived[-1].append(permute(piece, sent_to))
        if q in (0, 2):
            while len(theirs_next) < rows - (q == 0):
                nexts[len(theirs_next)] = tie(nexts[len(theirs_next)], pieces[0])
                theirs_next.append(permute(nexts[len(theirs_next)], across))
    for got, q in zip(arrived, (0, 2, 1, 3)):
        for piece, place in zip(got, arrive_at[q]):
            out = put(piece, out, scalars, place)
    return out


def solution(mesh):
    in_specs = (P("row", "col"), P("row", "col"), P("row", "col"), P(None, "col", None), P("row"))
    out_specs = P(("row", "col"), None)
    return jax.shard_map(
        on_device, mesh=mesh, in_specs=in_specs, out_specs=out_specs, check_vma=False
    )
```

```python
import functools

import jax
import jax.numpy as jnp
import numpy as np
from jax import lax
from jax.experimental import pallas as pl
from jax.experimental.pallas import tpu as pltpu
from jax.sharding import PartitionSpec as P

TILE = 128
NOTHING = pl.CostEstimate(flops=0, bytes_accessed=0, transcendentals=0)
MM_COLS = 512
VMEM_LIMIT = (64 << 20) - (256 << 10)


def params():
    return pltpu.CompilerParams(vmem_limit_bytes=VMEM_LIMIT)


def pack_body(row, ids_ref, mask_ref, src_ref, amp_ref, out_ref, again_ref, used_ref):
    col_tiles = src_ref.shape[1] // TILE
    tiles = col_tiles * (src_ref.shape[0] // TILE)
    for e in range(out_ref.shape[0]):
        t = jnp.minimum(ids_ref[row[0], e], tiles - 1)
        k = pl.multiple_of(lax.div(t, col_tiles) * TILE, TILE)
        n = pl.multiple_of(lax.rem(t, col_tiles) * TILE, TILE)
        out_ref[e] = again_ref[e] = src_ref[pl.ds(k, TILE), pl.ds(n, TILE)]
    for k in range(mask_ref.shape[0]):
        for a in range(mask_ref.shape[1]):
            at = (slice(a * TILE, (a + 1) * TILE), slice(k * TILE, (k + 1) * TILE))
            scale = mask_ref[k, a].astype(jnp.float32)
            used_ref[at] = (amp_ref[at].astype(jnp.float32) * scale).astype(used_ref.dtype)


def pack(row, lists, mask, integrals, amplitudes):
    count = lists.shape[1]
    smem, vmem = pl.BlockSpec(memory_space=pltpu.SMEM), pl.BlockSpec(memory_space=pltpu.VMEM)
    return pl.pallas_call(
        pack_body,
        out_shape=[
            jax.ShapeDtypeStruct((count, TILE, TILE), integrals.dtype),
            jax.ShapeDtypeStruct((count, TILE, TILE), integrals.dtype),
            jax.ShapeDtypeStruct(amplitudes.shape, amplitudes.dtype),
        ],
        in_specs=[smem, smem, smem, vmem, vmem],
        out_specs=[vmem, vmem, vmem],
        compiler_params=params(),
        cost_estimate=NOTHING,
        name="pack_tiles",
    )(row, lists, mask.T, integrals, amplitudes)


def pick_body(first, capacity, scalars, target_ref, *refs):
    amps, (mine, theirs) = refs[:-2], refs[-2:]
    step = pl.program_id(0)
    half = pl.num_programs(0) // 2
    rows = scalars[first + step] * capacity + lax.broadcasted_iota(jnp.int32, (capacity, target_ref.shape[1]), 0)
    chosen = jnp.where(rows == target_ref[...], 1.0, 0.0).astype(mine.dtype)
    for at, amp in enumerate(amps):
        value = jnp.dot(chosen, amp[...], preferred_element_type=jnp.float32).astype(mine.dtype)

        @pl.when(step < half)
        def _():
            theirs[at, 0] = value

        @pl.when(step >= half)
        def _():
            mine[at, 0] = value


def pick_rows(scalars, first, count, target, amps, capacity):
    n, k = amps[0].shape
    shape = jax.ShapeDtypeStruct((len(amps), count, capacity, k), amps[0].dtype)
    block = (len(amps), 1, capacity, k)
    return pl.pallas_call(
        functools.partial(pick_body, first, capacity),
        out_shape=[shape, shape],
        grid_spec=pltpu.PrefetchScalarGridSpec(
            num_scalar_prefetch=1,
            grid=(2 * count,),
            in_specs=[pl.BlockSpec((1, n), lambda i, s: (0, 0))]
            + [pl.BlockSpec((n, k), lambda i, s: (0, 0)) for _ in amps],
            out_specs=[
                pl.BlockSpec(block, lambda i, s: (0, jnp.maximum(i - count, 0), 0, 0)),
                pl.BlockSpec(block, lambda i, s: (0, jnp.minimum(i, count - 1), 0, 0)),
            ],
        ),
        compiler_params=params(),
        cost_estimate=NOTHING,
        name="pick_rows",
    )(scalars, target.reshape(1, n), *amps)


def product_body(at, has_acc, has_whole, final, scalars, table, mine, theirs, *refs):
    core_at, picks, rows_at, mine_at, theirs_at = at
    slot_count = len(rows_at)
    packed_hbm = refs[:slot_count]
    acc = refs[slot_count] if has_acc else None
    refs = refs[slot_count + has_acc + has_whole :]
    outs, (lhs_all, rhs_all, packed, lhs_sem, sems) = refs[:-5], refs[-5:]
    step = pl.program_id(0)
    capacity, part = mine.shape[2:]
    depth = lhs_all.shape[1] // slot_count
    width = rhs_all.shape[1]
    count = packed.shape[1]
    col_tiles = table.shape[1] // (depth // TILE)

    @pl.when(step == 0)
    def _():
        for s in range(slot_count):
            pltpu.make_async_copy(packed_hbm[s], packed.at[s], sems.at[s]).start()
        for s in range(slot_count):
            for source, chip, side in (
                (mine, scalars[mine_at[s]], scalars[core_at]),
                (theirs, scalars[theirs_at[s]], 1 - scalars[core_at]),
            ):
                lanes = pl.ds(pl.multiple_of(s * depth + side * part, part), part)
                for t, pick in enumerate(picks):
                    pltpu.make_async_copy(
                        source.at[chip, scalars[pick]], lhs_all.at[pl.ds(t * capacity, capacity), lanes], lhs_sem
                    ).start()
        for s in range(slot_count):
            pltpu.make_async_copy(packed_hbm[s], packed.at[s], sems.at[s]).wait()
        pltpu.make_async_copy(lhs_all, lhs_all, lhs_sem).wait()

    for s in range(slot_count):
        row = scalars[rows_at[s]]
        for k in range(depth // TILE):
            for n in range(width // TILE):
                e = table[row, k * col_tiles + step * (width // TILE) + n]
                tile = packed[s, jnp.minimum(e, count - 1)]
                rhs_all[s * depth + k * TILE : s * depth + (k + 1) * TILE, n * TILE : (n + 1) * TILE] = jnp.where(
                    e < count, tile, jnp.zeros_like(tile)
                )
    total = jnp.dot(lhs_all[...], rhs_all[...], preferred_element_type=jnp.float32)
    if has_acc:
        total = acc[...] + total
    if not final:
        outs[0][...] = total
        return
    for t in range(len(picks)):
        outs[t][...] = total[t * capacity : (t + 1) * capacity].astype(outs[t].dtype)


def product(scalars, table, mine, theirs, slots, int_cols, at, acc=None, whole_cols=None, whole=None, place_at=None):
    core_at, picks, rows_at, mine_at, theirs_at = at
    capacity, part = mine.shape[2:]
    slot_count, m = len(slots), len(picks) * capacity
    depth = 2 * part
    width = min(MM_COLS, int_cols)
    steps = int_cols // width
    hbm = pl.BlockSpec(memory_space=pltpu.HBM)
    operands = [scalars, table, mine, theirs, *slots]
    in_specs = [hbm] * (len(operands) - 2)
    aliases = {}
    chunk = pl.BlockSpec((m, width), lambda i, sc, tab: (0, i))
    if acc is not None:
        in_specs.append(chunk)
        operands.append(acc)
    if whole is not None:
        aliases = {len(operands): 0}
        in_specs.append(hbm)
        operands.append(whole)
    final = whole_cols is not None
    out_specs = [chunk]
    out_shape = [jax.ShapeDtypeStruct((m, int_cols), jnp.float32)]
    if final:
        out_specs = [pl.BlockSpec((capacity, width), lambda i, sc, tab: (0, sc[place_at] * steps + i))]
        out_shape = [jax.ShapeDtypeStruct((capacity, whole_cols), mine.dtype)]
    for _ in picks[1:] if final else ():
        out_specs.append(pl.BlockSpec((capacity, width), lambda i, sc, tab: (0, i)))
        out_shape.append(jax.ShapeDtypeStruct((capacity, int_cols), mine.dtype))
    k = slot_count * depth
    return pl.pallas_call(
        functools.partial(product_body, at, acc is not None, whole is not None, final),
        out_shape=out_shape,
        grid_spec=pltpu.PrefetchScalarGridSpec(
            num_scalar_prefetch=2,
            grid=(steps,),
            in_specs=in_specs,
            out_specs=out_specs,
            scratch_shapes=[
                pltpu.VMEM((m, k), mine.dtype),
                pltpu.VMEM((k, width), mine.dtype),
                pltpu.VMEM((slot_count, *slots[0].shape), mine.dtype),
                pltpu.SemaphoreType.DMA,
                pltpu.SemaphoreType.DMA((slot_count,)),
            ],
        ),
        input_output_aliases=aliases,
        compiler_params=params(),
        cost_estimate=NOTHING,
        name="product",
    )(*operands)


def tie_body(*refs):
    pass


def tie(value, *others):
    return pl.pallas_call(
        tie_body,
        out_shape=jax.ShapeDtypeStruct(value.shape, value.dtype),
        in_specs=[pl.BlockSpec(memory_space=pltpu.HBM)] * (1 + len(others)),
        out_specs=pl.BlockSpec(memory_space=pltpu.HBM),
        input_output_aliases={0: 0},
        compiler_params=params(),
        cost_estimate=NOTHING,
        name="tie",
    )(value, *others)


def choose_body(at, scalars, a_ref, b_ref, out_ref, sem):
    @pl.when(scalars[at] != 0)
    def _():
        pltpu.make_async_copy(a_ref, out_ref, sem).start()

    @pl.when(scalars[at] == 0)
    def _():
        pltpu.make_async_copy(b_ref, out_ref, sem).start()

    pltpu.make_async_copy(a_ref, out_ref, sem).wait()


def choose(scalars, at, a, b):
    hbm = pl.BlockSpec(memory_space=pltpu.HBM)
    return pl.pallas_call(
        functools.partial(choose_body, at),
        out_shape=jax.ShapeDtypeStruct(a.shape, a.dtype),
        in_specs=[pl.BlockSpec(memory_space=pltpu.SMEM), hbm, hbm],
        out_specs=pl.BlockSpec(memory_space=pltpu.VMEM),
        scratch_shapes=[pltpu.SemaphoreType.DMA],
        compiler_params=params(),
        cost_estimate=NOTHING,
        name="choose",
    )(scalars, a, b)


def put_body(scalars, piece_ref, whole_ref, out_ref):
    out_ref[...] = piece_ref[...]


def put(piece, whole, scalars, at):
    m, n = piece.shape
    width = min(2 * MM_COLS, n)
    steps = n // width
    return pl.pallas_call(
        put_body,
        out_shape=jax.ShapeDtypeStruct(whole.shape, whole.dtype),
        grid_spec=pltpu.PrefetchScalarGridSpec(
            num_scalar_prefetch=1,
            grid=(steps,),
            in_specs=[pl.BlockSpec((m, width), lambda i, s: (0, i)), pl.BlockSpec(memory_space=pltpu.HBM)],
            out_specs=pl.BlockSpec((m, width), lambda i, s: (0, s[at] * steps + i)),
        ),
        input_output_aliases={2: 0},
        compiler_params=params(),
        cost_estimate=NOTHING,
        name="put",
    )(scalars, piece, whole)


def col_index(ie, ia, ib, core):
    return ((ie * 2 + ia) * 2 + ib) * 2 + core


class Scalars:
    def __init__(self, rows, cols):
        self.places = [(z, me // 8, me // 4 % 2, me // 2 % 2, me % 2) for z in range(rows) for me in range(cols)]
        self.columns = []

    def add(self, value_of):
        self.columns.append([int(value_of(*place)) for place in self.places])
        return len(self.columns) - 1

    def of_device(self, z, me, cols):
        table = np.array(self.columns, np.int32).T
        return lax.dynamic_slice(jnp.asarray(table), (z * cols + me, 0), (1, table.shape[1]))[0]


def line_schedule(rows):
    if rows == 4:
        phases = [
            [(-1, [(0, 1), (1, 0), (2, 3), (3, 2)]), (-1, [(0, 2), (2, 0), (1, 3), (3, 1)])],
            [(-1, [(1, 2), (2, 1)]), (1, [(1, 0), (2, 3)])],
        ]
    else:
        partner = ({}, {})
        for i in range(rows):
            if i ^ 1 < rows:
                partner[0][i] = i ^ 1
            if 0 <= ((i + 1) ^ 1) - 1 < rows:
                partner[1][i] = ((i + 1) ^ 1) - 1
        phases, reached, last, count = [], (set(range(rows)), set(range(rows))), (-1, -1), 0
        while True:
            moves, now, fresh = [], [-1, -1], (set(), set())
            for side in (0, 1):
                pairs = [(p, i) for i, p in partner[side].items() if p in reached[1 - side]]
                fresh[side].update(i for _, i in pairs)
                if pairs:
                    moves.append((last[1 - side], pairs))
                    now[side] = count
                    count += 1
            if not moves:
                break
            phases.append(moves)
            reached, last = fresh, tuple(now)
    arrivals = [[] for _ in range(rows)]
    blocks = []
    for moves in phases:
        for source, pairs in moves:
            got = {b: a if source < 0 else blocks[source][a] for a, b in pairs}
            blocks.append(got)
            for i, block in got.items():
                arrivals[i].append((len(blocks) - 1, block))
    return phases, arrivals


def on_device(amplitudes, amp_mask, integrals, int_tiles, pair_dest):
    rows = lax.axis_size("row")
    cols = lax.axis_size("col")
    extra = cols // 8
    pair_rows, amp_cols = amplitudes.shape
    int_rows, int_cols = integrals.shape
    capacity = 2 * pair_rows // cols
    every = [(e, a, b, c) for e in range(extra) for a in range(2) for b in range(2) for c in range(2)]
    chips = [(e, a, b) for e in range(extra) for a in range(2) for b in range(2)]
    hops = [(de, turn) for de in range(extra) for turn in (0, 1)]
    turns = [(de, da, db) for de in range(extra) for da, db in ((0, 0), (1, 0), (0, 1))]
    phases, order = line_schedule(rows)

    def permute(value, moved_to):
        return lax.ppermute(value, "col", [(col_index(*at), col_index(*moved_to(*at))) for at in every])

    def along(e, a, b, c):
        return e, a ^ (c == 1), b ^ (c == 0), c

    def other(e, a, b, c):
        return e, a ^ (c == 0), b ^ (c == 1), c

    def across(e, a, b, c):
        return e, a, b, 1 - c

    consts = Scalars(rows, cols)
    core_at = consts.add(lambda z, e, a, b, c: c)
    wanted_at = len(consts.columns)
    for flip in (1, 0):
        for de, da, db in turns:
            consts.add(lambda z, e, a, b, c: col_index((e + de) % extra, a ^ da, b ^ db, c ^ flip))
    slot_rows = [lambda z: z] + [functools.partial(lambda j, z: order[z][j][1], j) for j in range(rows - 1)]
    rows_at = [consts.add(lambda z, e, a, b, c: row(z)) for row in slot_rows]
    low_rows_at = [consts.add(lambda z, e, a, b, c: rows + row(z)) for row in slot_rows]
    gathered = [(de, p, q) for de in range(extra) for q in (0, 1) for p in (0, 1)]

    def arrival(chip, e, a, b, c):
        ce, ca, cb = chips[chip]
        p, q = (cb ^ b, ca ^ a) if c == 0 else (ca ^ a, cb ^ b)
        return gathered.index(((ce - e) % extra, p, q))

    mine_at = [consts.add(lambda z, e, a, b, c: arrival(row(z), e, a, b, c)) for row in slot_rows]
    theirs_at = [consts.add(lambda z, e, a, b, c: arrival(row(z), e, a, b, 1 - c)) for row in slot_rows]
    picks_at, place_at, arrive_at = {}, {}, {}
    for q in range(4):
        flip, second = int(q >= 2), q % 2
        picks_at[q] = [
            consts.add(lambda z, e, a, b, c: 3 * de + turn * (1 + (c ^ flip))) for de, turn in hops
        ]

        def block(e, a, b, kind, turn):
            return col_index(e, a ^ (second if kind else turn), b ^ (turn if kind else second), kind)

        place_at[q] = consts.add(lambda z, e, a, b, c: block(e, a, b, c ^ flip, 0))
        arrive_at[q] = [
            consts.add(lambda z, e, a, b, c: block((e - de) % extra, a, b, c ^ flip, turn)) for de, turn in hops[1:]
        ]
    flags_at = {}
    for j in range(rows - 1):
        kinds = sorted({order[i][j][0] for i in range(rows)})
        for kind in kinds[:-1]:
            flags_at[j, kind] = consts.add(lambda z, e, a, b, c: order[z][j][0] == kind)
    scalars = consts.of_device(lax.axis_index("row"), lax.axis_index("col"), cols)

    own_lists = int_tiles[:, 0, :]
    row = lax.axis_index("row").astype(jnp.int32).reshape(1)
    packed, packed_again, amp_used = pack(row, own_lists, amp_mask, integrals, amplitudes)

    moved = []

    def line_phase(moves, own):
        return [lax.ppermute(own if source < 0 else moved[source], "row", pairs) for source, pairs in moves]

    fresh = line_phase(phases[0], packed)
    amp_next = permute(amp_used, along)
    amp_other = permute(amp_used, other)
    amps = [amp_used, amp_next, amp_other, permute(amp_next, other)]
    for de in range(1, extra):
        amps += [permute(amp, lambda e, a, b, c: ((e - de) % extra, a, b, c)) for amp in amps[:4]]

    count = own_lists.shape[1]
    tiles = (int_rows // TILE) * (int_cols // TILE)
    found = own_lists[:, None, :] == jnp.arange(tiles, dtype=jnp.int32)[None, :, None]
    own_table = jnp.min(jnp.where(found, jnp.arange(count, dtype=jnp.int32), count), axis=2)

    col_ids = jnp.arange(cols, dtype=jnp.int32)
    onehot = (pair_dest[:, None] == col_ids[None, :]).astype(jnp.int32)
    before = jnp.cumsum(onehot, axis=0) - onehot
    target = pair_dest * capacity + jnp.sum(before * onehot, axis=1)

    mine, for_them = pick_rows(scalars, wanted_at, len(turns), target, amps, capacity)
    sums = None
    slots, nexts, theirs_of, theirs_next = [packed], [permute(packed, along)], [permute(packed, across)], []
    for at, moves in enumerate(phases):
        if at > 0:
            fresh = line_phase(moves, packed_again)
        if at == 0:
            own_table = tie(own_table, amp_next)
            table_next = permute(own_table, along)
            pair_tables = permute(jnp.concatenate([own_table, table_next], axis=0), across)
            waited = (mine, nexts[0], theirs_of[0], pair_tables)
            fresh[0] = tie(fresh[0], mine, fresh[1])
        elif at == 1:
            theirs = permute(for_them, across)
            waited = (theirs, *nexts[1:])
        else:
            waited = (*nexts[-1:], *theirs_of[-1:])
            while len(theirs_next) < len(nexts) - 1:
                theirs_next.append(permute(nexts[len(theirs_next)], across))
                waited = (*waited, theirs_next[-1])
        if at == len(phases) - 1:
            parts = (core_at, picks_at[0], *(places[: rows - 1] for places in (rows_at, mine_at, theirs_at)))
            (sums,) = product(scalars, own_table, mine, theirs, slots, int_cols, parts)
            waited = (*waited, sums)
        tied = []
        for i, value in enumerate(fresh):
            if at > 0 or i > 0:
                value = tie(value, *waited, *fresh[i + 1 :], *(tied[:1] if at > 0 else ()))
            tied.append(value)
        moved += tied
        if at == 0:
            packed_again = tie(packed_again, moved[-1])
        while len(slots) < rows and all(order[i][len(slots) - 1][0] < len(moved) for i in range(rows)):
            j = len(slots) - 1
            kinds = sorted({order[i][j][0] for i in range(rows)})
            slot = moved[kinds[-1]]
            for kind in kinds[:-1]:
                slot = choose(scalars, flags_at[j, kind], moved[kind], slot)
            slots.append(slot)
            nexts.append(permute(slot, along))
            theirs_of.append(permute(slot, across))

    out = None
    arrived = []
    for turn_at, q in enumerate((0, 2, 1, 3)):
        if turn_at >= 2:
            out = tie(out, *arrived[turn_at - 2])
        parts = (core_at, picks_at[q], rows_at if q < 3 else low_rows_at, mine_at, theirs_at)
        blocks = (slots, nexts, theirs_of, theirs_next)[q]
        if q == 0 and rows > 1:
            blocks, parts = blocks[-1:], (*parts[:2], *(places[-1:] for places in parts[2:]))
        out, *pieces = product(
            scalars,
            (own_table, table_next, pair_tables, pair_tables)[q],
            mine,
            theirs,
            blocks,
            int_cols,
            parts,
            acc=sums if q == 0 else None,
            whole_cols=cols * int_cols,
            whole=out,
            place_at=place_at[q],
        )
        arrived.append([])
        for (de, turn), piece in zip(hops[1:], pieces):
            def sent_to(e, a, b, c):
                kind = c ^ int(q >= 2)
                return (e + de) % extra, a ^ (0 if kind else turn), b ^ (turn if kind else 0), c

            arrived[-1].append(permute(piece, sent_to))
        if q in (0, 2):
            while len(theirs_next) < rows - (q == 0):
                nexts[len(theirs_next)] = tie(nexts[len(theirs_next)], pieces[0])
                theirs_next.append(permute(nexts[len(theirs_next)], across))
    for got, q in zip(arrived, (0, 2, 1, 3)):
        for piece, place in zip(got, arrive_at[q]):
            out = put(piece, out, scalars, place)
    return out


def solution(mesh):
    in_specs = (P("row", "col"), P("row", "col"), P("row", "col"), P(None, "col", None), P("row"))
    out_specs = P(("row", "col"), None)
    return jax.shard_map(
        on_device, mesh=mesh, in_specs=in_specs, out_specs=out_specs, check_vma=False
    )
```

```python
import functools

import jax
import jax.numpy as jnp
import numpy as np
from jax import lax
from jax.experimental import pallas as pl
from jax.experimental.pallas import tpu as pltpu
from jax.sharding import PartitionSpec as P

TILE = 128
NOTHING = pl.CostEstimate(flops=0, bytes_accessed=0, transcendentals=0)
MM_COLS = 512
VMEM_LIMIT = (64 << 20) - (256 << 10)


def params():
    return pltpu.CompilerParams(vmem_limit_bytes=VMEM_LIMIT)


def pack_body(row, ids_ref, mask_ref, src_ref, amp_ref, out_ref, again_ref, used_ref):
    col_tiles = src_ref.shape[1] // TILE
    tiles = col_tiles * (src_ref.shape[0] // TILE)
    for e in range(out_ref.shape[0]):
        t = jnp.minimum(ids_ref[row[0], e], tiles - 1)
        k = pl.multiple_of(lax.div(t, col_tiles) * TILE, TILE)
        n = pl.multiple_of(lax.rem(t, col_tiles) * TILE, TILE)
        out_ref[e] = again_ref[e] = src_ref[pl.ds(k, TILE), pl.ds(n, TILE)]
    for k in range(mask_ref.shape[0]):
        for a in range(mask_ref.shape[1]):
            at = (slice(a * TILE, (a + 1) * TILE), slice(k * TILE, (k + 1) * TILE))
            scale = mask_ref[k, a].astype(jnp.float32)
            used_ref[at] = (amp_ref[at].astype(jnp.float32) * scale).astype(used_ref.dtype)


def pack(row, lists, mask, integrals, amplitudes):
    count = lists.shape[1]
    smem, vmem = pl.BlockSpec(memory_space=pltpu.SMEM), pl.BlockSpec(memory_space=pltpu.VMEM)
    return pl.pallas_call(
        pack_body,
        out_shape=[
            jax.ShapeDtypeStruct((count, TILE, TILE), integrals.dtype),
            jax.ShapeDtypeStruct((count, TILE, TILE), integrals.dtype),
            jax.ShapeDtypeStruct(amplitudes.shape, amplitudes.dtype),
        ],
        in_specs=[smem, smem, smem, vmem, vmem],
        out_specs=[vmem, vmem, vmem],
        compiler_params=params(),
        cost_estimate=NOTHING,
        name="pack_tiles",
    )(row, lists, mask.T, integrals, amplitudes)


def pick_body(first, count, capacity, scalars, target_ref, *refs):
    amps, (mine, theirs, chosen) = refs[:-3], refs[-3:]
    step = pl.program_id(0)
    slot = lax.broadcasted_iota(jnp.int32, (capacity, target_ref.shape[1]), 0)
    for d in range(count):
        wanted = scalars[first + step * count + d] * capacity + slot
        chosen[d * capacity : (d + 1) * capacity] = jnp.where(wanted == target_ref[...], 1.0, 0.0).astype(chosen.dtype)
    for at, amp in enumerate(amps):
        value = jnp.dot(chosen[...], amp[...], preferred_element_type=jnp.float32).astype(mine.dtype)
        value = value.reshape(count, capacity, amp.shape[1])

        @pl.when(step == 0)
        def _():
            theirs[at] = value

        @pl.when(step == 1)
        def _():
            mine[at] = value


def pick_rows(scalars, first, count, target, amps, capacity):
    n, k = amps[0].shape
    shape = jax.ShapeDtypeStruct((len(amps), count, capacity, k), amps[0].dtype)
    whole = pl.BlockSpec(shape.shape, lambda i, s: (0, 0, 0, 0))
    return pl.pallas_call(
        functools.partial(pick_body, first, count, capacity),
        out_shape=[shape, shape],
        grid_spec=pltpu.PrefetchScalarGridSpec(
            num_scalar_prefetch=1,
            grid=(2,),
            in_specs=[pl.BlockSpec((1, n), lambda i, s: (0, 0))]
            + [pl.BlockSpec((n, k), lambda i, s: (0, 0)) for _ in amps],
            out_specs=[whole, whole],
            scratch_shapes=[pltpu.VMEM((count * capacity, n), amps[0].dtype)],
        ),
        compiler_params=params(),
        cost_estimate=NOTHING,
        name="pick_rows",
    )(scalars, target.reshape(1, n), *amps)


class Numbers:
    def __init__(self, ref, base):
        self.ref, self.base = ref, base

    def __getitem__(self, at):
        width = self.ref.shape[1]
        return self.ref[self.base + at // width, at % width]


def product_body(at, has_acc, has_whole, final, numbers, mine, theirs, *refs):
    core_at, picks, rows_at, mine_at, theirs_at, tiles, base = at
    slot_count = len(rows_at)
    scalars = Numbers(numbers, base)
    packed_hbm = refs[:slot_count]
    acc = refs[slot_count] if has_acc else None
    refs = refs[slot_count + has_acc + has_whole :]
    outs, (lhs_all, rhs_all, packed, lhs_sem, sems) = refs[:-5], refs[-5:]
    step = pl.program_id(0)
    capacity, part = mine.shape[2:]
    depth = lhs_all.shape[1] // slot_count
    width = rhs_all.shape[1]
    count = packed.shape[1]
    col_tiles = tiles // (depth // TILE)

    @pl.when(step == 0)
    def _():
        for s in range(slot_count):
            pltpu.make_async_copy(packed_hbm[s], packed.at[s], sems.at[s]).start()
        for s in range(slot_count):
            for source, chip, side in (
                (mine, scalars[mine_at[s]], scalars[core_at]),
                (theirs, scalars[theirs_at[s]], 1 - scalars[core_at]),
            ):
                lanes = pl.ds(pl.multiple_of(s * depth + side * part, part), part)
                for t, pick in enumerate(picks):
                    pltpu.make_async_copy(
                        source.at[chip, scalars[pick]], lhs_all.at[pl.ds(t * capacity, capacity), lanes], lhs_sem
                    ).start()
    for s in range(slot_count):
        @pl.when(step == 0)
        def _():
            pltpu.make_async_copy(packed_hbm[s], packed.at[s], sems.at[s]).wait()

        row = scalars[rows_at[s]]
        for k in range(depth // TILE):
            for n in range(width // TILE):
                e = numbers[row, k * col_tiles + step * (width // TILE) + n]
                tile = packed[s, jnp.minimum(e, count - 1)]
                rhs_all[s * depth + k * TILE : s * depth + (k + 1) * TILE, n * TILE : (n + 1) * TILE] = jnp.where(
                    e < count, tile, jnp.zeros_like(tile)
                )

    @pl.when(step == 0)
    def _():
        pltpu.make_async_copy(lhs_all, lhs_all, lhs_sem).wait()

    total = jnp.dot(lhs_all[...], rhs_all[...], preferred_element_type=jnp.float32)
    if has_acc:
        total = acc[...] + total
    if not final:
        outs[0][...] = total
        return
    for t in range(len(picks)):
        outs[t][...] = total[t * capacity : (t + 1) * capacity].astype(outs[t].dtype)


def product(numbers, mine, theirs, slots, int_cols, at, acc=None, whole_cols=None, whole=None, place_at=None):
    picks, base = at[1], at[-1]
    capacity, part = mine.shape[2:]
    slot_count, m = len(slots), len(picks) * capacity
    depth = 2 * part
    width = min(MM_COLS, int_cols)
    steps = int_cols // width
    hbm = pl.BlockSpec(memory_space=pltpu.HBM)
    operands = [numbers, mine, theirs, *slots]
    in_specs = [hbm] * (len(operands) - 1)
    aliases = {}
    chunk = pl.BlockSpec((m, width), lambda i, numbers: (0, i))
    if acc is not None:
        in_specs.append(chunk)
        operands.append(acc)
    if whole is not None:
        aliases = {len(operands): 0}
        in_specs.append(hbm)
        operands.append(whole)
    final = whole_cols is not None
    out_specs = [chunk]
    out_shape = [jax.ShapeDtypeStruct((m, int_cols), jnp.float32)]
    if final:
        out_specs = [pl.BlockSpec((capacity, width), lambda i, numbers: (0, Numbers(numbers, base)[place_at] * steps + i))]
        out_shape = [jax.ShapeDtypeStruct((capacity, whole_cols), mine.dtype)]
    for _ in picks[1:] if final else ():
        out_specs.append(pl.BlockSpec((capacity, width), lambda i, numbers: (0, i)))
        out_shape.append(jax.ShapeDtypeStruct((capacity, int_cols), mine.dtype))
    k = slot_count * depth
    return pl.pallas_call(
        functools.partial(product_body, at, acc is not None, whole is not None, final),
        out_shape=out_shape,
        grid_spec=pltpu.PrefetchScalarGridSpec(
            num_scalar_prefetch=1,
            grid=(steps,),
            in_specs=in_specs,
            out_specs=out_specs,
            scratch_shapes=[
                pltpu.VMEM((m, k), mine.dtype),
                pltpu.VMEM((k, width), mine.dtype),
                pltpu.VMEM((slot_count, *slots[0].shape), mine.dtype),
                pltpu.SemaphoreType.DMA,
                pltpu.SemaphoreType.DMA((slot_count,)),
            ],
        ),
        input_output_aliases=aliases,
        compiler_params=params(),
        cost_estimate=NOTHING,
        name="product",
    )(*operands)


def tie_body(*refs):
    pass


def tie(value, *others):
    return pl.pallas_call(
        tie_body,
        out_shape=jax.ShapeDtypeStruct(value.shape, value.dtype),
        in_specs=[pl.BlockSpec(memory_space=pltpu.HBM)] * (1 + len(others)),
        out_specs=pl.BlockSpec(memory_space=pltpu.HBM),
        input_output_aliases={0: 0},
        compiler_params=params(),
        cost_estimate=NOTHING,
        name="tie",
    )(value, *others)


def choose_body(at, scalars, a_ref, b_ref, out_ref, sem):
    @pl.when(scalars[at] != 0)
    def _():
        pltpu.make_async_copy(a_ref, out_ref, sem).start()

    @pl.when(scalars[at] == 0)
    def _():
        pltpu.make_async_copy(b_ref, out_ref, sem).start()

    pltpu.make_async_copy(a_ref, out_ref, sem).wait()


def choose(scalars, at, a, b):
    hbm = pl.BlockSpec(memory_space=pltpu.HBM)
    return pl.pallas_call(
        functools.partial(choose_body, at),
        out_shape=jax.ShapeDtypeStruct(a.shape, a.dtype),
        in_specs=[pl.BlockSpec(memory_space=pltpu.SMEM), hbm, hbm],
        out_specs=pl.BlockSpec(memory_space=pltpu.VMEM),
        scratch_shapes=[pltpu.SemaphoreType.DMA],
        compiler_params=params(),
        cost_estimate=NOTHING,
        name="choose",
    )(scalars, a, b)


def put_body(scalars, piece_ref, whole_ref, out_ref):
    out_ref[...] = piece_ref[...]


def put(piece, whole, scalars, at):
    m, n = piece.shape
    width = min(2 * MM_COLS, n)
    steps = n // width
    return pl.pallas_call(
        put_body,
        out_shape=jax.ShapeDtypeStruct(whole.shape, whole.dtype),
        grid_spec=pltpu.PrefetchScalarGridSpec(
            num_scalar_prefetch=1,
            grid=(steps,),
            in_specs=[pl.BlockSpec((m, width), lambda i, s: (0, i)), pl.BlockSpec(memory_space=pltpu.HBM)],
            out_specs=pl.BlockSpec((m, width), lambda i, s: (0, s[at] * steps + i)),
        ),
        input_output_aliases={2: 0},
        compiler_params=params(),
        cost_estimate=NOTHING,
        name="put",
    )(scalars, piece, whole)


def col_index(ie, ia, ib, core):
    return ((ie * 2 + ia) * 2 + ib) * 2 + core


class Scalars:
    def __init__(self, rows, cols):
        self.places = [(z, me // 8, me // 4 % 2, me // 2 % 2, me % 2) for z in range(rows) for me in range(cols)]
        self.columns = []

    def add(self, value_of):
        self.columns.append([int(value_of(*place)) for place in self.places])
        return len(self.columns) - 1

    def of_device(self, z, me, cols):
        table = np.array(self.columns, np.int32).T
        return lax.dynamic_slice(jnp.asarray(table), (z * cols + me, 0), (1, table.shape[1]))[0]


def line_schedule(rows):
    if rows == 4:
        phases = [
            [(-1, [(0, 1), (1, 0), (2, 3), (3, 2)]), (-1, [(0, 2), (2, 0), (1, 3), (3, 1)])],
            [(-1, [(1, 2), (2, 1)]), (1, [(1, 0), (2, 3)])],
        ]
    else:
        partner = ({}, {})
        for i in range(rows):
            if i ^ 1 < rows:
                partner[0][i] = i ^ 1
            if 0 <= ((i + 1) ^ 1) - 1 < rows:
                partner[1][i] = ((i + 1) ^ 1) - 1
        phases, reached, last, count = [], (set(range(rows)), set(range(rows))), (-1, -1), 0
        while True:
            moves, now, fresh = [], [-1, -1], (set(), set())
            for side in (0, 1):
                pairs = [(p, i) for i, p in partner[side].items() if p in reached[1 - side]]
                fresh[side].update(i for _, i in pairs)
                if pairs:
                    moves.append((last[1 - side], pairs))
                    now[side] = count
                    count += 1
            if not moves:
                break
            phases.append(moves)
            reached, last = fresh, tuple(now)
    arrivals = [[] for _ in range(rows)]
    blocks = []
    for moves in phases:
        for source, pairs in moves:
            got = {b: a if source < 0 else blocks[source][a] for a, b in pairs}
            blocks.append(got)
            for i, block in got.items():
                arrivals[i].append((len(blocks) - 1, block))
    return phases, arrivals


def on_device(amplitudes, amp_mask, integrals, int_tiles, pair_dest):
    rows = lax.axis_size("row")
    cols = lax.axis_size("col")
    extra = cols // 8
    pair_rows, amp_cols = amplitudes.shape
    int_rows, int_cols = integrals.shape
    capacity = 2 * pair_rows // cols
    every = [(e, a, b, c) for e in range(extra) for a in range(2) for b in range(2) for c in range(2)]
    chips = [(e, a, b) for e in range(extra) for a in range(2) for b in range(2)]
    hops = [(de, turn) for de in range(extra) for turn in (0, 1)]
    turns = [(de, da, db) for de in range(extra) for da, db in ((0, 0), (1, 0), (0, 1))]
    phases, order = line_schedule(rows)

    def permute(value, moved_to):
        return lax.ppermute(value, "col", [(col_index(*at), col_index(*moved_to(*at))) for at in every])

    def along(e, a, b, c):
        return e, a ^ (c == 1), b ^ (c == 0), c

    def other(e, a, b, c):
        return e, a ^ (c == 0), b ^ (c == 1), c

    def across(e, a, b, c):
        return e, a, b, 1 - c

    consts = Scalars(rows, cols)
    core_at = consts.add(lambda z, e, a, b, c: c)
    wanted_at = len(consts.columns)
    for flip in (1, 0):
        for de, da, db in turns:
            consts.add(lambda z, e, a, b, c: col_index((e + de) % extra, a ^ da, b ^ db, c ^ flip))
    slot_rows = [lambda z: z] + [functools.partial(lambda j, z: order[z][j][1], j) for j in range(rows - 1)]
    rows_at = {
        q: [consts.add(lambda z, e, a, b, c: q * rows + row(z)) for row in slot_rows] for q in range(4)
    }
    gathered = [(de, p, q) for de in range(extra) for q in (0, 1) for p in (0, 1)]

    def arrival(chip, e, a, b, c):
        ce, ca, cb = chips[chip]
        p, q = (cb ^ b, ca ^ a) if c == 0 else (ca ^ a, cb ^ b)
        return gathered.index(((ce - e) % extra, p, q))

    mine_at = [consts.add(lambda z, e, a, b, c: arrival(row(z), e, a, b, c)) for row in slot_rows]
    theirs_at = [consts.add(lambda z, e, a, b, c: arrival(row(z), e, a, b, 1 - c)) for row in slot_rows]
    picks_at, place_at, arrive_at = {}, {}, {}
    for q in range(4):
        flip, second = int(q >= 2), q % 2
        picks_at[q] = [
            consts.add(lambda z, e, a, b, c: 3 * de + turn * (1 + (c ^ flip))) for de, turn in hops
        ]

        def block(e, a, b, kind, turn):
            return col_index(e, a ^ (second if kind else turn), b ^ (turn if kind else second), kind)

        place_at[q] = consts.add(lambda z, e, a, b, c: block(e, a, b, c ^ flip, 0))
        arrive_at[q] = [
            consts.add(lambda z, e, a, b, c: block((e - de) % extra, a, b, c ^ flip, turn)) for de, turn in hops[1:]
        ]
    flags_at = {}
    for j in range(rows - 1):
        kinds = sorted({order[i][j][0] for i in range(rows)})
        for kind in kinds[:-1]:
            flags_at[j, kind] = consts.add(lambda z, e, a, b, c: order[z][j][0] == kind)
    scalars = consts.of_device(lax.axis_index("row"), lax.axis_index("col"), cols)

    own_lists = int_tiles[:, 0, :]
    row = lax.axis_index("row").astype(jnp.int32).reshape(1)
    packed, packed_again, amp_used = pack(row, own_lists, amp_mask, integrals, amplitudes)

    moved = []

    def line_phase(moves, own):
        return [lax.ppermute(own if source < 0 else moved[source], "row", pairs) for source, pairs in moves]

    fresh = line_phase(phases[0], packed)
    amp_next = permute(amp_used, along)
    amp_other = permute(amp_used, other)
    amps = [amp_used, amp_next, amp_other, permute(amp_next, other)]
    for de in range(1, extra):
        amps += [permute(amp, lambda e, a, b, c: ((e - de) % extra, a, b, c)) for amp in amps[:4]]

    count = own_lists.shape[1]
    tiles = (int_rows // TILE) * (int_cols // TILE)
    found = own_lists[:, None, :] == jnp.arange(tiles, dtype=jnp.int32)[None, :, None]
    own_table = jnp.min(jnp.where(found, jnp.arange(count, dtype=jnp.int32), count), axis=2)

    col_ids = jnp.arange(cols, dtype=jnp.int32)
    onehot = (pair_dest[:, None] == col_ids[None, :]).astype(jnp.int32)
    before = jnp.cumsum(onehot, axis=0) - onehot
    target = pair_dest * capacity + jnp.sum(before * onehot, axis=1)

    table_next = permute(own_table, along)
    pair_tables = permute(jnp.concatenate([own_table, table_next], axis=0), across)
    sums = None
    slots, nexts, theirs_of, theirs_next = [packed], [permute(packed, along)], [permute(packed, across)], []
    target = tie(target, pair_tables)
    mine, for_them = pick_rows(scalars, wanted_at, len(turns), target, amps, capacity)
    for at, moves in enumerate(phases):
        if at > 0:
            fresh = line_phase(moves, packed_again)
        if at == 0:
            width = own_table.shape[1]
            tail = jnp.pad(scalars, (0, -scalars.shape[0] % width)).reshape(-1, width)
            numbers = jnp.concatenate([own_table, table_next, pair_tables, tail], axis=0)
            waited = (mine, nexts[0], theirs_of[0])
            fresh[0] = tie(fresh[0], mine, fresh[1])
        elif at == 1:
            theirs = permute(for_them, across)
            waited = (theirs, nexts[-1])
        else:
            waited = (*nexts[-1:], *theirs_of[-1:])
            while len(theirs_next) < len(nexts) - 1:
                theirs_next.append(permute(nexts[len(theirs_next)], across))
                waited = (*waited, theirs_next[-1])
        if at == len(phases) - 1:
            parts = (core_at, picks_at[0], *(places[: rows - 1] for places in (rows_at[0], mine_at, theirs_at)), tiles, 4 * rows)
            (sums,) = product(numbers, mine, theirs, slots, int_cols, parts)
            waited = (*waited, sums)
            for j in range(len(theirs_next), len(nexts) - 1):
                nexts[j] = tie(nexts[j], sums)
                theirs_next.append(permute(nexts[j], across))
                waited = (*waited, theirs_next[j])
        tied = []
        for i, value in enumerate(fresh):
            if at > 0 or i > 0:
                value = tie(value, *waited, *fresh[i + 1 :], *(tied[:1] if at > 0 else ()))
            tied.append(value)
        moved += tied
        if at == 0:
            packed_again = tie(packed_again, moved[-1])
        while len(slots) < rows and all(order[i][len(slots) - 1][0] < len(moved) for i in range(rows)):
            j = len(slots) - 1
            kinds = sorted({order[i][j][0] for i in range(rows)})
            slot = moved[kinds[-1]]
            for kind in kinds[:-1]:
                slot = choose(scalars, flags_at[j, kind], moved[kind], slot)
            slots.append(slot)
            nexts.append(permute(slot, along))
            theirs_of.append(permute(slot, across))

    out = None
    arrived = []
    for turn_at, q in enumerate((0, 2, 1, 3)):
        if turn_at == 3:
            out = tie(out, *arrived[0], *arrived[1])
        places = (rows_at[q], mine_at, theirs_at)
        blocks = (slots, nexts, theirs_of, theirs_next)[q]
        if q == 0 and rows > 1:
            blocks, places = blocks[-1:], [place[-1:] for place in places]
        out, *pieces = product(
            numbers,
            mine,
            theirs,
            blocks,
            int_cols,
            (core_at, picks_at[q], *places, tiles, 4 * rows),
            acc=sums if q == 0 else None,
            whole_cols=cols * int_cols,
            whole=out,
            place_at=place_at[q],
        )
        arrived.append([])
        for (de, turn), piece in zip(hops[1:], pieces):
            def sent_to(e, a, b, c):
                kind = c ^ int(q >= 2)
                return (e + de) % extra, a ^ (0 if kind else turn), b ^ (turn if kind else 0), c

            arrived[-1].append(permute(piece, sent_to))
        if q in (0, 2):
            while len(theirs_next) < rows - (q == 0):
                nexts[len(theirs_next)] = tie(nexts[len(theirs_next)], pieces[0])
                theirs_next.append(permute(nexts[len(theirs_next)], across))
    for got, q in zip(arrived, (0, 2, 1, 3)):
        for piece, place in zip(got, arrive_at[q]):
            out = put(piece, out, scalars, place)
    return out


def solution(mesh):
    in_specs = (P("row", "col"), P("row", "col"), P("row", "col"), P(None, "col", None), P("row"))
    out_specs = P(("row", "col"), None)
    return jax.shard_map(
        on_device, mesh=mesh, in_specs=in_specs, out_specs=out_specs, check_vma=False
    )
```

```python
import functools

import jax
import jax.numpy as jnp
import numpy as np
from jax import lax
from jax.experimental import pallas as pl
from jax.experimental.pallas import tpu as pltpu
from jax.sharding import PartitionSpec as P

TILE = 128
NOTHING = pl.CostEstimate(flops=0, bytes_accessed=0, transcendentals=0)
MM_COLS = 512
VMEM_LIMIT = (64 << 20) - (256 << 10)


def params():
    return pltpu.CompilerParams(vmem_limit_bytes=VMEM_LIMIT)


def pack_body(row, ids_ref, mask_ref, src_ref, amp_ref, out_ref, again_ref, used_ref):
    col_tiles = src_ref.shape[1] // TILE
    tiles = col_tiles * (src_ref.shape[0] // TILE)
    for e in range(out_ref.shape[0]):
        t = jnp.minimum(ids_ref[row[0], e], tiles - 1)
        k = pl.multiple_of(lax.div(t, col_tiles) * TILE, TILE)
        n = pl.multiple_of(lax.rem(t, col_tiles) * TILE, TILE)
        out_ref[e] = again_ref[e] = src_ref[pl.ds(k, TILE), pl.ds(n, TILE)]
    for k in range(mask_ref.shape[0]):
        for a in range(mask_ref.shape[1]):
            at = (slice(a * TILE, (a + 1) * TILE), slice(k * TILE, (k + 1) * TILE))
            scale = mask_ref[k, a].astype(jnp.float32)
            used_ref[at] = (amp_ref[at].astype(jnp.float32) * scale).astype(used_ref.dtype)


def pack(row, lists, mask, integrals, amplitudes):
    count = lists.shape[1]
    smem, vmem = pl.BlockSpec(memory_space=pltpu.SMEM), pl.BlockSpec(memory_space=pltpu.VMEM)
    return pl.pallas_call(
        pack_body,
        out_shape=[
            jax.ShapeDtypeStruct((count, TILE, TILE), integrals.dtype),
            jax.ShapeDtypeStruct((count, TILE, TILE), integrals.dtype),
            jax.ShapeDtypeStruct(amplitudes.shape, amplitudes.dtype),
        ],
        in_specs=[smem, smem, smem, vmem, vmem],
        out_specs=[vmem, vmem, vmem],
        compiler_params=params(),
        cost_estimate=NOTHING,
        name="pack_tiles",
    )(row, lists, mask.T, integrals, amplitudes)


def pick_body(first, count, capacity, scalars, target_ref, *refs):
    amps, (mine, theirs, chosen) = refs[:-3], refs[-3:]
    step = pl.program_id(0)
    slot = lax.broadcasted_iota(jnp.int32, (capacity, target_ref.shape[1]), 0)
    for d in range(count):
        wanted = scalars[first + step * count + d] * capacity + slot
        chosen[d * capacity : (d + 1) * capacity] = jnp.where(wanted == target_ref[...], 1.0, 0.0).astype(chosen.dtype)
    for at, amp in enumerate(amps):
        value = jnp.dot(chosen[...], amp[...], preferred_element_type=jnp.float32).astype(mine.dtype)
        value = value.reshape(count, capacity, amp.shape[1])

        @pl.when(step == 0)
        def _():
            theirs[at] = value

        @pl.when(step == 1)
        def _():
            mine[at] = value


def pick_rows(scalars, first, count, target, amps, capacity):
    n, k = amps[0].shape
    shape = jax.ShapeDtypeStruct((len(amps), count, capacity, k), amps[0].dtype)
    whole = pl.BlockSpec(shape.shape, lambda i, s: (0, 0, 0, 0))
    return pl.pallas_call(
        functools.partial(pick_body, first, count, capacity),
        out_shape=[shape, shape],
        grid_spec=pltpu.PrefetchScalarGridSpec(
            num_scalar_prefetch=1,
            grid=(2,),
            in_specs=[pl.BlockSpec((1, n), lambda i, s: (0, 0))]
            + [pl.BlockSpec((n, k), lambda i, s: (0, 0)) for _ in amps],
            out_specs=[whole, whole],
            scratch_shapes=[pltpu.VMEM((count * capacity, n), amps[0].dtype)],
        ),
        compiler_params=params(),
        cost_estimate=NOTHING,
        name="pick_rows",
    )(scalars, target.reshape(1, n), *amps)


class Numbers:
    def __init__(self, ref, base):
        self.ref, self.base = ref, base

    def __getitem__(self, at):
        width = self.ref.shape[1]
        return self.ref[self.base + at // width, at % width]


def product_body(at, has_acc, has_whole, final, numbers, mine, theirs, *refs):
    core_at, picks, rows_at, mine_at, theirs_at, tiles, base = at
    slot_count = len(rows_at)
    scalars = Numbers(numbers, base)
    packed_hbm = refs[:slot_count]
    acc = refs[slot_count] if has_acc else None
    refs = refs[slot_count + has_acc + has_whole :]
    outs, (lhs_all, rhs_all, packed, lhs_sem, sems) = refs[:-5], refs[-5:]
    step = pl.program_id(0)
    capacity, part = mine.shape[2:]
    depth = lhs_all.shape[1] // slot_count
    width = rhs_all.shape[1]
    count = packed.shape[1]
    col_tiles = tiles // (depth // TILE)

    @pl.when(step == 0)
    def _():
        for s in range(slot_count):
            pltpu.make_async_copy(packed_hbm[s], packed.at[s], sems.at[s]).start()
        for s in range(slot_count):
            for source, chip, side in (
                (mine, scalars[mine_at[s]], scalars[core_at]),
                (theirs, scalars[theirs_at[s]], 1 - scalars[core_at]),
            ):
                lanes = pl.ds(pl.multiple_of(s * depth + side * part, part), part)
                for t, pick in enumerate(picks):
                    pltpu.make_async_copy(
                        source.at[chip, scalars[pick]], lhs_all.at[pl.ds(t * capacity, capacity), lanes], lhs_sem
                    ).start()
        for s in range(slot_count):
            pltpu.make_async_copy(packed_hbm[s], packed.at[s], sems.at[s]).wait()
        pltpu.make_async_copy(lhs_all, lhs_all, lhs_sem).wait()

    for s in range(slot_count):
        row = scalars[rows_at[s]]
        for k in range(depth // TILE):
            for n in range(width // TILE):
                e = numbers[row, k * col_tiles + step * (width // TILE) + n]
                tile = packed[s, jnp.minimum(e, count - 1)]
                rhs_all[s * depth + k * TILE : s * depth + (k + 1) * TILE, n * TILE : (n + 1) * TILE] = jnp.where(
                    e < count, tile, jnp.zeros_like(tile)
                )
    total = jnp.dot(lhs_all[...], rhs_all[...], preferred_element_type=jnp.float32)
    if has_acc:
        total = acc[...] + total
    if not final:
        outs[0][...] = total
        return
    for t in range(len(picks)):
        outs[t][...] = total[t * capacity : (t + 1) * capacity].astype(outs[t].dtype)


def product(numbers, mine, theirs, slots, int_cols, at, acc=None, whole_cols=None, whole=None, place_at=None,
            pieces_only=False):
    picks, base = at[1], at[-1]
    capacity, part = mine.shape[2:]
    slot_count, m = len(slots), len(picks) * capacity
    depth = 2 * part
    width = min(MM_COLS, int_cols)
    steps = int_cols // width
    hbm = pl.BlockSpec(memory_space=pltpu.HBM)
    operands = [numbers, mine, theirs, *slots]
    in_specs = [hbm] * (len(operands) - 1)
    aliases = {}
    chunk = pl.BlockSpec((m, width), lambda i, numbers: (0, i))
    if acc is not None:
        in_specs.append(chunk)
        operands.append(acc)
    if whole is not None:
        aliases = {len(operands): 0}
        in_specs.append(hbm)
        operands.append(whole)
    final = pieces_only or whole_cols is not None
    out_specs = [chunk]
    out_shape = [jax.ShapeDtypeStruct((m, int_cols), jnp.float32)]
    if pieces_only:
        out_specs, out_shape = [], []
    elif final:
        out_specs = [pl.BlockSpec((capacity, width), lambda i, numbers: (0, Numbers(numbers, base)[place_at] * steps + i))]
        out_shape = [jax.ShapeDtypeStruct((capacity, whole_cols), mine.dtype)]
    for _ in picks if pieces_only else picks[1:] if final else ():
        out_specs.append(pl.BlockSpec((capacity, width), lambda i, numbers: (0, i)))
        out_shape.append(jax.ShapeDtypeStruct((capacity, int_cols), mine.dtype))
    k = slot_count * depth
    return pl.pallas_call(
        functools.partial(product_body, at, acc is not None, whole is not None, final),
        out_shape=out_shape,
        grid_spec=pltpu.PrefetchScalarGridSpec(
            num_scalar_prefetch=1,
            grid=(steps,),
            in_specs=in_specs,
            out_specs=out_specs,
            scratch_shapes=[
                pltpu.VMEM((m, k), mine.dtype),
                pltpu.VMEM((k, width), mine.dtype),
                pltpu.VMEM((slot_count, *slots[0].shape), mine.dtype),
                pltpu.SemaphoreType.DMA,
                pltpu.SemaphoreType.DMA((slot_count,)),
            ],
        ),
        input_output_aliases=aliases,
        compiler_params=params(),
        cost_estimate=NOTHING,
        name="product",
    )(*operands)


def tie_body(*refs):
    pass


def tie(value, *others):
    return pl.pallas_call(
        tie_body,
        out_shape=jax.ShapeDtypeStruct(value.shape, value.dtype),
        in_specs=[pl.BlockSpec(memory_space=pltpu.HBM)] * (1 + len(others)),
        out_specs=pl.BlockSpec(memory_space=pltpu.HBM),
        input_output_aliases={0: 0},
        compiler_params=params(),
        cost_estimate=NOTHING,
        name="tie",
    )(value, *others)


def choose_body(at, scalars, a_ref, b_ref, out_ref, sem):
    @pl.when(scalars[at] != 0)
    def _():
        pltpu.make_async_copy(a_ref, out_ref, sem).start()

    @pl.when(scalars[at] == 0)
    def _():
        pltpu.make_async_copy(b_ref, out_ref, sem).start()

    pltpu.make_async_copy(a_ref, out_ref, sem).wait()


def choose(scalars, at, a, b):
    hbm = pl.BlockSpec(memory_space=pltpu.HBM)
    return pl.pallas_call(
        functools.partial(choose_body, at),
        out_shape=jax.ShapeDtypeStruct(a.shape, a.dtype),
        in_specs=[pl.BlockSpec(memory_space=pltpu.SMEM), hbm, hbm],
        out_specs=pl.BlockSpec(memory_space=pltpu.VMEM),
        scratch_shapes=[pltpu.SemaphoreType.DMA],
        compiler_params=params(),
        cost_estimate=NOTHING,
        name="choose",
    )(scalars, a, b)


def put_body(scalars, piece_ref, whole_ref, out_ref):
    out_ref[...] = piece_ref[...]


def put(piece, whole, scalars, at):
    m, n = piece.shape
    width = min(2 * MM_COLS, n)
    steps = n // width
    return pl.pallas_call(
        put_body,
        out_shape=jax.ShapeDtypeStruct(whole.shape, whole.dtype),
        grid_spec=pltpu.PrefetchScalarGridSpec(
            num_scalar_prefetch=1,
            grid=(steps,),
            in_specs=[pl.BlockSpec((m, width), lambda i, s: (0, i)), pl.BlockSpec(memory_space=pltpu.HBM)],
            out_specs=pl.BlockSpec((m, width), lambda i, s: (0, s[at] * steps + i)),
        ),
        input_output_aliases={2: 0},
        compiler_params=params(),
        cost_estimate=NOTHING,
        name="put",
    )(scalars, piece, whole)


def col_index(ie, ia, ib, core):
    return ((ie * 2 + ia) * 2 + ib) * 2 + core


class Scalars:
    def __init__(self, rows, cols):
        self.places = [(z, me // 8, me // 4 % 2, me // 2 % 2, me % 2) for z in range(rows) for me in range(cols)]
        self.columns = []

    def add(self, value_of):
        self.columns.append([int(value_of(*place)) for place in self.places])
        return len(self.columns) - 1

    def of_device(self, z, me, cols):
        table = np.array(self.columns, np.int32).T
        return lax.dynamic_slice(jnp.asarray(table), (z * cols + me, 0), (1, table.shape[1]))[0]


def line_schedule(rows):
    if rows == 4:
        phases = [
            [(-1, [(0, 1), (1, 0), (2, 3), (3, 2)]), (-1, [(0, 2), (2, 0), (1, 3), (3, 1)])],
            [(-1, [(1, 2), (2, 1)]), (1, [(1, 0), (2, 3)])],
        ]
    else:
        partner = ({}, {})
        for i in range(rows):
            if i ^ 1 < rows:
                partner[0][i] = i ^ 1
            if 0 <= ((i + 1) ^ 1) - 1 < rows:
                partner[1][i] = ((i + 1) ^ 1) - 1
        phases, reached, last, count = [], (set(range(rows)), set(range(rows))), (-1, -1), 0
        while True:
            moves, now, fresh = [], [-1, -1], (set(), set())
            for side in (0, 1):
                pairs = [(p, i) for i, p in partner[side].items() if p in reached[1 - side]]
                fresh[side].update(i for _, i in pairs)
                if pairs:
                    moves.append((last[1 - side], pairs))
                    now[side] = count
                    count += 1
            if not moves:
                break
            phases.append(moves)
            reached, last = fresh, tuple(now)
    arrivals = [[] for _ in range(rows)]
    blocks = []
    for moves in phases:
        for source, pairs in moves:
            got = {b: a if source < 0 else blocks[source][a] for a, b in pairs}
            blocks.append(got)
            for i, block in got.items():
                arrivals[i].append((len(blocks) - 1, block))
    return phases, arrivals


def on_device(amplitudes, amp_mask, integrals, int_tiles, pair_dest):
    rows = lax.axis_size("row")
    cols = lax.axis_size("col")
    extra = cols // 8
    pair_rows, amp_cols = amplitudes.shape
    int_rows, int_cols = integrals.shape
    capacity = 2 * pair_rows // cols
    every = [(e, a, b, c) for e in range(extra) for a in range(2) for b in range(2) for c in range(2)]
    chips = [(e, a, b) for e in range(extra) for a in range(2) for b in range(2)]
    hops = [(de, turn) for de in range(extra) for turn in (0, 1)]
    turns = [(de, da, db) for de in range(extra) for da, db in ((0, 0), (1, 0), (0, 1))]
    phases, order = line_schedule(rows)

    def permute(value, moved_to):
        return lax.ppermute(value, "col", [(col_index(*at), col_index(*moved_to(*at))) for at in every])

    def along(e, a, b, c):
        return e, a ^ (c == 1), b ^ (c == 0), c

    def other(e, a, b, c):
        return e, a ^ (c == 0), b ^ (c == 1), c

    def across(e, a, b, c):
        return e, a, b, 1 - c

    consts = Scalars(rows, cols)
    core_at = consts.add(lambda z, e, a, b, c: c)
    wanted_at = len(consts.columns)
    for flip in (1, 0):
        for de, da, db in turns:
            consts.add(lambda z, e, a, b, c: col_index((e + de) % extra, a ^ da, b ^ db, c ^ flip))
    slot_rows = [lambda z: z] + [functools.partial(lambda j, z: order[z][j][1], j) for j in range(rows - 1)]
    rows_at = {
        q: [consts.add(lambda z, e, a, b, c: q * rows + row(z)) for row in slot_rows] for q in range(4)
    }
    gathered = [(de, p, q) for de in range(extra) for q in (0, 1) for p in (0, 1)]

    def arrival(chip, e, a, b, c):
        ce, ca, cb = chips[chip]
        p, q = (cb ^ b, ca ^ a) if c == 0 else (ca ^ a, cb ^ b)
        return gathered.index(((ce - e) % extra, p, q))

    mine_at = [consts.add(lambda z, e, a, b, c: arrival(row(z), e, a, b, c)) for row in slot_rows]
    theirs_at = [consts.add(lambda z, e, a, b, c: arrival(row(z), e, a, b, 1 - c)) for row in slot_rows]
    picks_at, place_at, arrive_at = {}, {}, {}
    for q in range(4):
        flip, second = int(q >= 2), q % 2
        picks_at[q] = [
            consts.add(lambda z, e, a, b, c: 3 * de + turn * (1 + (c ^ flip))) for de, turn in hops
        ]

        def block(e, a, b, kind, turn):
            return col_index(e, a ^ (second if kind else turn), b ^ (turn if kind else second), kind)

        place_at[q] = consts.add(lambda z, e, a, b, c: block(e, a, b, c ^ flip, 0))
        arrive_at[q] = [
            consts.add(lambda z, e, a, b, c: block((e - de) % extra, a, b, c ^ flip, turn)) for de, turn in hops[1:]
        ]
    flags_at = {}
    for j in range(rows - 1):
        kinds = sorted({order[i][j][0] for i in range(rows)})
        for kind in kinds[:-1]:
            flags_at[j, kind] = consts.add(lambda z, e, a, b, c: order[z][j][0] == kind)
    scalars = consts.of_device(lax.axis_index("row"), lax.axis_index("col"), cols)

    own_lists = int_tiles[:, 0, :]
    row = lax.axis_index("row").astype(jnp.int32).reshape(1)
    packed, packed_again, amp_used = pack(row, own_lists, amp_mask, integrals, amplitudes)

    moved = []

    def line_phase(moves, own):
        return [lax.ppermute(own if source < 0 else moved[source], "row", pairs) for source, pairs in moves]

    fresh = line_phase(phases[0], packed)
    amp_next = permute(amp_used, along)
    amp_other = permute(amp_used, other)
    amps = [amp_used, amp_next, amp_other, permute(amp_next, other)]
    for de in range(1, extra):
        amps += [permute(amp, lambda e, a, b, c: ((e - de) % extra, a, b, c)) for amp in amps[:4]]

    count = own_lists.shape[1]
    tiles = (int_rows // TILE) * (int_cols // TILE)
    found = own_lists[:, None, :] == jnp.arange(tiles, dtype=jnp.int32)[None, :, None]
    own_table = jnp.min(jnp.where(found, jnp.arange(count, dtype=jnp.int32), count), axis=2)

    col_ids = jnp.arange(cols, dtype=jnp.int32)
    onehot = (pair_dest[:, None] == col_ids[None, :]).astype(jnp.int32)
    before = jnp.cumsum(onehot, axis=0) - onehot
    target = pair_dest * capacity + jnp.sum(before * onehot, axis=1)

    table_next = permute(own_table, along)
    pair_tables = permute(jnp.concatenate([own_table, table_next], axis=0), across)
    sums = None
    slots, nexts, theirs_of, theirs_next = [packed], [permute(packed, along)], [permute(packed, across)], []
    width = own_table.shape[1]
    tail = jnp.pad(scalars, (0, -scalars.shape[0] % width)).reshape(-1, width)
    numbers = jnp.concatenate([own_table, table_next, pair_tables, tail], axis=0)
    target = tie(target, numbers)
    mine, for_them = pick_rows(scalars, wanted_at, len(turns), target, amps, capacity)
    for at, moves in enumerate(phases):
        if at > 0:
            fresh = line_phase(moves, packed_again)
        if at == 0:
            waited = (mine, nexts[0], theirs_of[0])
            fresh[0] = tie(fresh[0], mine, fresh[1])
        elif at == 1:
            theirs = permute(for_them, across)
            waited = (theirs, nexts[-1])
        else:
            waited = (*nexts[-1:], *theirs_of[-1:])
            while len(theirs_next) < len(nexts) - 1:
                theirs_next.append(permute(nexts[len(theirs_next)], across))
                waited = (*waited, theirs_next[-1])
        if at == len(phases) - 1:
            parts = (core_at, picks_at[0], *(places[: rows - 1] for places in (rows_at[0], mine_at, theirs_at)), tiles, 4 * rows)
            (sums,) = product(numbers, mine, theirs, slots, int_cols, parts)
            waited = (*waited, sums)
            for j in range(len(theirs_next), len(nexts) - 1):
                nexts[j] = tie(nexts[j], sums)
                theirs_next.append(permute(nexts[j], across))
                waited = (*waited, theirs_next[j])
        tied = []
        for i, value in enumerate(fresh):
            if at > 0 or i > 0:
                value = tie(value, *waited, *fresh[i + 1 :], *(tied[:1] if at > 0 else ()))
            tied.append(value)
        moved += tied
        if at == 0:
            packed_again = tie(packed_again, fresh[1])
        while len(slots) < rows and all(order[i][len(slots) - 1][0] < len(moved) for i in range(rows)):
            j = len(slots) - 1
            kinds = sorted({order[i][j][0] for i in range(rows)})
            slot = moved[kinds[-1]]
            for kind in kinds[:-1]:
                slot = choose(scalars, flags_at[j, kind], moved[kind], slot)
            slots.append(slot)
            nexts.append(permute(slot, along))
            theirs_of.append(permute(slot, across))

    out = None
    arrived = []
    for turn_at, q in enumerate((0, 2, 1, 3)):
        if turn_at == 3:
            theirs_next[-1] = tie(theirs_next[-1], *arrived[0], *arrived[1])
        places = (rows_at[q], mine_at, theirs_at)
        blocks = (slots, nexts, theirs_of, theirs_next)[q]
        if q == 0 and rows > 1:
            blocks, places = blocks[-1:], [place[-1:] for place in places]
        call = functools.partial(product, numbers, mine, theirs, blocks, int_cols)
        own = dict(whole_cols=cols * int_cols, whole=out, place_at=place_at[q])
        if turn_at < 3:
            out, *pieces = call(
                (core_at, picks_at[q], *places, tiles, 4 * rows), acc=sums if q == 0 else None, **own
            )
        else:
            pieces = call((core_at, picks_at[q][1:], *places, tiles, 4 * rows), pieces_only=True)
        arrived.append([])
        for (de, turn), piece in zip(hops[1:], pieces):
            def sent_to(e, a, b, c):
                kind = c ^ int(q >= 2)
                return (e + de) % extra, a ^ (0 if kind else turn), b ^ (turn if kind else 0), c

            arrived[-1].append(permute(piece, sent_to))
        if q in (0, 2):
            while len(theirs_next) < rows - (q == 0):
                nexts[len(theirs_next)] = tie(nexts[len(theirs_next)], pieces[0])
                theirs_next.append(permute(nexts[len(theirs_next)], across))
    own["whole"] = tie(out, pieces[0])
    (out,) = call((core_at, picks_at[q][:1], *places, tiles, 4 * rows), **own)
    for got, q in zip(arrived, (0, 2, 1, 3)):
        for piece, place in zip(got, arrive_at[q]):
            out = put(piece, out, scalars, place)
    return out


def solution(mesh):
    in_specs = (P("row", "col"), P("row", "col"), P("row", "col"), P(None, "col", None), P("row"))
    out_specs = P(("row", "col"), None)
    return jax.shard_map(
        on_device, mesh=mesh, in_specs=in_specs, out_specs=out_specs, check_vma=False
    )
```

```python
import functools

import jax
import jax.numpy as jnp
import numpy as np
from jax import lax
from jax.experimental import pallas as pl
from jax.experimental.pallas import tpu as pltpu
from jax.sharding import PartitionSpec as P

TILE = 128
NOTHING = pl.CostEstimate(flops=0, bytes_accessed=0, transcendentals=0)
MM_COLS = 512
VMEM_LIMIT = (64 << 20) - (256 << 10)


def params():
    return pltpu.CompilerParams(vmem_limit_bytes=VMEM_LIMIT)


def pack_body(row, ids_ref, mask_ref, src_ref, amp_ref, out_ref, again_ref, used_ref):
    col_tiles = src_ref.shape[1] // TILE
    tiles = col_tiles * (src_ref.shape[0] // TILE)
    for e in range(out_ref.shape[0]):
        t = jnp.minimum(ids_ref[row[0], e], tiles - 1)
        k = pl.multiple_of(lax.div(t, col_tiles) * TILE, TILE)
        n = pl.multiple_of(lax.rem(t, col_tiles) * TILE, TILE)
        out_ref[e] = again_ref[e] = src_ref[pl.ds(k, TILE), pl.ds(n, TILE)]
    for k in range(mask_ref.shape[0]):
        for a in range(mask_ref.shape[1]):
            at = (slice(a * TILE, (a + 1) * TILE), slice(k * TILE, (k + 1) * TILE))
            scale = mask_ref[k, a].astype(jnp.float32)
            used_ref[at] = (amp_ref[at].astype(jnp.float32) * scale).astype(used_ref.dtype)


def pack(row, lists, mask, integrals, amplitudes):
    count = lists.shape[1]
    smem, vmem = pl.BlockSpec(memory_space=pltpu.SMEM), pl.BlockSpec(memory_space=pltpu.VMEM)
    return pl.pallas_call(
        pack_body,
        out_shape=[
            jax.ShapeDtypeStruct((count, TILE, TILE), integrals.dtype),
            jax.ShapeDtypeStruct((count, TILE, TILE), integrals.dtype),
            jax.ShapeDtypeStruct(amplitudes.shape, amplitudes.dtype),
        ],
        in_specs=[smem, smem, smem, vmem, vmem],
        out_specs=[vmem, vmem, vmem],
        compiler_params=params(),
        cost_estimate=NOTHING,
        name="pack_tiles",
    )(row, lists, mask.T, integrals, amplitudes)


def pick_body(first, count, capacity, scalars, target_ref, *refs):
    amps, (mine, theirs, chosen) = refs[:-3], refs[-3:]
    step = pl.program_id(0)
    slot = lax.broadcasted_iota(jnp.int32, (capacity, target_ref.shape[1]), 0)
    for d in range(count):
        wanted = scalars[first + step * count + d] * capacity + slot
        chosen[d * capacity : (d + 1) * capacity] = jnp.where(wanted == target_ref[...], 1.0, 0.0).astype(chosen.dtype)
    for at, amp in enumerate(amps):
        value = jnp.dot(chosen[...], amp[...], preferred_element_type=jnp.float32).astype(mine.dtype)
        value = value.reshape(count, capacity, amp.shape[1])

        @pl.when(step == 0)
        def _():
            theirs[at] = value

        @pl.when(step == 1)
        def _():
            mine[at] = value


def pick_rows(scalars, first, count, target, amps, capacity):
    n, k = amps[0].shape
    shape = jax.ShapeDtypeStruct((len(amps), count, capacity, k), amps[0].dtype)
    whole = pl.BlockSpec(shape.shape, lambda i, s: (0, 0, 0, 0))
    return pl.pallas_call(
        functools.partial(pick_body, first, count, capacity),
        out_shape=[shape, shape],
        grid_spec=pltpu.PrefetchScalarGridSpec(
            num_scalar_prefetch=1,
            grid=(2,),
            in_specs=[pl.BlockSpec((1, n), lambda i, s: (0, 0))]
            + [pl.BlockSpec((n, k), lambda i, s: (0, 0)) for _ in amps],
            out_specs=[whole, whole],
            scratch_shapes=[pltpu.VMEM((count * capacity, n), amps[0].dtype)],
        ),
        compiler_params=params(),
        cost_estimate=NOTHING,
        name="pick_rows",
    )(scalars, target.reshape(1, n), *amps)


class Numbers:
    def __init__(self, ref, base):
        self.ref, self.base = ref, base

    def __getitem__(self, at):
        width = self.ref.shape[1]
        return self.ref[self.base + at // width, at % width]


def product_body(at, has_acc, has_whole, final, numbers, mine, theirs, *refs):
    core_at, picks, rows_at, mine_at, theirs_at, tiles, base = at
    slot_count = len(rows_at)
    scalars = Numbers(numbers, base)
    packed_hbm = refs[:slot_count]
    acc = refs[slot_count] if has_acc else None
    refs = refs[slot_count + has_acc + has_whole :]
    outs, (lhs_all, rhs_all, packed, lhs_sem, sems) = refs[:-5], refs[-5:]
    step = pl.program_id(0)
    capacity, part = mine.shape[2:]
    depth = lhs_all.shape[1] // slot_count
    width = rhs_all.shape[1]
    count = packed.shape[1]
    col_tiles = tiles // (depth // TILE)

    @pl.when(step == 0)
    def _():
        for s in range(slot_count):
            pltpu.make_async_copy(packed_hbm[s], packed.at[s], sems.at[s]).start()
        for s in range(slot_count):
            for source, chip, side in (
                (mine, scalars[mine_at[s]], scalars[core_at]),
                (theirs, scalars[theirs_at[s]], 1 - scalars[core_at]),
            ):
                lanes = pl.ds(pl.multiple_of(s * depth + side * part, part), part)
                for t, pick in enumerate(picks):
                    pltpu.make_async_copy(
                        source.at[chip, scalars[pick]], lhs_all.at[pl.ds(t * capacity, capacity), lanes], lhs_sem
                    ).start()
        for s in range(slot_count):
            pltpu.make_async_copy(packed_hbm[s], packed.at[s], sems.at[s]).wait()
        pltpu.make_async_copy(lhs_all, lhs_all, lhs_sem).wait()

    for s in range(slot_count):
        row = scalars[rows_at[s]]
        for k in range(depth // TILE):
            for n in range(width // TILE):
                e = numbers[row, k * col_tiles + step * (width // TILE) + n]
                tile = packed[s, jnp.minimum(e, count - 1)]
                rhs_all[s * depth + k * TILE : s * depth + (k + 1) * TILE, n * TILE : (n + 1) * TILE] = jnp.where(
                    e < count, tile, jnp.zeros_like(tile)
                )
    total = jnp.dot(lhs_all[...], rhs_all[...], preferred_element_type=jnp.float32)
    if has_acc:
        total = acc[...] + total
    if not final:
        outs[0][...] = total
        return
    for t in range(len(picks)):
        outs[t][...] = total[t * capacity : (t + 1) * capacity].astype(outs[t].dtype)


def product(numbers, mine, theirs, slots, int_cols, at, acc=None, whole_cols=None, whole=None, place_at=None):
    picks, base = at[1], at[-1]
    capacity, part = mine.shape[2:]
    slot_count, m = len(slots), len(picks) * capacity
    depth = 2 * part
    width = min(MM_COLS, int_cols)
    steps = int_cols // width
    hbm = pl.BlockSpec(memory_space=pltpu.HBM)
    operands = [numbers, mine, theirs, *slots]
    in_specs = [hbm] * (len(operands) - 1)
    aliases = {}
    chunk = pl.BlockSpec((m, width), lambda i, numbers: (0, i))
    if acc is not None:
        in_specs.append(chunk)
        operands.append(acc)
    if whole is not None:
        aliases = {len(operands): 0}
        in_specs.append(hbm)
        operands.append(whole)
    final = whole_cols is not None
    out_specs = [chunk]
    out_shape = [jax.ShapeDtypeStruct((m, int_cols), jnp.float32)]
    if final:
        out_specs = [pl.BlockSpec((capacity, width), lambda i, numbers: (0, Numbers(numbers, base)[place_at] * steps + i))]
        out_shape = [jax.ShapeDtypeStruct((capacity, whole_cols), mine.dtype)]
    for _ in picks[1:] if final else ():
        out_specs.append(pl.BlockSpec((capacity, width), lambda i, numbers: (0, i)))
        out_shape.append(jax.ShapeDtypeStruct((capacity, int_cols), mine.dtype))
    k = slot_count * depth
    return pl.pallas_call(
        functools.partial(product_body, at, acc is not None, whole is not None, final),
        out_shape=out_shape,
        grid_spec=pltpu.PrefetchScalarGridSpec(
            num_scalar_prefetch=1,
            grid=(steps,),
            in_specs=in_specs,
            out_specs=out_specs,
            scratch_shapes=[
                pltpu.VMEM((m, k), mine.dtype),
                pltpu.VMEM((k, width), mine.dtype),
                pltpu.VMEM((slot_count, *slots[0].shape), mine.dtype),
                pltpu.SemaphoreType.DMA,
                pltpu.SemaphoreType.DMA((slot_count,)),
            ],
        ),
        input_output_aliases=aliases,
        compiler_params=params(),
        cost_estimate=NOTHING,
        name="product",
    )(*operands)


def tie_body(*refs):
    pass


def tie(value, *others):
    return pl.pallas_call(
        tie_body,
        out_shape=jax.ShapeDtypeStruct(value.shape, value.dtype),
        in_specs=[pl.BlockSpec(memory_space=pltpu.HBM)] * (1 + len(others)),
        out_specs=pl.BlockSpec(memory_space=pltpu.HBM),
        input_output_aliases={0: 0},
        compiler_params=params(),
        cost_estimate=NOTHING,
        name="tie",
    )(value, *others)


def choose_body(at, scalars, a_ref, b_ref, out_ref, sem):
    @pl.when(scalars[at] != 0)
    def _():
        pltpu.make_async_copy(a_ref, out_ref, sem).start()

    @pl.when(scalars[at] == 0)
    def _():
        pltpu.make_async_copy(b_ref, out_ref, sem).start()

    pltpu.make_async_copy(a_ref, out_ref, sem).wait()


def choose(scalars, at, a, b):
    hbm = pl.BlockSpec(memory_space=pltpu.HBM)
    return pl.pallas_call(
        functools.partial(choose_body, at),
        out_shape=jax.ShapeDtypeStruct(a.shape, a.dtype),
        in_specs=[pl.BlockSpec(memory_space=pltpu.SMEM), hbm, hbm],
        out_specs=pl.BlockSpec(memory_space=pltpu.VMEM),
        scratch_shapes=[pltpu.SemaphoreType.DMA],
        compiler_params=params(),
        cost_estimate=NOTHING,
        name="choose",
    )(scalars, a, b)


def put_body(scalars, piece_ref, whole_ref, out_ref):
    out_ref[...] = piece_ref[...]


def put(piece, whole, scalars, at):
    m, n = piece.shape
    width = min(2 * MM_COLS, n)
    steps = n // width
    return pl.pallas_call(
        put_body,
        out_shape=jax.ShapeDtypeStruct(whole.shape, whole.dtype),
        grid_spec=pltpu.PrefetchScalarGridSpec(
            num_scalar_prefetch=1,
            grid=(steps,),
            in_specs=[pl.BlockSpec((m, width), lambda i, s: (0, i)), pl.BlockSpec(memory_space=pltpu.HBM)],
            out_specs=pl.BlockSpec((m, width), lambda i, s: (0, s[at] * steps + i)),
        ),
        input_output_aliases={2: 0},
        compiler_params=params(),
        cost_estimate=NOTHING,
        name="put",
    )(scalars, piece, whole)


def col_index(ie, ia, ib, core):
    return ((ie * 2 + ia) * 2 + ib) * 2 + core


class Scalars:
    def __init__(self, rows, cols):
        self.places = [(z, me // 8, me // 4 % 2, me // 2 % 2, me % 2) for z in range(rows) for me in range(cols)]
        self.columns = []

    def add(self, value_of):
        self.columns.append([int(value_of(*place)) for place in self.places])
        return len(self.columns) - 1

    def of_device(self, z, me, cols):
        table = np.array(self.columns, np.int32).T
        return lax.dynamic_slice(jnp.asarray(table), (z * cols + me, 0), (1, table.shape[1]))[0]


def line_schedule(rows):
    if rows == 4:
        phases = [
            [(-1, [(0, 1), (1, 0), (2, 3), (3, 2)]), (-1, [(0, 2), (2, 0), (1, 3), (3, 1)])],
            [(-1, [(1, 2), (2, 1)]), (1, [(1, 0), (2, 3)])],
        ]
    else:
        partner = ({}, {})
        for i in range(rows):
            if i ^ 1 < rows:
                partner[0][i] = i ^ 1
            if 0 <= ((i + 1) ^ 1) - 1 < rows:
                partner[1][i] = ((i + 1) ^ 1) - 1
        phases, reached, last, count = [], (set(range(rows)), set(range(rows))), (-1, -1), 0
        while True:
            moves, now, fresh = [], [-1, -1], (set(), set())
            for side in (0, 1):
                pairs = [(p, i) for i, p in partner[side].items() if p in reached[1 - side]]
                fresh[side].update(i for _, i in pairs)
                if pairs:
                    moves.append((last[1 - side], pairs))
                    now[side] = count
                    count += 1
            if not moves:
                break
            phases.append(moves)
            reached, last = fresh, tuple(now)
    arrivals = [[] for _ in range(rows)]
    blocks = []
    for moves in phases:
        for source, pairs in moves:
            got = {b: a if source < 0 else blocks[source][a] for a, b in pairs}
            blocks.append(got)
            for i, block in got.items():
                arrivals[i].append((len(blocks) - 1, block))
    return phases, arrivals


def on_device(amplitudes, amp_mask, integrals, int_tiles, pair_dest):
    rows = lax.axis_size("row")
    cols = lax.axis_size("col")
    extra = cols // 8
    pair_rows, amp_cols = amplitudes.shape
    int_rows, int_cols = integrals.shape
    capacity = 2 * pair_rows // cols
    every = [(e, a, b, c) for e in range(extra) for a in range(2) for b in range(2) for c in range(2)]
    chips = [(e, a, b) for e in range(extra) for a in range(2) for b in range(2)]
    hops = [(de, turn) for de in range(extra) for turn in (0, 1)]
    turns = [(de, da, db) for de in range(extra) for da, db in ((0, 0), (1, 0), (0, 1))]
    phases, order = line_schedule(rows)

    def permute(value, moved_to):
        return lax.ppermute(value, "col", [(col_index(*at), col_index(*moved_to(*at))) for at in every])

    def along(e, a, b, c):
        return e, a ^ (c == 1), b ^ (c == 0), c

    def other(e, a, b, c):
        return e, a ^ (c == 0), b ^ (c == 1), c

    def across(e, a, b, c):
        return e, a, b, 1 - c

    consts = Scalars(rows, cols)
    core_at = consts.add(lambda z, e, a, b, c: c)
    wanted_at = len(consts.columns)
    for flip in (1, 0):
        for de, da, db in turns:
            consts.add(lambda z, e, a, b, c: col_index((e + de) % extra, a ^ da, b ^ db, c ^ flip))
    slot_rows = [lambda z: z] + [functools.partial(lambda j, z: order[z][j][1], j) for j in range(rows - 1)]
    rows_at = {
        q: [consts.add(lambda z, e, a, b, c: q * rows + row(z)) for row in slot_rows] for q in range(4)
    }
    gathered = [(de, p, q) for de in range(extra) for q in (0, 1) for p in (0, 1)]

    def arrival(chip, e, a, b, c):
        ce, ca, cb = chips[chip]
        p, q = (cb ^ b, ca ^ a) if c == 0 else (ca ^ a, cb ^ b)
        return gathered.index(((ce - e) % extra, p, q))

    mine_at = [consts.add(lambda z, e, a, b, c: arrival(row(z), e, a, b, c)) for row in slot_rows]
    theirs_at = [consts.add(lambda z, e, a, b, c: arrival(row(z), e, a, b, 1 - c)) for row in slot_rows]
    picks_at, place_at, arrive_at = {}, {}, {}
    for q in range(4):
        flip, second = int(q >= 2), q % 2
        picks_at[q] = [
            consts.add(lambda z, e, a, b, c: 3 * de + turn * (1 + (c ^ flip))) for de, turn in hops
        ]

        def block(e, a, b, kind, turn):
            return col_index(e, a ^ (second if kind else turn), b ^ (turn if kind else second), kind)

        place_at[q] = consts.add(lambda z, e, a, b, c: block(e, a, b, c ^ flip, 0))
        arrive_at[q] = [
            consts.add(lambda z, e, a, b, c: block((e - de) % extra, a, b, c ^ flip, turn)) for de, turn in hops[1:]
        ]
    flags_at = {}
    for j in range(rows - 1):
        kinds = sorted({order[i][j][0] for i in range(rows)})
        for kind in kinds[:-1]:
            flags_at[j, kind] = consts.add(lambda z, e, a, b, c: order[z][j][0] == kind)
    scalars = consts.of_device(lax.axis_index("row"), lax.axis_index("col"), cols)

    own_lists = int_tiles[:, 0, :]
    row = lax.axis_index("row").astype(jnp.int32).reshape(1)
    packed, packed_again, amp_used = pack(row, own_lists, amp_mask, integrals, amplitudes)

    moved = []

    def line_phase(moves, own):
        return [lax.ppermute(own if source < 0 else moved[source], "row", pairs) for source, pairs in moves]

    fresh = line_phase(phases[0], packed)
    count = own_lists.shape[1]
    tiles = (int_rows // TILE) * (int_cols // TILE)
    found = own_lists[:, None, :] == jnp.arange(tiles, dtype=jnp.int32)[None, :, None]
    own_table = jnp.min(jnp.where(found, jnp.arange(count, dtype=jnp.int32), count), axis=2)

    col_ids = jnp.arange(cols, dtype=jnp.int32)
    onehot = (pair_dest[:, None] == col_ids[None, :]).astype(jnp.int32)
    before = jnp.cumsum(onehot, axis=0) - onehot
    target = pair_dest * capacity + jnp.sum(before * onehot, axis=1)

    table_next = permute(own_table, along)
    amp_used = tie(amp_used, table_next)
    amp_next = permute(amp_used, along)
    amp_other = permute(amp_used, other)
    amps = [amp_used, amp_next, amp_other, permute(amp_next, other)]
    for de in range(1, extra):
        amps += [permute(amp, lambda e, a, b, c: ((e - de) % extra, a, b, c)) for amp in amps[:4]]
    pair_tables = permute(jnp.concatenate([own_table, table_next], axis=0), across)
    sums = None
    slots, nexts, theirs_of, theirs_next = [packed], [permute(packed, along)], [permute(packed, across)], []
    width = own_table.shape[1]
    tail = jnp.pad(scalars, (0, -scalars.shape[0] % width)).reshape(-1, width)
    numbers = jnp.concatenate([own_table, table_next, pair_tables, tail], axis=0)
    target = tie(target, numbers)
    mine, for_them = pick_rows(scalars, wanted_at, len(turns), target, amps, capacity)
    for at, moves in enumerate(phases):
        if at > 0:
            fresh = line_phase(moves, packed_again)
        if at == 0:
            waited = (mine, theirs_of[0])
            fresh[0] = tie(fresh[0], mine, fresh[1])
        elif at == 1:
            theirs = permute(for_them, across)
            waited = (theirs, nexts[-1])
        else:
            waited = (*nexts[-1:], *theirs_of[-1:])
            while len(theirs_next) < len(nexts) - 1:
                theirs_next.append(permute(nexts[len(theirs_next)], across))
                waited = (*waited, theirs_next[-1])
        if at == len(phases) - 1:
            parts = (core_at, picks_at[0], *(places[: rows - 1] for places in (rows_at[0], mine_at, theirs_at)), tiles, 4 * rows)
            (sums,) = product(numbers, mine, theirs, slots, int_cols, parts)
            waited = (*waited, sums)
            for j in range(len(theirs_next), len(nexts) - 1):
                nexts[j] = tie(nexts[j], sums)
                theirs_next.append(permute(nexts[j], across))
                waited = (*waited, theirs_next[j])
        tied = []
        for i, value in enumerate(fresh):
            if at > 0 or i > 0:
                value = tie(value, *waited, *fresh[i + 1 :], *(tied[:1] if at > 0 else ()))
            tied.append(value)
        moved += tied
        if at == 0:
            packed_again = tie(packed_again, fresh[1])
        while len(slots) < rows and all(order[i][len(slots) - 1][0] < len(moved) for i in range(rows)):
            j = len(slots) - 1
            kinds = sorted({order[i][j][0] for i in range(rows)})
            slot = moved[kinds[-1]]
            for kind in kinds[:-1]:
                slot = choose(scalars, flags_at[j, kind], moved[kind], slot)
            slots.append(slot)
            nexts.append(permute(slot, along))
            theirs_of.append(permute(slot, across))

    out = None
    arrived = []
    for turn_at, q in enumerate((0, 2, 1, 3)):
        if turn_at == 3:
            for piece, place in zip(arrived[0], arrive_at[0]):
                out = put(piece, out, scalars, place)
            out = tie(out, *arrived[1])
        places = (rows_at[q], mine_at, theirs_at)
        blocks = (slots, nexts, theirs_of, theirs_next)[q]
        if q == 0 and rows > 1:
            blocks, places = blocks[-1:], [place[-1:] for place in places]
        out, *pieces = product(
            numbers,
            mine,
            theirs,
            blocks,
            int_cols,
            (core_at, picks_at[q], *places, tiles, 4 * rows),
            acc=sums if q == 0 else None,
            whole_cols=cols * int_cols,
            whole=out,
            place_at=place_at[q],
        )
        arrived.append([])
        for (de, turn), piece in zip(hops[1:], pieces):
            def sent_to(e, a, b, c):
                kind = c ^ int(q >= 2)
                return (e + de) % extra, a ^ (0 if kind else turn), b ^ (turn if kind else 0), c

            arrived[-1].append(permute(piece, sent_to))
        if q in (0, 2):
            while len(theirs_next) < rows - (q == 0):
                nexts[len(theirs_next)] = tie(nexts[len(theirs_next)], pieces[0])
                theirs_next.append(permute(nexts[len(theirs_next)], across))
    for got, q in zip(arrived[1:], (2, 1, 3)):
        for piece, place in zip(got, arrive_at[q]):
            out = put(piece, out, scalars, place)
    return out


def solution(mesh):
    in_specs = (P("row", "col"), P("row", "col"), P("row", "col"), P(None, "col", None), P("row"))
    out_specs = P(("row", "col"), None)
    return jax.shard_map(
        on_device, mesh=mesh, in_specs=in_specs, out_specs=out_specs, check_vma=False
    )
```

```python
import functools

import jax
import jax.numpy as jnp
import numpy as np
from jax import lax
from jax.experimental import pallas as pl
from jax.experimental.pallas import tpu as pltpu
from jax.sharding import PartitionSpec as P

TILE = 128
NOTHING = pl.CostEstimate(flops=0, bytes_accessed=0, transcendentals=0)
MM_COLS = 512
VMEM_LIMIT = (64 << 20) - (256 << 10)


def params():
    return pltpu.CompilerParams(vmem_limit_bytes=VMEM_LIMIT)


def pack_body(row, ids_ref, mask_ref, src_ref, amp_ref, out_ref, again_ref, used_ref):
    col_tiles = src_ref.shape[1] // TILE
    tiles = col_tiles * (src_ref.shape[0] // TILE)
    for e in range(out_ref.shape[0]):
        t = jnp.minimum(ids_ref[row[0], e], tiles - 1)
        k = pl.multiple_of(lax.div(t, col_tiles) * TILE, TILE)
        n = pl.multiple_of(lax.rem(t, col_tiles) * TILE, TILE)
        out_ref[e] = again_ref[e] = src_ref[pl.ds(k, TILE), pl.ds(n, TILE)]
    for k in range(mask_ref.shape[0]):
        for a in range(mask_ref.shape[1]):
            at = (slice(a * TILE, (a + 1) * TILE), slice(k * TILE, (k + 1) * TILE))
            scale = mask_ref[k, a].astype(jnp.float32)
            used_ref[at] = (amp_ref[at].astype(jnp.float32) * scale).astype(used_ref.dtype)


def pack(row, lists, mask, integrals, amplitudes):
    count = lists.shape[1]
    smem, vmem = pl.BlockSpec(memory_space=pltpu.SMEM), pl.BlockSpec(memory_space=pltpu.VMEM)
    return pl.pallas_call(
        pack_body,
        out_shape=[
            jax.ShapeDtypeStruct((count, TILE, TILE), integrals.dtype),
            jax.ShapeDtypeStruct((count, TILE, TILE), integrals.dtype),
            jax.ShapeDtypeStruct(amplitudes.shape, amplitudes.dtype),
        ],
        in_specs=[smem, smem, smem, vmem, vmem],
        out_specs=[vmem, vmem, vmem],
        compiler_params=params(),
        cost_estimate=NOTHING,
        name="pack_tiles",
    )(row, lists, mask.T, integrals, amplitudes)


def pick_body(first, count, capacity, scalars, target_ref, *refs):
    amps, (mine, theirs, chosen) = refs[:-3], refs[-3:]
    step = pl.program_id(0)
    slot = lax.broadcasted_iota(jnp.int32, (capacity, target_ref.shape[1]), 0)
    for d in range(count):
        wanted = scalars[first + step * count + d] * capacity + slot
        chosen[d * capacity : (d + 1) * capacity] = jnp.where(wanted == target_ref[...], 1.0, 0.0).astype(chosen.dtype)
    for at, amp in enumerate(amps):
        value = jnp.dot(chosen[...], amp[...], preferred_element_type=jnp.float32).astype(mine.dtype)
        value = value.reshape(count, capacity, amp.shape[1])

        @pl.when(step == 0)
        def _():
            theirs[at] = value

        @pl.when(step == 1)
        def _():
            mine[at] = value


def pick_rows(scalars, first, count, target, amps, capacity):
    n, k = amps[0].shape
    shape = jax.ShapeDtypeStruct((len(amps), count, capacity, k), amps[0].dtype)
    whole = pl.BlockSpec(shape.shape, lambda i, s: (0, 0, 0, 0))
    return pl.pallas_call(
        functools.partial(pick_body, first, count, capacity),
        out_shape=[shape, shape],
        grid_spec=pltpu.PrefetchScalarGridSpec(
            num_scalar_prefetch=1,
            grid=(2,),
            in_specs=[pl.BlockSpec((1, n), lambda i, s: (0, 0))]
            + [pl.BlockSpec((n, k), lambda i, s: (0, 0)) for _ in amps],
            out_specs=[whole, whole],
            scratch_shapes=[pltpu.VMEM((count * capacity, n), amps[0].dtype)],
        ),
        compiler_params=params(),
        cost_estimate=NOTHING,
        name="pick_rows",
    )(scalars, target.reshape(1, n), *amps)


class Numbers:
    def __init__(self, ref, base):
        self.ref, self.base = ref, base

    def __getitem__(self, at):
        width = self.ref.shape[1]
        return self.ref[self.base + at // width, at % width]


def product_body(at, has_acc, has_whole, final, numbers, mine, theirs, *refs):
    core_at, picks, rows_at, mine_at, theirs_at, tiles, base = at
    slot_count = len(rows_at)
    scalars = Numbers(numbers, base)
    packed_hbm = refs[:slot_count]
    acc = refs[slot_count] if has_acc else None
    refs = refs[slot_count + has_acc + has_whole :]
    outs, (lhs_all, rhs_all, packed, lhs_sem, sems) = refs[:-5], refs[-5:]
    step = pl.program_id(0)
    capacity, part = mine.shape[2:]
    depth = lhs_all.shape[1] // slot_count
    width = rhs_all.shape[1]
    count = packed.shape[1]
    col_tiles = tiles // (depth // TILE)

    @pl.when(step == 0)
    def _():
        for s in range(slot_count):
            pltpu.make_async_copy(packed_hbm[s], packed.at[s], sems.at[s]).start()
        for s in range(slot_count):
            for source, chip, side in (
                (mine, scalars[mine_at[s]], scalars[core_at]),
                (theirs, scalars[theirs_at[s]], 1 - scalars[core_at]),
            ):
                lanes = pl.ds(pl.multiple_of(s * depth + side * part, part), part)
                for t, pick in enumerate(picks):
                    pltpu.make_async_copy(
                        source.at[chip, scalars[pick]], lhs_all.at[pl.ds(t * capacity, capacity), lanes], lhs_sem
                    ).start()
        for s in range(slot_count):
            pltpu.make_async_copy(packed_hbm[s], packed.at[s], sems.at[s]).wait()
        pltpu.make_async_copy(lhs_all, lhs_all, lhs_sem).wait()

    for s in range(slot_count):
        row = scalars[rows_at[s]]
        for k in range(depth // TILE):
            for n in range(width // TILE):
                e = numbers[row, k * col_tiles + step * (width // TILE) + n]
                tile = packed[s, jnp.minimum(e, count - 1)]
                rhs_all[s * depth + k * TILE : s * depth + (k + 1) * TILE, n * TILE : (n + 1) * TILE] = jnp.where(
                    e < count, tile, jnp.zeros_like(tile)
                )
    total = jnp.dot(lhs_all[...], rhs_all[...], preferred_element_type=jnp.float32)
    if has_acc:
        total = acc[...] + total
    if not final:
        outs[0][...] = total
        return
    for t in range(len(picks)):
        outs[t][...] = total[t * capacity : (t + 1) * capacity].astype(outs[t].dtype)


def product(numbers, mine, theirs, slots, int_cols, at, acc=None, whole_cols=None, whole=None, place_at=None,
            pieces_only=False):
    picks, base = at[1], at[-1]
    capacity, part = mine.shape[2:]
    slot_count, m = len(slots), len(picks) * capacity
    depth = 2 * part
    width = min(MM_COLS, int_cols)
    steps = int_cols // width
    hbm = pl.BlockSpec(memory_space=pltpu.HBM)
    operands = [numbers, mine, theirs, *slots]
    in_specs = [hbm] * (len(operands) - 1)
    aliases = {}
    chunk = pl.BlockSpec((m, width), lambda i, numbers: (0, i))
    if acc is not None:
        in_specs.append(chunk)
        operands.append(acc)
    if whole is not None:
        aliases = {len(operands): 0}
        in_specs.append(hbm)
        operands.append(whole)
    final = pieces_only or whole_cols is not None
    out_specs = [chunk]
    out_shape = [jax.ShapeDtypeStruct((m, int_cols), jnp.float32)]
    if pieces_only:
        out_specs, out_shape = [], []
    elif final:
        out_specs = [pl.BlockSpec((capacity, width), lambda i, numbers: (0, Numbers(numbers, base)[place_at] * steps + i))]
        out_shape = [jax.ShapeDtypeStruct((capacity, whole_cols), mine.dtype)]
    for _ in picks if pieces_only else picks[1:] if final else ():
        out_specs.append(pl.BlockSpec((capacity, width), lambda i, numbers: (0, i)))
        out_shape.append(jax.ShapeDtypeStruct((capacity, int_cols), mine.dtype))
    k = slot_count * depth
    return pl.pallas_call(
        functools.partial(product_body, at, acc is not None, whole is not None, final),
        out_shape=out_shape,
        grid_spec=pltpu.PrefetchScalarGridSpec(
            num_scalar_prefetch=1,
            grid=(steps,),
            in_specs=in_specs,
            out_specs=out_specs,
            scratch_shapes=[
                pltpu.VMEM((m, k), mine.dtype),
                pltpu.VMEM((k, width), mine.dtype),
                pltpu.VMEM((slot_count, *slots[0].shape), mine.dtype),
                pltpu.SemaphoreType.DMA,
                pltpu.SemaphoreType.DMA((slot_count,)),
            ],
        ),
        input_output_aliases=aliases,
        compiler_params=params(),
        cost_estimate=NOTHING,
        name="product",
    )(*operands)


def tie_body(*refs):
    pass


def tie(value, *others):
    return pl.pallas_call(
        tie_body,
        out_shape=jax.ShapeDtypeStruct(value.shape, value.dtype),
        in_specs=[pl.BlockSpec(memory_space=pltpu.HBM)] * (1 + len(others)),
        out_specs=pl.BlockSpec(memory_space=pltpu.HBM),
        input_output_aliases={0: 0},
        compiler_params=params(),
        cost_estimate=NOTHING,
        name="tie",
    )(value, *others)


def choose_body(at, scalars, a_ref, b_ref, out_ref, sem):
    @pl.when(scalars[at] != 0)
    def _():
        pltpu.make_async_copy(a_ref, out_ref, sem).start()

    @pl.when(scalars[at] == 0)
    def _():
        pltpu.make_async_copy(b_ref, out_ref, sem).start()

    pltpu.make_async_copy(a_ref, out_ref, sem).wait()


def choose(scalars, at, a, b):
    hbm = pl.BlockSpec(memory_space=pltpu.HBM)
    return pl.pallas_call(
        functools.partial(choose_body, at),
        out_shape=jax.ShapeDtypeStruct(a.shape, a.dtype),
        in_specs=[pl.BlockSpec(memory_space=pltpu.SMEM), hbm, hbm],
        out_specs=pl.BlockSpec(memory_space=pltpu.VMEM),
        scratch_shapes=[pltpu.SemaphoreType.DMA],
        compiler_params=params(),
        cost_estimate=NOTHING,
        name="choose",
    )(scalars, a, b)


def put_body(scalars, piece_ref, whole_ref, out_ref):
    out_ref[...] = piece_ref[...]


def put(piece, whole, scalars, at):
    m, n = piece.shape
    width = min(2 * MM_COLS, n)
    steps = n // width
    return pl.pallas_call(
        put_body,
        out_shape=jax.ShapeDtypeStruct(whole.shape, whole.dtype),
        grid_spec=pltpu.PrefetchScalarGridSpec(
            num_scalar_prefetch=1,
            grid=(steps,),
            in_specs=[pl.BlockSpec((m, width), lambda i, s: (0, i)), pl.BlockSpec(memory_space=pltpu.HBM)],
            out_specs=pl.BlockSpec((m, width), lambda i, s: (0, s[at] * steps + i)),
        ),
        input_output_aliases={2: 0},
        compiler_params=params(),
        cost_estimate=NOTHING,
        name="put",
    )(scalars, piece, whole)


def col_index(ie, ia, ib, core):
    return ((ie * 2 + ia) * 2 + ib) * 2 + core


class Scalars:
    def __init__(self, rows, cols):
        self.places = [(z, me // 8, me // 4 % 2, me // 2 % 2, me % 2) for z in range(rows) for me in range(cols)]
        self.columns = []

    def add(self, value_of):
        self.columns.append([int(value_of(*place)) for place in self.places])
        return len(self.columns) - 1

    def of_device(self, z, me, cols):
        table = np.array(self.columns, np.int32).T
        return lax.dynamic_slice(jnp.asarray(table), (z * cols + me, 0), (1, table.shape[1]))[0]


def line_schedule(rows):
    if rows == 4:
        phases = [
            [(-1, [(0, 1), (1, 0), (2, 3), (3, 2)]), (-1, [(0, 2), (2, 0), (1, 3), (3, 1)])],
            [(-1, [(1, 2), (2, 1)]), (1, [(1, 0), (2, 3)])],
        ]
    else:
        partner = ({}, {})
        for i in range(rows):
            if i ^ 1 < rows:
                partner[0][i] = i ^ 1
            if 0 <= ((i + 1) ^ 1) - 1 < rows:
                partner[1][i] = ((i + 1) ^ 1) - 1
        phases, reached, last, count = [], (set(range(rows)), set(range(rows))), (-1, -1), 0
        while True:
            moves, now, fresh = [], [-1, -1], (set(), set())
            for side in (0, 1):
                pairs = [(p, i) for i, p in partner[side].items() if p in reached[1 - side]]
                fresh[side].update(i for _, i in pairs)
                if pairs:
                    moves.append((last[1 - side], pairs))
                    now[side] = count
                    count += 1
            if not moves:
                break
            phases.append(moves)
            reached, last = fresh, tuple(now)
    arrivals = [[] for _ in range(rows)]
    blocks = []
    for moves in phases:
        for source, pairs in moves:
            got = {b: a if source < 0 else blocks[source][a] for a, b in pairs}
            blocks.append(got)
            for i, block in got.items():
                arrivals[i].append((len(blocks) - 1, block))
    return phases, arrivals


def on_device(amplitudes, amp_mask, integrals, int_tiles, pair_dest):
    rows = lax.axis_size("row")
    cols = lax.axis_size("col")
    extra = cols // 8
    pair_rows, amp_cols = amplitudes.shape
    int_rows, int_cols = integrals.shape
    capacity = 2 * pair_rows // cols
    every = [(e, a, b, c) for e in range(extra) for a in range(2) for b in range(2) for c in range(2)]
    chips = [(e, a, b) for e in range(extra) for a in range(2) for b in range(2)]
    hops = [(de, turn) for de in range(extra) for turn in (0, 1)]
    turns = [(de, da, db) for de in range(extra) for da, db in ((0, 0), (1, 0), (0, 1))]
    phases, order = line_schedule(rows)

    def permute(value, moved_to):
        return lax.ppermute(value, "col", [(col_index(*at), col_index(*moved_to(*at))) for at in every])

    def along(e, a, b, c):
        return e, a ^ (c == 1), b ^ (c == 0), c

    def other(e, a, b, c):
        return e, a ^ (c == 0), b ^ (c == 1), c

    def across(e, a, b, c):
        return e, a, b, 1 - c

    consts = Scalars(rows, cols)
    core_at = consts.add(lambda z, e, a, b, c: c)
    wanted_at = len(consts.columns)
    for flip in (1, 0):
        for de, da, db in turns:
            consts.add(lambda z, e, a, b, c: col_index((e + de) % extra, a ^ da, b ^ db, c ^ flip))
    slot_rows = [lambda z: z] + [functools.partial(lambda j, z: order[z][j][1], j) for j in range(rows - 1)]
    rows_at = {
        q: [consts.add(lambda z, e, a, b, c: q * rows + row(z)) for row in slot_rows] for q in range(4)
    }
    gathered = [(de, p, q) for de in range(extra) for q in (0, 1) for p in (0, 1)]

    def arrival(chip, e, a, b, c):
        ce, ca, cb = chips[chip]
        p, q = (cb ^ b, ca ^ a) if c == 0 else (ca ^ a, cb ^ b)
        return gathered.index(((ce - e) % extra, p, q))

    mine_at = [consts.add(lambda z, e, a, b, c: arrival(row(z), e, a, b, c)) for row in slot_rows]
    theirs_at = [consts.add(lambda z, e, a, b, c: arrival(row(z), e, a, b, 1 - c)) for row in slot_rows]
    picks_at, place_at, arrive_at = {}, {}, {}
    for q in range(4):
        flip, second = int(q >= 2), q % 2
        picks_at[q] = [
            consts.add(lambda z, e, a, b, c: 3 * de + turn * (1 + (c ^ flip))) for de, turn in hops
        ]

        def block(e, a, b, kind, turn):
            return col_index(e, a ^ (second if kind else turn), b ^ (turn if kind else second), kind)

        place_at[q] = consts.add(lambda z, e, a, b, c: block(e, a, b, c ^ flip, 0))
        arrive_at[q] = [
            consts.add(lambda z, e, a, b, c: block((e - de) % extra, a, b, c ^ flip, turn)) for de, turn in hops[1:]
        ]
    flags_at = {}
    for j in range(rows - 1):
        kinds = sorted({order[i][j][0] for i in range(rows)})
        for kind in kinds[:-1]:
            flags_at[j, kind] = consts.add(lambda z, e, a, b, c: order[z][j][0] == kind)
    scalars = consts.of_device(lax.axis_index("row"), lax.axis_index("col"), cols)

    own_lists = int_tiles[:, 0, :]
    row = lax.axis_index("row").astype(jnp.int32).reshape(1)
    packed, packed_again, amp_used = pack(row, own_lists, amp_mask, integrals, amplitudes)

    moved = []

    def line_phase(moves, own):
        return [lax.ppermute(own if source < 0 else moved[source], "row", pairs) for source, pairs in moves]

    fresh = line_phase(phases[0], packed)
    count = own_lists.shape[1]
    tiles = (int_rows // TILE) * (int_cols // TILE)
    found = own_lists[:, None, :] == jnp.arange(tiles, dtype=jnp.int32)[None, :, None]
    own_table = jnp.min(jnp.where(found, jnp.arange(count, dtype=jnp.int32), count), axis=2)

    col_ids = jnp.arange(cols, dtype=jnp.int32)
    onehot = (pair_dest[:, None] == col_ids[None, :]).astype(jnp.int32)
    before = jnp.cumsum(onehot, axis=0) - onehot
    target = pair_dest * capacity + jnp.sum(before * onehot, axis=1)

    table_next = permute(own_table, along)
    slots, nexts, theirs_of, theirs_next = [packed], [permute(packed, along)], [permute(packed, across)], []
    amp_used = tie(amp_used, table_next, nexts[0])
    amp_next = permute(amp_used, along)
    amp_other = permute(amp_used, other)
    amps = [amp_used, amp_next, amp_other, permute(amp_next, other)]
    for de in range(1, extra):
        amps += [permute(amp, lambda e, a, b, c: ((e - de) % extra, a, b, c)) for amp in amps[:4]]
    pair_tables = permute(jnp.concatenate([own_table, table_next], axis=0), across)
    sums = None
    width = own_table.shape[1]
    tail = jnp.pad(scalars, (0, -scalars.shape[0] % width)).reshape(-1, width)
    numbers = jnp.concatenate([own_table, table_next, pair_tables, tail], axis=0)
    target = tie(target, numbers)
    mine, for_them = pick_rows(scalars, wanted_at, len(turns), target, amps, capacity)
    for at, moves in enumerate(phases):
        if at > 0:
            fresh = line_phase(moves, packed_again)
        if at == 0:
            waited = (mine, theirs_of[0])
            fresh[0] = tie(fresh[0], mine, fresh[1])
        elif at == 1:
            theirs = permute(for_them, across)
            waited = (theirs, nexts[-1])
        else:
            waited = (*nexts[-1:], *theirs_of[-1:])
            while len(theirs_next) < len(nexts) - 1:
                theirs_next.append(permute(nexts[len(theirs_next)], across))
                waited = (*waited, theirs_next[-1])
        if at == len(phases) - 1:
            parts = (core_at, picks_at[0], *(places[: rows - 1] for places in (rows_at[0], mine_at, theirs_at)), tiles, 4 * rows)
            (sums,) = product(numbers, mine, theirs, slots, int_cols, parts)
            waited = (*waited, sums)
            for j in range(len(theirs_next), len(nexts) - 1):
                nexts[j] = tie(nexts[j], sums)
                theirs_next.append(permute(nexts[j], across))
                waited = (*waited, theirs_next[j])
        tied = []
        for i, value in enumerate(fresh):
            if at > 0 or i > 0:
                value = tie(value, *waited, *fresh[i + 1 :], *(tied[:1] if at > 0 else ()))
            tied.append(value)
        moved += tied
        if at == 0:
            packed_again = tie(packed_again, fresh[1])
        while len(slots) < rows and all(order[i][len(slots) - 1][0] < len(moved) for i in range(rows)):
            j = len(slots) - 1
            kinds = sorted({order[i][j][0] for i in range(rows)})
            slot = moved[kinds[-1]]
            for kind in kinds[:-1]:
                slot = choose(scalars, flags_at[j, kind], moved[kind], slot)
            slots.append(slot)
            nexts.append(permute(slot, along))
            theirs_of.append(permute(slot, across))

    out = None
    arrived = []
    for turn_at, q in enumerate((0, 2, 1, 3)):
        if turn_at == 3:
            for piece, place in zip(arrived[0], arrive_at[0]):
                out = put(piece, out, scalars, place)
            theirs_next[-1] = tie(theirs_next[-1], *arrived[1], out)
        places = (rows_at[q], mine_at, theirs_at)
        blocks = (slots, nexts, theirs_of, theirs_next)[q]
        if q == 0 and rows > 1:
            blocks, places = blocks[-1:], [place[-1:] for place in places]
        call = functools.partial(product, numbers, mine, theirs, blocks, int_cols)
        own = dict(whole_cols=cols * int_cols, whole=out, place_at=place_at[q])
        if turn_at < 3:
            out, *pieces = call(
                (core_at, picks_at[q], *places, tiles, 4 * rows), acc=sums if q == 0 else None, **own
            )
        else:
            pieces = call((core_at, picks_at[q][1:], *places, tiles, 4 * rows), pieces_only=True)
        arrived.append([])
        for (de, turn), piece in zip(hops[1:], pieces):
            def sent_to(e, a, b, c):
                kind = c ^ int(q >= 2)
                return (e + de) % extra, a ^ (0 if kind else turn), b ^ (turn if kind else 0), c

            arrived[-1].append(permute(piece, sent_to))
        if q in (0, 2):
            while len(theirs_next) < rows - (q == 0):
                nexts[len(theirs_next)] = tie(nexts[len(theirs_next)], pieces[0])
                theirs_next.append(permute(nexts[len(theirs_next)], across))
    own["whole"] = tie(out, pieces[0])
    (out,) = call((core_at, picks_at[q][:1], *places, tiles, 4 * rows), **own)
    for got, q in zip(arrived[1:], (2, 1, 3)):
        for piece, place in zip(got, arrive_at[q]):
            out = put(piece, out, scalars, place)
    return out


def solution(mesh):
    in_specs = (P("row", "col"), P("row", "col"), P("row", "col"), P(None, "col", None), P("row"))
    out_specs = P(("row", "col"), None)
    return jax.shard_map(
        on_device, mesh=mesh, in_specs=in_specs, out_specs=out_specs, check_vma=False
    )
```

```python
import functools

import jax
import jax.numpy as jnp
import numpy as np
from jax import lax
from jax.experimental import pallas as pl
from jax.experimental.pallas import tpu as pltpu
from jax.sharding import PartitionSpec as P

TILE = 128
NOTHING = pl.CostEstimate(flops=0, bytes_accessed=0, transcendentals=0)
MM_COLS = 512
VMEM_LIMIT = (64 << 20) - (256 << 10)


def params():
    return pltpu.CompilerParams(vmem_limit_bytes=VMEM_LIMIT)


def pack_body(row, ids_ref, mask_ref, src_ref, amp_ref, out_ref, again_ref, used_ref):
    col_tiles = src_ref.shape[1] // TILE
    tiles = col_tiles * (src_ref.shape[0] // TILE)
    for e in range(out_ref.shape[0]):
        t = jnp.minimum(ids_ref[row[0], e], tiles - 1)
        k = pl.multiple_of(lax.div(t, col_tiles) * TILE, TILE)
        n = pl.multiple_of(lax.rem(t, col_tiles) * TILE, TILE)
        out_ref[e] = again_ref[e] = src_ref[pl.ds(k, TILE), pl.ds(n, TILE)]
    for k in range(mask_ref.shape[0]):
        for a in range(mask_ref.shape[1]):
            at = (slice(a * TILE, (a + 1) * TILE), slice(k * TILE, (k + 1) * TILE))
            scale = mask_ref[k, a].astype(jnp.float32)
            used_ref[at] = (amp_ref[at].astype(jnp.float32) * scale).astype(used_ref.dtype)


def pack(row, lists, mask, integrals, amplitudes):
    count = lists.shape[1]
    smem, vmem = pl.BlockSpec(memory_space=pltpu.SMEM), pl.BlockSpec(memory_space=pltpu.VMEM)
    return pl.pallas_call(
        pack_body,
        out_shape=[
            jax.ShapeDtypeStruct((count, TILE, TILE), integrals.dtype),
            jax.ShapeDtypeStruct((count, TILE, TILE), integrals.dtype),
            jax.ShapeDtypeStruct(amplitudes.shape, amplitudes.dtype),
        ],
        in_specs=[smem, smem, smem, vmem, vmem],
        out_specs=[vmem, vmem, vmem],
        compiler_params=params(),
        cost_estimate=NOTHING,
        name="pack_tiles",
    )(row, lists, mask.T, integrals, amplitudes)


def pick_body(first, count, capacity, scalars, target_ref, *refs):
    amps, (mine, theirs, chosen) = refs[:-3], refs[-3:]
    step = pl.program_id(0)
    slot = lax.broadcasted_iota(jnp.int32, (capacity, target_ref.shape[1]), 0)
    for d in range(count):
        wanted = scalars[first + step * count + d] * capacity + slot
        chosen[d * capacity : (d + 1) * capacity] = jnp.where(wanted == target_ref[...], 1.0, 0.0).astype(chosen.dtype)
    for at, amp in enumerate(amps):
        value = jnp.dot(chosen[...], amp[...], preferred_element_type=jnp.float32).astype(mine.dtype)
        value = value.reshape(count, capacity, amp.shape[1])

        @pl.when(step == 0)
        def _():
            theirs[at] = value

        @pl.when(step == 1)
        def _():
            mine[at] = value


def pick_rows(scalars, first, count, target, amps, capacity):
    n, k = amps[0].shape
    shape = jax.ShapeDtypeStruct((len(amps), count, capacity, k), amps[0].dtype)
    whole = pl.BlockSpec(shape.shape, lambda i, s: (0, 0, 0, 0))
    return pl.pallas_call(
        functools.partial(pick_body, first, count, capacity),
        out_shape=[shape, shape],
        grid_spec=pltpu.PrefetchScalarGridSpec(
            num_scalar_prefetch=1,
            grid=(2,),
            in_specs=[pl.BlockSpec((1, n), lambda i, s: (0, 0))]
            + [pl.BlockSpec((n, k), lambda i, s: (0, 0)) for _ in amps],
            out_specs=[whole, whole],
            scratch_shapes=[pltpu.VMEM((count * capacity, n), amps[0].dtype)],
        ),
        compiler_params=params(),
        cost_estimate=NOTHING,
        name="pick_rows",
    )(scalars, target.reshape(1, n), *amps)


class Numbers:
    def __init__(self, ref, base):
        self.ref, self.base = ref, base

    def __getitem__(self, at):
        width = self.ref.shape[1]
        return self.ref[self.base + at // width, at % width]


def product_body(at, has_acc, has_whole, final, numbers, mine, theirs, *refs):
    core_at, picks, rows_at, mine_at, theirs_at, tiles, base = at
    slot_count = len(rows_at)
    scalars = Numbers(numbers, base)
    packed_hbm = refs[:slot_count]
    acc = refs[slot_count] if has_acc else None
    refs = refs[slot_count + has_acc + has_whole :]
    outs, (lhs_all, rhs_all, packed, lhs_sem, sems) = refs[:-5], refs[-5:]
    step = pl.program_id(0)
    capacity, part = mine.shape[2:]
    depth = lhs_all.shape[1] // slot_count
    width = rhs_all.shape[1]
    count = packed.shape[1]
    col_tiles = tiles // (depth // TILE)

    @pl.when(step == 0)
    def _():
        for s in range(slot_count):
            pltpu.make_async_copy(packed_hbm[s], packed.at[s], sems.at[s]).start()
        for s in range(slot_count):
            for source, chip, side in (
                (mine, scalars[mine_at[s]], scalars[core_at]),
                (theirs, scalars[theirs_at[s]], 1 - scalars[core_at]),
            ):
                lanes = pl.ds(pl.multiple_of(s * depth + side * part, part), part)
                for t, pick in enumerate(picks):
                    pltpu.make_async_copy(
                        source.at[chip, scalars[pick]], lhs_all.at[pl.ds(t * capacity, capacity), lanes], lhs_sem
                    ).start()
        for s in range(slot_count):
            pltpu.make_async_copy(packed_hbm[s], packed.at[s], sems.at[s]).wait()
        pltpu.make_async_copy(lhs_all, lhs_all, lhs_sem).wait()

    for s in range(slot_count):
        row = scalars[rows_at[s]]
        for k in range(depth // TILE):
            for n in range(width // TILE):
                e = numbers[row, k * col_tiles + step * (width // TILE) + n]
                tile = packed[s, jnp.minimum(e, count - 1)]
                rhs_all[s * depth + k * TILE : s * depth + (k + 1) * TILE, n * TILE : (n + 1) * TILE] = jnp.where(
                    e < count, tile, jnp.zeros_like(tile)
                )
    total = jnp.dot(lhs_all[...], rhs_all[...], preferred_element_type=jnp.float32)
    if has_acc:
        total = acc[...] + total
    if not final:
        outs[0][...] = total
        return
    for t in range(len(picks)):
        outs[t][...] = total[t * capacity : (t + 1) * capacity].astype(outs[t].dtype)


def product(numbers, mine, theirs, slots, int_cols, at, acc=None, whole_cols=None, whole=None, place_at=None,
            pieces_only=False):
    picks, base = at[1], at[-1]
    capacity, part = mine.shape[2:]
    slot_count, m = len(slots), len(picks) * capacity
    depth = 2 * part
    width = min(MM_COLS, int_cols)
    steps = int_cols // width
    hbm = pl.BlockSpec(memory_space=pltpu.HBM)
    operands = [numbers, mine, theirs, *slots]
    in_specs = [hbm] * (len(operands) - 1)
    aliases = {}
    chunk = pl.BlockSpec((m, width), lambda i, numbers: (0, i))
    if acc is not None:
        in_specs.append(chunk)
        operands.append(acc)
    if whole is not None:
        aliases = {len(operands): 0}
        in_specs.append(hbm)
        operands.append(whole)
    final = pieces_only or whole_cols is not None
    out_specs = [chunk]
    out_shape = [jax.ShapeDtypeStruct((m, int_cols), jnp.float32)]
    if pieces_only:
        out_specs, out_shape = [], []
    elif final:
        out_specs = [pl.BlockSpec((capacity, width), lambda i, numbers: (0, Numbers(numbers, base)[place_at] * steps + i))]
        out_shape = [jax.ShapeDtypeStruct((capacity, whole_cols), mine.dtype)]
    for _ in picks if pieces_only else picks[1:] if final else ():
        out_specs.append(pl.BlockSpec((capacity, width), lambda i, numbers: (0, i)))
        out_shape.append(jax.ShapeDtypeStruct((capacity, int_cols), mine.dtype))
    k = slot_count * depth
    return pl.pallas_call(
        functools.partial(product_body, at, acc is not None, whole is not None, final),
        out_shape=out_shape,
        grid_spec=pltpu.PrefetchScalarGridSpec(
            num_scalar_prefetch=1,
            grid=(steps,),
            in_specs=in_specs,
            out_specs=out_specs,
            scratch_shapes=[
                pltpu.VMEM((m, k), mine.dtype),
                pltpu.VMEM((k, width), mine.dtype),
                pltpu.VMEM((slot_count, *slots[0].shape), mine.dtype),
                pltpu.SemaphoreType.DMA,
                pltpu.SemaphoreType.DMA((slot_count,)),
            ],
        ),
        input_output_aliases=aliases,
        compiler_params=params(),
        cost_estimate=NOTHING,
        name="product",
    )(*operands)


def tie_body(*refs):
    pass


def tie(value, *others):
    return pl.pallas_call(
        tie_body,
        out_shape=jax.ShapeDtypeStruct(value.shape, value.dtype),
        in_specs=[pl.BlockSpec(memory_space=pltpu.HBM)] * (1 + len(others)),
        out_specs=pl.BlockSpec(memory_space=pltpu.HBM),
        input_output_aliases={0: 0},
        compiler_params=params(),
        cost_estimate=NOTHING,
        name="tie",
    )(value, *others)


def choose_body(at, scalars, a_ref, b_ref, out_ref, sem):
    @pl.when(scalars[at] != 0)
    def _():
        pltpu.make_async_copy(a_ref, out_ref, sem).start()

    @pl.when(scalars[at] == 0)
    def _():
        pltpu.make_async_copy(b_ref, out_ref, sem).start()

    pltpu.make_async_copy(a_ref, out_ref, sem).wait()


def choose(scalars, at, a, b):
    hbm = pl.BlockSpec(memory_space=pltpu.HBM)
    return pl.pallas_call(
        functools.partial(choose_body, at),
        out_shape=jax.ShapeDtypeStruct(a.shape, a.dtype),
        in_specs=[pl.BlockSpec(memory_space=pltpu.SMEM), hbm, hbm],
        out_specs=pl.BlockSpec(memory_space=pltpu.VMEM),
        scratch_shapes=[pltpu.SemaphoreType.DMA],
        compiler_params=params(),
        cost_estimate=NOTHING,
        name="choose",
    )(scalars, a, b)


def put_body(scalars, *refs):
    pieces, out_ref = refs[:-2], refs[-1]
    for p, piece in enumerate(pieces):

        @pl.when(pl.program_id(0) == p)
        def _():
            out_ref[...] = piece[...]


def put(pieces, whole, scalars, places):
    m, n = pieces[0].shape
    width = min(2 * MM_COLS, n)
    steps = n // width

    def piece_at(p):
        return lambda i, j, s: (0, jnp.where(i == p, j, jnp.where(i < p, 0, steps - 1)))

    def out_at(i, j, s):
        place = s[places[0]]
        for p in range(1, len(places)):
            place = jnp.where(i == p, s[places[p]], place)
        return (0, place * steps + j)

    return pl.pallas_call(
        put_body,
        out_shape=jax.ShapeDtypeStruct(whole.shape, whole.dtype),
        grid_spec=pltpu.PrefetchScalarGridSpec(
            num_scalar_prefetch=1,
            grid=(len(pieces), steps),
            in_specs=[pl.BlockSpec((m, width), piece_at(p)) for p in range(len(pieces))]
            + [pl.BlockSpec(memory_space=pltpu.HBM)],
            out_specs=pl.BlockSpec((m, width), out_at),
        ),
        input_output_aliases={1 + len(pieces): 0},
        compiler_params=params(),
        cost_estimate=NOTHING,
        name="put",
    )(scalars, *pieces, whole)


def col_index(ie, ia, ib, core):
    return ((ie * 2 + ia) * 2 + ib) * 2 + core


class Scalars:
    def __init__(self, rows, cols):
        self.places = [(z, me // 8, me // 4 % 2, me // 2 % 2, me % 2) for z in range(rows) for me in range(cols)]
        self.columns = []

    def add(self, value_of):
        self.columns.append([int(value_of(*place)) for place in self.places])
        return len(self.columns) - 1

    def of_device(self, z, me, cols):
        table = np.array(self.columns, np.int32).T
        return lax.dynamic_slice(jnp.asarray(table), (z * cols + me, 0), (1, table.shape[1]))[0]


def line_schedule(rows):
    if rows == 4:
        phases = [
            [(-1, [(0, 1), (1, 0), (2, 3), (3, 2)]), (-1, [(0, 2), (2, 0), (1, 3), (3, 1)])],
            [(-1, [(1, 2), (2, 1)]), (1, [(1, 0), (2, 3)])],
        ]
    else:
        partner = ({}, {})
        for i in range(rows):
            if i ^ 1 < rows:
                partner[0][i] = i ^ 1
            if 0 <= ((i + 1) ^ 1) - 1 < rows:
                partner[1][i] = ((i + 1) ^ 1) - 1
        phases, reached, last, count = [], (set(range(rows)), set(range(rows))), (-1, -1), 0
        while True:
            moves, now, fresh = [], [-1, -1], (set(), set())
            for side in (0, 1):
                pairs = [(p, i) for i, p in partner[side].items() if p in reached[1 - side]]
                fresh[side].update(i for _, i in pairs)
                if pairs:
                    moves.append((last[1 - side], pairs))
                    now[side] = count
                    count += 1
            if not moves:
                break
            phases.append(moves)
            reached, last = fresh, tuple(now)
    arrivals = [[] for _ in range(rows)]
    blocks = []
    for moves in phases:
        for source, pairs in moves:
            got = {b: a if source < 0 else blocks[source][a] for a, b in pairs}
            blocks.append(got)
            for i, block in got.items():
                arrivals[i].append((len(blocks) - 1, block))
    return phases, arrivals


def on_device(amplitudes, amp_mask, integrals, int_tiles, pair_dest):
    rows = lax.axis_size("row")
    cols = lax.axis_size("col")
    extra = cols // 8
    pair_rows, amp_cols = amplitudes.shape
    int_rows, int_cols = integrals.shape
    capacity = 2 * pair_rows // cols
    every = [(e, a, b, c) for e in range(extra) for a in range(2) for b in range(2) for c in range(2)]
    chips = [(e, a, b) for e in range(extra) for a in range(2) for b in range(2)]
    hops = [(de, turn) for de in range(extra) for turn in (0, 1)]
    turns = [(de, da, db) for de in range(extra) for da, db in ((0, 0), (1, 0), (0, 1))]
    phases, order = line_schedule(rows)

    def permute(value, moved_to):
        return lax.ppermute(value, "col", [(col_index(*at), col_index(*moved_to(*at))) for at in every])

    def along(e, a, b, c):
        return e, a ^ (c == 1), b ^ (c == 0), c

    def other(e, a, b, c):
        return e, a ^ (c == 0), b ^ (c == 1), c

    def across(e, a, b, c):
        return e, a, b, 1 - c

    consts = Scalars(rows, cols)
    core_at = consts.add(lambda z, e, a, b, c: c)
    wanted_at = len(consts.columns)
    for flip in (1, 0):
        for de, da, db in turns:
            consts.add(lambda z, e, a, b, c: col_index((e + de) % extra, a ^ da, b ^ db, c ^ flip))
    slot_rows = [lambda z: z] + [functools.partial(lambda j, z: order[z][j][1], j) for j in range(rows - 1)]
    rows_at = {
        q: [consts.add(lambda z, e, a, b, c: q * rows + row(z)) for row in slot_rows] for q in range(4)
    }
    gathered = [(de, p, q) for de in range(extra) for q in (0, 1) for p in (0, 1)]

    def arrival(chip, e, a, b, c):
        ce, ca, cb = chips[chip]
        p, q = (cb ^ b, ca ^ a) if c == 0 else (ca ^ a, cb ^ b)
        return gathered.index(((ce - e) % extra, p, q))

    mine_at = [consts.add(lambda z, e, a, b, c: arrival(row(z), e, a, b, c)) for row in slot_rows]
    theirs_at = [consts.add(lambda z, e, a, b, c: arrival(row(z), e, a, b, 1 - c)) for row in slot_rows]
    picks_at, place_at, arrive_at = {}, {}, {}
    for q in range(4):
        flip, second = int(q >= 2), q % 2
        picks_at[q] = [
            consts.add(lambda z, e, a, b, c: 3 * de + turn * (1 + (c ^ flip))) for de, turn in hops
        ]

        def block(e, a, b, kind, turn):
            return col_index(e, a ^ (second if kind else turn), b ^ (turn if kind else second), kind)

        place_at[q] = consts.add(lambda z, e, a, b, c: block(e, a, b, c ^ flip, 0))
        arrive_at[q] = [
            consts.add(lambda z, e, a, b, c: block((e - de) % extra, a, b, c ^ flip, turn)) for de, turn in hops[1:]
        ]
    flags_at = {}
    for j in range(rows - 1):
        kinds = sorted({order[i][j][0] for i in range(rows)})
        for kind in kinds[:-1]:
            flags_at[j, kind] = consts.add(lambda z, e, a, b, c: order[z][j][0] == kind)
    scalars = consts.of_device(lax.axis_index("row"), lax.axis_index("col"), cols)

    own_lists = int_tiles[:, 0, :]
    row = lax.axis_index("row").astype(jnp.int32).reshape(1)
    packed, packed_again, amp_used = pack(row, own_lists, amp_mask, integrals, amplitudes)

    moved = []

    def line_phase(moves, own):
        return [lax.ppermute(own if source < 0 else moved[source], "row", pairs) for source, pairs in moves]

    fresh = line_phase(phases[0], packed)
    amp_next = permute(amp_used, along)
    amp_other = permute(amp_used, other)
    amps = [amp_used, amp_next, amp_other, permute(amp_next, other)]
    for de in range(1, extra):
        amps += [permute(amp, lambda e, a, b, c: ((e - de) % extra, a, b, c)) for amp in amps[:4]]

    count = own_lists.shape[1]
    tiles = (int_rows // TILE) * (int_cols // TILE)
    found = own_lists[:, None, :] == jnp.arange(tiles, dtype=jnp.int32)[None, :, None]
    own_table = jnp.min(jnp.where(found, jnp.arange(count, dtype=jnp.int32), count), axis=2)

    col_ids = jnp.arange(cols, dtype=jnp.int32)
    onehot = (pair_dest[:, None] == col_ids[None, :]).astype(jnp.int32)
    before = jnp.cumsum(onehot, axis=0) - onehot
    target = pair_dest * capacity + jnp.sum(before * onehot, axis=1)

    table_next = permute(own_table, along)
    pair_tables = permute(jnp.concatenate([own_table, table_next], axis=0), across)
    sums = None
    slots, nexts, theirs_of, theirs_next = [packed], [permute(packed, along)], [permute(packed, across)], []
    width = own_table.shape[1]
    tail = jnp.pad(scalars, (0, -scalars.shape[0] % width)).reshape(-1, width)
    numbers = jnp.concatenate([own_table, table_next, pair_tables, tail], axis=0)
    target = tie(target, numbers)
    mine, for_them = pick_rows(scalars, wanted_at, len(turns), target, amps, capacity)
    for at, moves in enumerate(phases):
        if at > 0:
            fresh = line_phase(moves, packed_again)
        if at == 0:
            waited = (mine, nexts[0], theirs_of[0])
            fresh[0] = tie(fresh[0], mine, fresh[1])
        elif at == 1:
            theirs = permute(for_them, across)
            waited = (theirs, nexts[-1])
        else:
            waited = (*nexts[-1:], *theirs_of[-1:])
            while len(theirs_next) < len(nexts) - 1:
                theirs_next.append(permute(nexts[len(theirs_next)], across))
                waited = (*waited, theirs_next[-1])
        if at == len(phases) - 1:
            parts = (core_at, picks_at[0], *(places[: rows - 1] for places in (rows_at[0], mine_at, theirs_at)), tiles, 4 * rows)
            (sums,) = product(numbers, mine, theirs, slots, int_cols, parts)
            waited = (*waited, sums)
            for j in range(len(theirs_next), len(nexts) - 1):
                nexts[j] = tie(nexts[j], sums)
                theirs_next.append(permute(nexts[j], across))
                waited = (*waited, theirs_next[j])
        tied = []
        for i, value in enumerate(fresh):
            if at > 0 or i > 0:
                value = tie(value, *waited, *fresh[i + 1 :], *(tied[:1] if at > 0 else ()))
            tied.append(value)
        moved += tied
        if at == 0:
            packed_again = tie(packed_again, fresh[1])
        while len(slots) < rows and all(order[i][len(slots) - 1][0] < len(moved) for i in range(rows)):
            j = len(slots) - 1
            kinds = sorted({order[i][j][0] for i in range(rows)})
            slot = moved[kinds[-1]]
            for kind in kinds[:-1]:
                slot = choose(scalars, flags_at[j, kind], moved[kind], slot)
            slots.append(slot)
            nexts.append(permute(slot, along))
            theirs_of.append(permute(slot, across))

    out = None
    arrived = []
    for turn_at, q in enumerate((0, 2, 1, 3)):
        if turn_at == 3:
            out = put(arrived[0], out, scalars, arrive_at[0])
            theirs_next[-1] = tie(theirs_next[-1], *arrived[1], out)
        places = (rows_at[q], mine_at, theirs_at)
        blocks = (slots, nexts, theirs_of, theirs_next)[q]
        if q == 0 and rows > 1:
            blocks, places = blocks[-1:], [place[-1:] for place in places]
        call = functools.partial(product, numbers, mine, theirs, blocks, int_cols)
        own = dict(whole_cols=cols * int_cols, whole=out, place_at=place_at[q])
        if turn_at < 3:
            out, *pieces = call(
                (core_at, picks_at[q], *places, tiles, 4 * rows), acc=sums if q == 0 else None, **own
            )
        else:
            pieces = call((core_at, picks_at[q][1:], *places, tiles, 4 * rows), pieces_only=True)
        arrived.append([])
        for (de, turn), piece in zip(hops[1:], pieces):
            def sent_to(e, a, b, c):
                kind = c ^ int(q >= 2)
                return (e + de) % extra, a ^ (0 if kind else turn), b ^ (turn if kind else 0), c

            arrived[-1].append(permute(piece, sent_to))
        if q in (0, 2):
            while len(theirs_next) < rows - (q == 0):
                nexts[len(theirs_next)] = tie(nexts[len(theirs_next)], pieces[0])
                theirs_next.append(permute(nexts[len(theirs_next)], across))
    own["whole"] = tie(out, pieces[0])
    (out,) = call((core_at, picks_at[q][:1], *places, tiles, 4 * rows), **own)
    out = put(arrived[1] + arrived[2], out, scalars, arrive_at[2] + arrive_at[1])
    out = put(arrived[3], out, scalars, arrive_at[3])
    return out


def solution(mesh):
    in_specs = (P("row", "col"), P("row", "col"), P("row", "col"), P(None, "col", None), P("row"))
    out_specs = P(("row", "col"), None)
    return jax.shard_map(
        on_device, mesh=mesh, in_specs=in_specs, out_specs=out_specs, check_vma=False
    )
```

```python
import functools

import jax
import jax.numpy as jnp
import numpy as np
from jax import lax
from jax.experimental import pallas as pl
from jax.experimental.pallas import tpu as pltpu
from jax.sharding import PartitionSpec as P

TILE = 128
NOTHING = pl.CostEstimate(flops=0, bytes_accessed=0, transcendentals=0)
MM_COLS = 512
VMEM_LIMIT = (64 << 20) - (256 << 10)


def params():
    return pltpu.CompilerParams(vmem_limit_bytes=VMEM_LIMIT)


def pack_body(row, ids_ref, mask_ref, src_ref, amp_ref, out_ref, again_ref, used_ref):
    col_tiles = src_ref.shape[1] // TILE
    tiles = col_tiles * (src_ref.shape[0] // TILE)
    for e in range(out_ref.shape[0]):
        t = jnp.minimum(ids_ref[row[0], e], tiles - 1)
        k = pl.multiple_of(lax.div(t, col_tiles) * TILE, TILE)
        n = pl.multiple_of(lax.rem(t, col_tiles) * TILE, TILE)
        out_ref[e] = again_ref[e] = src_ref[pl.ds(k, TILE), pl.ds(n, TILE)]
    for k in range(mask_ref.shape[0]):
        for a in range(mask_ref.shape[1]):
            at = (slice(a * TILE, (a + 1) * TILE), slice(k * TILE, (k + 1) * TILE))
            scale = mask_ref[k, a].astype(jnp.float32)
            used_ref[at] = (amp_ref[at].astype(jnp.float32) * scale).astype(used_ref.dtype)


def pack(row, lists, mask, integrals, amplitudes):
    count = lists.shape[1]
    smem, vmem = pl.BlockSpec(memory_space=pltpu.SMEM), pl.BlockSpec(memory_space=pltpu.VMEM)
    return pl.pallas_call(
        pack_body,
        out_shape=[
            jax.ShapeDtypeStruct((count, TILE, TILE), integrals.dtype),
            jax.ShapeDtypeStruct((count, TILE, TILE), integrals.dtype),
            jax.ShapeDtypeStruct(amplitudes.shape, amplitudes.dtype),
        ],
        in_specs=[smem, smem, smem, vmem, vmem],
        out_specs=[vmem, vmem, vmem],
        compiler_params=params(),
        cost_estimate=NOTHING,
        name="pack_tiles",
    )(row, lists, mask.T, integrals, amplitudes)


def pick_body(first, count, capacity, scalars, target_ref, *refs):
    amps, (mine, theirs, chosen) = refs[:-3], refs[-3:]
    step = pl.program_id(0)
    slot = lax.broadcasted_iota(jnp.int32, (capacity, target_ref.shape[1]), 0)
    for d in range(count):
        wanted = scalars[first + step * count + d] * capacity + slot
        chosen[d * capacity : (d + 1) * capacity] = jnp.where(wanted == target_ref[...], 1.0, 0.0).astype(chosen.dtype)
    for at, amp in enumerate(amps):
        value = jnp.dot(chosen[...], amp[...], preferred_element_type=jnp.float32).astype(mine.dtype)
        value = value.reshape(count, capacity, amp.shape[1])

        @pl.when(step == 0)
        def _():
            theirs[at] = value

        @pl.when(step == 1)
        def _():
            mine[at] = value


def pick_rows(scalars, first, count, target, amps, capacity):
    n, k = amps[0].shape
    shape = jax.ShapeDtypeStruct((len(amps), count, capacity, k), amps[0].dtype)
    whole = pl.BlockSpec(shape.shape, lambda i, s: (0, 0, 0, 0))
    return pl.pallas_call(
        functools.partial(pick_body, first, count, capacity),
        out_shape=[shape, shape],
        grid_spec=pltpu.PrefetchScalarGridSpec(
            num_scalar_prefetch=1,
            grid=(2,),
            in_specs=[pl.BlockSpec((1, n), lambda i, s: (0, 0))]
            + [pl.BlockSpec((n, k), lambda i, s: (0, 0)) for _ in amps],
            out_specs=[whole, whole],
            scratch_shapes=[pltpu.VMEM((count * capacity, n), amps[0].dtype)],
        ),
        compiler_params=params(),
        cost_estimate=NOTHING,
        name="pick_rows",
    )(scalars, target.reshape(1, n), *amps)


class Numbers:
    def __init__(self, ref, base):
        self.ref, self.base = ref, base

    def __getitem__(self, at):
        width = self.ref.shape[1]
        return self.ref[self.base + at // width, at % width]


def product_body(at, has_acc, has_whole, final, numbers, mine, theirs, *refs):
    core_at, picks, rows_at, mine_at, theirs_at, tiles, base = at
    slot_count = len(rows_at)
    scalars = Numbers(numbers, base)
    packed_hbm = refs[:slot_count]
    acc = refs[slot_count] if has_acc else None
    refs = refs[slot_count + has_acc + has_whole :]
    outs, (lhs_all, rhs_all, packed, lhs_sem, sems) = refs[:-5], refs[-5:]
    step = pl.program_id(0)
    capacity, part = mine.shape[2:]
    depth = lhs_all.shape[1] // slot_count
    width = rhs_all.shape[1]
    count = packed.shape[1]
    col_tiles = tiles // (depth // TILE)

    @pl.when(step == 0)
    def _():
        for s in range(slot_count):
            pltpu.make_async_copy(packed_hbm[s], packed.at[s], sems.at[s]).start()
        for s in range(slot_count):
            for source, chip, side in (
                (mine, scalars[mine_at[s]], scalars[core_at]),
                (theirs, scalars[theirs_at[s]], 1 - scalars[core_at]),
            ):
                lanes = pl.ds(pl.multiple_of(s * depth + side * part, part), part)
                for t, pick in enumerate(picks):
                    pltpu.make_async_copy(
                        source.at[chip, scalars[pick]], lhs_all.at[pl.ds(t * capacity, capacity), lanes], lhs_sem
                    ).start()
        for s in range(slot_count):
            pltpu.make_async_copy(packed_hbm[s], packed.at[s], sems.at[s]).wait()
        pltpu.make_async_copy(lhs_all, lhs_all, lhs_sem).wait()

    for s in range(slot_count):
        row = scalars[rows_at[s]]
        for k in range(depth // TILE):
            for n in range(width // TILE):
                e = numbers[row, k * col_tiles + step * (width // TILE) + n]
                tile = packed[s, jnp.minimum(e, count - 1)]
                rhs_all[s * depth + k * TILE : s * depth + (k + 1) * TILE, n * TILE : (n + 1) * TILE] = jnp.where(
                    e < count, tile, jnp.zeros_like(tile)
                )
    total = jnp.dot(lhs_all[...], rhs_all[...], preferred_element_type=jnp.float32)
    if has_acc:
        total = acc[...] + total
    if not final:
        outs[0][...] = total
        return
    for t in range(len(picks)):
        outs[t][...] = total[t * capacity : (t + 1) * capacity].astype(outs[t].dtype)


def product(numbers, mine, theirs, slots, int_cols, at, acc=None, whole_cols=None, whole=None, place_at=None,
            pieces_only=False):
    picks, base = at[1], at[-1]
    capacity, part = mine.shape[2:]
    slot_count, m = len(slots), len(picks) * capacity
    depth = 2 * part
    width = min(2 * MM_COLS, int_cols)
    steps = int_cols // width
    hbm = pl.BlockSpec(memory_space=pltpu.HBM)
    operands = [numbers, mine, theirs, *slots]
    in_specs = [hbm] * (len(operands) - 1)
    aliases = {}
    chunk = pl.BlockSpec((m, width), lambda i, numbers: (0, i))
    if acc is not None:
        in_specs.append(chunk)
        operands.append(acc)
    if whole is not None:
        aliases = {len(operands): 0}
        in_specs.append(hbm)
        operands.append(whole)
    final = pieces_only or whole_cols is not None
    out_specs = [chunk]
    out_shape = [jax.ShapeDtypeStruct((m, int_cols), jnp.float32)]
    if pieces_only:
        out_specs, out_shape = [], []
    elif final:
        out_specs = [pl.BlockSpec((capacity, width), lambda i, numbers: (0, Numbers(numbers, base)[place_at] * steps + i))]
        out_shape = [jax.ShapeDtypeStruct((capacity, whole_cols), mine.dtype)]
    for _ in picks if pieces_only else picks[1:] if final else ():
        out_specs.append(pl.BlockSpec((capacity, width), lambda i, numbers: (0, i)))
        out_shape.append(jax.ShapeDtypeStruct((capacity, int_cols), mine.dtype))
    k = slot_count * depth
    return pl.pallas_call(
        functools.partial(product_body, at, acc is not None, whole is not None, final),
        out_shape=out_shape,
        grid_spec=pltpu.PrefetchScalarGridSpec(
            num_scalar_prefetch=1,
            grid=(steps,),
            in_specs=in_specs,
            out_specs=out_specs,
            scratch_shapes=[
                pltpu.VMEM((m, k), mine.dtype),
                pltpu.VMEM((k, width), mine.dtype),
                pltpu.VMEM((slot_count, *slots[0].shape), mine.dtype),
                pltpu.SemaphoreType.DMA,
                pltpu.SemaphoreType.DMA((slot_count,)),
            ],
        ),
        input_output_aliases=aliases,
        compiler_params=params(),
        cost_estimate=NOTHING,
        name="product",
    )(*operands)


def tie_body(*refs):
    pass


def tie(value, *others):
    return pl.pallas_call(
        tie_body,
        out_shape=jax.ShapeDtypeStruct(value.shape, value.dtype),
        in_specs=[pl.BlockSpec(memory_space=pltpu.HBM)] * (1 + len(others)),
        out_specs=pl.BlockSpec(memory_space=pltpu.HBM),
        input_output_aliases={0: 0},
        compiler_params=params(),
        cost_estimate=NOTHING,
        name="tie",
    )(value, *others)


def choose_body(at, scalars, a_ref, b_ref, out_ref, sem):
    @pl.when(scalars[at] != 0)
    def _():
        pltpu.make_async_copy(a_ref, out_ref, sem).start()

    @pl.when(scalars[at] == 0)
    def _():
        pltpu.make_async_copy(b_ref, out_ref, sem).start()

    pltpu.make_async_copy(a_ref, out_ref, sem).wait()


def choose(scalars, at, a, b):
    hbm = pl.BlockSpec(memory_space=pltpu.HBM)
    return pl.pallas_call(
        functools.partial(choose_body, at),
        out_shape=jax.ShapeDtypeStruct(a.shape, a.dtype),
        in_specs=[pl.BlockSpec(memory_space=pltpu.SMEM), hbm, hbm],
        out_specs=pl.BlockSpec(memory_space=pltpu.VMEM),
        scratch_shapes=[pltpu.SemaphoreType.DMA],
        compiler_params=params(),
        cost_estimate=NOTHING,
        name="choose",
    )(scalars, a, b)


def put_body(scalars, *refs):
    pieces, out_ref = refs[:-2], refs[-1]
    for p, piece in enumerate(pieces):

        @pl.when(pl.program_id(0) == p)
        def _():
            out_ref[...] = piece[...]


def put(pieces, whole, scalars, places):
    m, n = pieces[0].shape
    width = min(2 * MM_COLS, n)
    steps = n // width

    def piece_at(p):
        return lambda i, j, s: (0, jnp.where(i == p, j, jnp.where(i < p, 0, steps - 1)))

    def out_at(i, j, s):
        place = s[places[0]]
        for p in range(1, len(places)):
            place = jnp.where(i == p, s[places[p]], place)
        return (0, place * steps + j)

    return pl.pallas_call(
        put_body,
        out_shape=jax.ShapeDtypeStruct(whole.shape, whole.dtype),
        grid_spec=pltpu.PrefetchScalarGridSpec(
            num_scalar_prefetch=1,
            grid=(len(pieces), steps),
            in_specs=[pl.BlockSpec((m, width), piece_at(p)) for p in range(len(pieces))]
            + [pl.BlockSpec(memory_space=pltpu.HBM)],
            out_specs=pl.BlockSpec((m, width), out_at),
        ),
        input_output_aliases={1 + len(pieces): 0},
        compiler_params=params(),
        cost_estimate=NOTHING,
        name="put",
    )(scalars, *pieces, whole)


def col_index(ie, ia, ib, core):
    return ((ie * 2 + ia) * 2 + ib) * 2 + core


class Scalars:
    def __init__(self, rows, cols):
        self.places = [(z, me // 8, me // 4 % 2, me // 2 % 2, me % 2) for z in range(rows) for me in range(cols)]
        self.columns = []

    def add(self, value_of):
        self.columns.append([int(value_of(*place)) for place in self.places])
        return len(self.columns) - 1

    def of_device(self, z, me, cols):
        table = np.array(self.columns, np.int32).T
        return lax.dynamic_slice(jnp.asarray(table), (z * cols + me, 0), (1, table.shape[1]))[0]


def line_schedule(rows):
    if rows == 4:
        phases = [
            [(-1, [(0, 1), (1, 0), (2, 3), (3, 2)]), (-1, [(0, 2), (2, 0), (1, 3), (3, 1)])],
            [(-1, [(1, 2), (2, 1)]), (1, [(1, 0), (2, 3)])],
        ]
    else:
        partner = ({}, {})
        for i in range(rows):
            if i ^ 1 < rows:
                partner[0][i] = i ^ 1
            if 0 <= ((i + 1) ^ 1) - 1 < rows:
                partner[1][i] = ((i + 1) ^ 1) - 1
        phases, reached, last, count = [], (set(range(rows)), set(range(rows))), (-1, -1), 0
        while True:
            moves, now, fresh = [], [-1, -1], (set(), set())
            for side in (0, 1):
                pairs = [(p, i) for i, p in partner[side].items() if p in reached[1 - side]]
                fresh[side].update(i for _, i in pairs)
                if pairs:
                    moves.append((last[1 - side], pairs))
                    now[side] = count
                    count += 1
            if not moves:
                break
            phases.append(moves)
            reached, last = fresh, tuple(now)
    arrivals = [[] for _ in range(rows)]
    blocks = []
    for moves in phases:
        for source, pairs in moves:
            got = {b: a if source < 0 else blocks[source][a] for a, b in pairs}
            blocks.append(got)
            for i, block in got.items():
                arrivals[i].append((len(blocks) - 1, block))
    return phases, arrivals


def on_device(amplitudes, amp_mask, integrals, int_tiles, pair_dest):
    rows = lax.axis_size("row")
    cols = lax.axis_size("col")
    extra = cols // 8
    pair_rows, amp_cols = amplitudes.shape
    int_rows, int_cols = integrals.shape
    capacity = 2 * pair_rows // cols
    every = [(e, a, b, c) for e in range(extra) for a in range(2) for b in range(2) for c in range(2)]
    chips = [(e, a, b) for e in range(extra) for a in range(2) for b in range(2)]
    hops = [(de, turn) for de in range(extra) for turn in (0, 1)]
    turns = [(de, da, db) for de in range(extra) for da, db in ((0, 0), (1, 0), (0, 1))]
    phases, order = line_schedule(rows)

    def permute(value, moved_to):
        return lax.ppermute(value, "col", [(col_index(*at), col_index(*moved_to(*at))) for at in every])

    def along(e, a, b, c):
        return e, a ^ (c == 1), b ^ (c == 0), c

    def other(e, a, b, c):
        return e, a ^ (c == 0), b ^ (c == 1), c

    def across(e, a, b, c):
        return e, a, b, 1 - c

    consts = Scalars(rows, cols)
    core_at = consts.add(lambda z, e, a, b, c: c)
    wanted_at = len(consts.columns)
    for flip in (1, 0):
        for de, da, db in turns:
            consts.add(lambda z, e, a, b, c: col_index((e + de) % extra, a ^ da, b ^ db, c ^ flip))
    slot_rows = [lambda z: z] + [functools.partial(lambda j, z: order[z][j][1], j) for j in range(rows - 1)]
    rows_at = {
        q: [consts.add(lambda z, e, a, b, c: q * rows + row(z)) for row in slot_rows] for q in range(4)
    }
    gathered = [(de, p, q) for de in range(extra) for q in (0, 1) for p in (0, 1)]

    def arrival(chip, e, a, b, c):
        ce, ca, cb = chips[chip]
        p, q = (cb ^ b, ca ^ a) if c == 0 else (ca ^ a, cb ^ b)
        return gathered.index(((ce - e) % extra, p, q))

    mine_at = [consts.add(lambda z, e, a, b, c: arrival(row(z), e, a, b, c)) for row in slot_rows]
    theirs_at = [consts.add(lambda z, e, a, b, c: arrival(row(z), e, a, b, 1 - c)) for row in slot_rows]
    picks_at, place_at, arrive_at = {}, {}, {}
    for q in range(4):
        flip, second = int(q >= 2), q % 2
        picks_at[q] = [
            consts.add(lambda z, e, a, b, c: 3 * de + turn * (1 + (c ^ flip))) for de, turn in hops
        ]

        def block(e, a, b, kind, turn):
            return col_index(e, a ^ (second if kind else turn), b ^ (turn if kind else second), kind)

        place_at[q] = consts.add(lambda z, e, a, b, c: block(e, a, b, c ^ flip, 0))
        arrive_at[q] = [
            consts.add(lambda z, e, a, b, c: block((e - de) % extra, a, b, c ^ flip, turn)) for de, turn in hops[1:]
        ]
    flags_at = {}
    for j in range(rows - 1):
        kinds = sorted({order[i][j][0] for i in range(rows)})
        for kind in kinds[:-1]:
            flags_at[j, kind] = consts.add(lambda z, e, a, b, c: order[z][j][0] == kind)
    scalars = consts.of_device(lax.axis_index("row"), lax.axis_index("col"), cols)

    own_lists = int_tiles[:, 0, :]
    row = lax.axis_index("row").astype(jnp.int32).reshape(1)
    packed, packed_again, amp_used = pack(row, own_lists, amp_mask, integrals, amplitudes)

    moved = []

    def line_phase(moves, own):
        return [lax.ppermute(own if source < 0 else moved[source], "row", pairs) for source, pairs in moves]

    fresh = line_phase(phases[0], packed)
    amp_next = permute(amp_used, along)
    amp_other = permute(amp_used, other)
    amps = [amp_used, amp_next, amp_other, permute(amp_next, other)]
    for de in range(1, extra):
        amps += [permute(amp, lambda e, a, b, c: ((e - de) % extra, a, b, c)) for amp in amps[:4]]

    count = own_lists.shape[1]
    tiles = (int_rows // TILE) * (int_cols // TILE)
    found = own_lists[:, None, :] == jnp.arange(tiles, dtype=jnp.int32)[None, :, None]
    own_table = jnp.min(jnp.where(found, jnp.arange(count, dtype=jnp.int32), count), axis=2)

    col_ids = jnp.arange(cols, dtype=jnp.int32)
    onehot = (pair_dest[:, None] == col_ids[None, :]).astype(jnp.int32)
    before = jnp.cumsum(onehot, axis=0) - onehot
    target = pair_dest * capacity + jnp.sum(before * onehot, axis=1)

    table_next = permute(own_table, along)
    pair_tables = permute(jnp.concatenate([own_table, table_next], axis=0), across)
    sums = None
    slots, nexts, theirs_of, theirs_next = [packed], [permute(packed, along)], [permute(packed, across)], []
    width = own_table.shape[1]
    tail = jnp.pad(scalars, (0, -scalars.shape[0] % width)).reshape(-1, width)
    numbers = jnp.concatenate([own_table, table_next, pair_tables, tail], axis=0)
    target = tie(target, numbers)
    mine, for_them = pick_rows(scalars, wanted_at, len(turns), target, amps, capacity)
    for at, moves in enumerate(phases):
        if at > 0:
            fresh = line_phase(moves, packed_again)
        if at == 0:
            waited = (mine, nexts[0], theirs_of[0])
            fresh[0] = tie(fresh[0], mine, fresh[1])
        elif at == 1:
            theirs = permute(for_them, across)
            waited = (theirs, nexts[-1])
        else:
            waited = (*nexts[-1:], *theirs_of[-1:])
            while len(theirs_next) < len(nexts) - 1:
                theirs_next.append(permute(nexts[len(theirs_next)], across))
                waited = (*waited, theirs_next[-1])
        if at == len(phases) - 1:
            parts = (core_at, picks_at[0], *(places[: rows - 1] for places in (rows_at[0], mine_at, theirs_at)), tiles, 4 * rows)
            (sums,) = product(numbers, mine, theirs, slots, int_cols, parts)
            waited = (*waited, sums)
            for j in range(len(theirs_next), len(nexts) - 1):
                nexts[j] = tie(nexts[j], sums)
                theirs_next.append(permute(nexts[j], across))
                waited = (*waited, theirs_next[j])
        tied = []
        for i, value in enumerate(fresh):
            if at > 0 or i > 0:
                value = tie(value, *waited, *fresh[i + 1 :], *(tied[:1] if at > 0 else ()))
            tied.append(value)
        moved += tied
        if at == 0:
            packed_again = tie(packed_again, fresh[1])
        while len(slots) < rows and all(order[i][len(slots) - 1][0] < len(moved) for i in range(rows)):
            j = len(slots) - 1
            kinds = sorted({order[i][j][0] for i in range(rows)})
            slot = moved[kinds[-1]]
            for kind in kinds[:-1]:
                slot = choose(scalars, flags_at[j, kind], moved[kind], slot)
            slots.append(slot)
            nexts.append(permute(slot, along))
            theirs_of.append(permute(slot, across))

    out = None
    arrived = []
    for turn_at, q in enumerate((0, 2, 1, 3)):
        if turn_at == 3:
            out = put(arrived[0], out, scalars, arrive_at[0])
            theirs_next[-1] = tie(theirs_next[-1], *arrived[1], out)
        places = (rows_at[q], mine_at, theirs_at)
        blocks = (slots, nexts, theirs_of, theirs_next)[q]
        if q == 0 and rows > 1:
            blocks, places = blocks[-1:], [place[-1:] for place in places]
        call = functools.partial(product, numbers, mine, theirs, blocks, int_cols)
        own = dict(whole_cols=cols * int_cols, whole=out, place_at=place_at[q])
        if turn_at < 3:
            out, *pieces = call(
                (core_at, picks_at[q], *places, tiles, 4 * rows), acc=sums if q == 0 else None, **own
            )
        else:
            pieces = call((core_at, picks_at[q][1:], *places, tiles, 4 * rows), pieces_only=True)
        arrived.append([])
        for (de, turn), piece in zip(hops[1:], pieces):
            def sent_to(e, a, b, c):
                kind = c ^ int(q >= 2)
                return (e + de) % extra, a ^ (0 if kind else turn), b ^ (turn if kind else 0), c

            arrived[-1].append(permute(piece, sent_to))
        if q in (0, 2):
            while len(theirs_next) < rows - (q == 0):
                nexts[len(theirs_next)] = tie(nexts[len(theirs_next)], pieces[0])
                theirs_next.append(permute(nexts[len(theirs_next)], across))
    own["whole"] = tie(out, pieces[0])
    (out,) = call((core_at, picks_at[q][:1], *places, tiles, 4 * rows), **own)
    out = put(arrived[1] + arrived[2], out, scalars, arrive_at[2] + arrive_at[1])
    out = put(arrived[3], out, scalars, arrive_at[3])
    return out


def solution(mesh):
    in_specs = (P("row", "col"), P("row", "col"), P("row", "col"), P(None, "col", None), P("row"))
    out_specs = P(("row", "col"), None)
    return jax.shard_map(
        on_device, mesh=mesh, in_specs=in_specs, out_specs=out_specs, check_vma=False
    )
```

```python
import functools

import jax
import jax.numpy as jnp
import numpy as np
from jax import lax
from jax.experimental import pallas as pl
from jax.experimental.pallas import tpu as pltpu
from jax.sharding import PartitionSpec as P

TILE = 128
NOTHING = pl.CostEstimate(flops=0, bytes_accessed=0, transcendentals=0)
MM_COLS = 512
VMEM_LIMIT = (64 << 20) - (256 << 10)


def params():
    return pltpu.CompilerParams(vmem_limit_bytes=VMEM_LIMIT)


def pack_body(row, ids_ref, mask_ref, src_ref, amp_ref, out_ref, again_ref, used_ref):
    col_tiles = src_ref.shape[1] // TILE
    tiles = col_tiles * (src_ref.shape[0] // TILE)
    for e in range(out_ref.shape[0]):
        t = jnp.minimum(ids_ref[row[0], e], tiles - 1)
        k = pl.multiple_of(lax.div(t, col_tiles) * TILE, TILE)
        n = pl.multiple_of(lax.rem(t, col_tiles) * TILE, TILE)
        out_ref[e] = again_ref[e] = src_ref[pl.ds(k, TILE), pl.ds(n, TILE)]
    for k in range(mask_ref.shape[0]):
        for a in range(mask_ref.shape[1]):
            at = (slice(a * TILE, (a + 1) * TILE), slice(k * TILE, (k + 1) * TILE))
            scale = mask_ref[k, a].astype(jnp.float32)
            used_ref[at] = (amp_ref[at].astype(jnp.float32) * scale).astype(used_ref.dtype)


def pack(row, lists, mask, integrals, amplitudes):
    count = lists.shape[1]
    smem, vmem = pl.BlockSpec(memory_space=pltpu.SMEM), pl.BlockSpec(memory_space=pltpu.VMEM)
    return pl.pallas_call(
        pack_body,
        out_shape=[
            jax.ShapeDtypeStruct((count, TILE, TILE), integrals.dtype),
            jax.ShapeDtypeStruct((count, TILE, TILE), integrals.dtype),
            jax.ShapeDtypeStruct(amplitudes.shape, amplitudes.dtype),
        ],
        in_specs=[smem, smem, smem, vmem, vmem],
        out_specs=[vmem, vmem, vmem],
        compiler_params=params(),
        cost_estimate=NOTHING,
        name="pack_tiles",
    )(row, lists, mask.T, integrals, amplitudes)


def pick_body(first, count, capacity, scalars, target_ref, *refs):
    amps, (mine, theirs, chosen) = refs[:-3], refs[-3:]
    step = pl.program_id(0)
    slot = lax.broadcasted_iota(jnp.int32, (capacity, target_ref.shape[1]), 0)
    for d in range(count):
        wanted = scalars[first + step * count + d] * capacity + slot
        chosen[d * capacity : (d + 1) * capacity] = jnp.where(wanted == target_ref[...], 1.0, 0.0).astype(chosen.dtype)
    for at, amp in enumerate(amps):
        value = jnp.dot(chosen[...], amp[...], preferred_element_type=jnp.float32).astype(mine.dtype)
        value = value.reshape(count, capacity, amp.shape[1])

        @pl.when(step == 0)
        def _():
            theirs[at] = value

        @pl.when(step == 1)
        def _():
            mine[at] = value


def pick_rows(scalars, first, count, target, amps, capacity):
    n, k = amps[0].shape
    shape = jax.ShapeDtypeStruct((len(amps), count, capacity, k), amps[0].dtype)
    whole = pl.BlockSpec(shape.shape, lambda i, s: (0, 0, 0, 0))
    return pl.pallas_call(
        functools.partial(pick_body, first, count, capacity),
        out_shape=[shape, shape],
        grid_spec=pltpu.PrefetchScalarGridSpec(
            num_scalar_prefetch=1,
            grid=(2,),
            in_specs=[pl.BlockSpec((1, n), lambda i, s: (0, 0))]
            + [pl.BlockSpec((n, k), lambda i, s: (0, 0)) for _ in amps],
            out_specs=[whole, whole],
            scratch_shapes=[pltpu.VMEM((count * capacity, n), amps[0].dtype)],
        ),
        compiler_params=params(),
        cost_estimate=NOTHING,
        name="pick_rows",
    )(scalars, target.reshape(1, n), *amps)


class Numbers:
    def __init__(self, ref, base):
        self.ref, self.base = ref, base

    def __getitem__(self, at):
        width = self.ref.shape[1]
        return self.ref[self.base + at // width, at % width]


def product_body(at, has_acc, has_whole, final, numbers, mine, theirs, *refs):
    core_at, picks, rows_at, mine_at, theirs_at, tiles, base = at
    slot_count = len(rows_at)
    scalars = Numbers(numbers, base)
    packed_hbm = refs[:slot_count]
    acc = refs[slot_count] if has_acc else None
    refs = refs[slot_count + has_acc + has_whole :]
    outs, (lhs_all, rhs_all, packed, lhs_sem, sems) = refs[:-5], refs[-5:]
    step = pl.program_id(0)
    capacity, part = mine.shape[2:]
    depth = lhs_all.shape[1] // slot_count
    width = rhs_all.shape[1]
    count = packed.shape[1]
    col_tiles = tiles // (depth // TILE)

    @pl.when(step == 0)
    def _():
        for s in range(slot_count):
            pltpu.make_async_copy(packed_hbm[s], packed.at[s], sems.at[s]).start()
        for s in range(slot_count):
            for source, chip, side in (
                (mine, scalars[mine_at[s]], scalars[core_at]),
                (theirs, scalars[theirs_at[s]], 1 - scalars[core_at]),
            ):
                lanes = pl.ds(pl.multiple_of(s * depth + side * part, part), part)
                for t, pick in enumerate(picks):
                    pltpu.make_async_copy(
                        source.at[chip, scalars[pick]], lhs_all.at[pl.ds(t * capacity, capacity), lanes], lhs_sem
                    ).start()
        for s in range(slot_count):
            pltpu.make_async_copy(packed_hbm[s], packed.at[s], sems.at[s]).wait()
        pltpu.make_async_copy(lhs_all, lhs_all, lhs_sem).wait()

    for s in range(slot_count):
        row = scalars[rows_at[s]]
        for k in range(depth // TILE):
            for n in range(width // TILE):
                e = numbers[row, k * col_tiles + step * (width // TILE) + n]
                tile = packed[s, jnp.minimum(e, count - 1)]
                rhs_all[s * depth + k * TILE : s * depth + (k + 1) * TILE, n * TILE : (n + 1) * TILE] = jnp.where(
                    e < count, tile, jnp.zeros_like(tile)
                )
    total = jnp.dot(lhs_all[...], rhs_all[...], preferred_element_type=jnp.float32)
    if has_acc:
        total = acc[...] + total
    if not final:
        outs[0][...] = total
        return
    for t in range(len(picks)):
        outs[t][...] = total[t * capacity : (t + 1) * capacity].astype(outs[t].dtype)


def product(numbers, mine, theirs, slots, int_cols, at, acc=None, whole_cols=None, whole=None, place_at=None,
            pieces_only=False):
    picks, base = at[1], at[-1]
    capacity, part = mine.shape[2:]
    slot_count, m = len(slots), len(picks) * capacity
    depth = 2 * part
    width = min(2 * MM_COLS, int_cols)
    steps = int_cols // width
    hbm = pl.BlockSpec(memory_space=pltpu.HBM)
    operands = [numbers, mine, theirs, *slots]
    in_specs = [hbm] * (len(operands) - 1)
    aliases = {}
    chunk = pl.BlockSpec((m, width), lambda i, numbers: (0, i))
    if acc is not None:
        in_specs.append(chunk)
        operands.append(acc)
    if whole is not None:
        aliases = {len(operands): 0}
        in_specs.append(hbm)
        operands.append(whole)
    final = pieces_only or whole_cols is not None
    out_specs = [chunk]
    out_shape = [jax.ShapeDtypeStruct((m, int_cols), jnp.float32)]
    if pieces_only:
        out_specs, out_shape = [], []
    elif final:
        out_specs = [pl.BlockSpec((capacity, width), lambda i, numbers: (0, Numbers(numbers, base)[place_at] * steps + i))]
        out_shape = [jax.ShapeDtypeStruct((capacity, whole_cols), mine.dtype)]
    for _ in picks if pieces_only else picks[1:] if final else ():
        out_specs.append(pl.BlockSpec((capacity, width), lambda i, numbers: (0, i)))
        out_shape.append(jax.ShapeDtypeStruct((capacity, int_cols), mine.dtype))
    k = slot_count * depth
    return pl.pallas_call(
        functools.partial(product_body, at, acc is not None, whole is not None, final),
        out_shape=out_shape,
        grid_spec=pltpu.PrefetchScalarGridSpec(
            num_scalar_prefetch=1,
            grid=(steps,),
            in_specs=in_specs,
            out_specs=out_specs,
            scratch_shapes=[
                pltpu.VMEM((m, k), mine.dtype),
                pltpu.VMEM((k, width), mine.dtype),
                pltpu.VMEM((slot_count, *slots[0].shape), mine.dtype),
                pltpu.SemaphoreType.DMA,
                pltpu.SemaphoreType.DMA((slot_count,)),
            ],
        ),
        input_output_aliases=aliases,
        compiler_params=params(),
        cost_estimate=NOTHING,
        name="product",
    )(*operands)


def tie_body(*refs):
    pass


def tie(value, *others):
    return pl.pallas_call(
        tie_body,
        out_shape=jax.ShapeDtypeStruct(value.shape, value.dtype),
        in_specs=[pl.BlockSpec(memory_space=pltpu.HBM)] * (1 + len(others)),
        out_specs=pl.BlockSpec(memory_space=pltpu.HBM),
        input_output_aliases={0: 0},
        compiler_params=params(),
        cost_estimate=NOTHING,
        name="tie",
    )(value, *others)


def choose_body(at, scalars, a_ref, b_ref, out_ref, sem):
    @pl.when(scalars[at] != 0)
    def _():
        pltpu.make_async_copy(a_ref, out_ref, sem).start()

    @pl.when(scalars[at] == 0)
    def _():
        pltpu.make_async_copy(b_ref, out_ref, sem).start()

    pltpu.make_async_copy(a_ref, out_ref, sem).wait()


def choose(scalars, at, a, b):
    hbm = pl.BlockSpec(memory_space=pltpu.HBM)
    return pl.pallas_call(
        functools.partial(choose_body, at),
        out_shape=jax.ShapeDtypeStruct(a.shape, a.dtype),
        in_specs=[pl.BlockSpec(memory_space=pltpu.SMEM), hbm, hbm],
        out_specs=pl.BlockSpec(memory_space=pltpu.VMEM),
        scratch_shapes=[pltpu.SemaphoreType.DMA],
        compiler_params=params(),
        cost_estimate=NOTHING,
        name="choose",
    )(scalars, a, b)


def put_body(scalars, *refs):
    pieces, out_ref = refs[:-2], refs[-1]
    for p, piece in enumerate(pieces):

        @pl.when(pl.program_id(0) == p)
        def _():
            out_ref[...] = piece[...]


def put(pieces, whole, scalars, places):
    m, n = pieces[0].shape
    width = min(MM_COLS, n)
    steps = n // width

    def piece_at(p):
        return lambda i, j, s: (0, jnp.where(i == p, j, jnp.where(i < p, 0, steps - 1)))

    def out_at(i, j, s):
        place = s[places[0]]
        for p in range(1, len(places)):
            place = jnp.where(i == p, s[places[p]], place)
        return (0, place * steps + j)

    return pl.pallas_call(
        put_body,
        out_shape=jax.ShapeDtypeStruct(whole.shape, whole.dtype),
        grid_spec=pltpu.PrefetchScalarGridSpec(
            num_scalar_prefetch=1,
            grid=(len(pieces), steps),
            in_specs=[pl.BlockSpec((m, width), piece_at(p)) for p in range(len(pieces))]
            + [pl.BlockSpec(memory_space=pltpu.HBM)],
            out_specs=pl.BlockSpec((m, width), out_at),
        ),
        input_output_aliases={1 + len(pieces): 0},
        compiler_params=params(),
        cost_estimate=NOTHING,
        name="put",
    )(scalars, *pieces, whole)


def col_index(ie, ia, ib, core):
    return ((ie * 2 + ia) * 2 + ib) * 2 + core


class Scalars:
    def __init__(self, rows, cols):
        self.places = [(z, me // 8, me // 4 % 2, me // 2 % 2, me % 2) for z in range(rows) for me in range(cols)]
        self.columns = []

    def add(self, value_of):
        self.columns.append([int(value_of(*place)) for place in self.places])
        return len(self.columns) - 1

    def of_device(self, z, me, cols):
        table = np.array(self.columns, np.int32).T
        return lax.dynamic_slice(jnp.asarray(table), (z * cols + me, 0), (1, table.shape[1]))[0]


def line_schedule(rows):
    if rows == 4:
        phases = [
            [(-1, [(0, 1), (1, 0), (2, 3), (3, 2)]), (-1, [(0, 2), (2, 0), (1, 3), (3, 1)])],
            [(-1, [(1, 2), (2, 1)]), (1, [(1, 0), (2, 3)])],
        ]
    else:
        partner = ({}, {})
        for i in range(rows):
            if i ^ 1 < rows:
                partner[0][i] = i ^ 1
            if 0 <= ((i + 1) ^ 1) - 1 < rows:
                partner[1][i] = ((i + 1) ^ 1) - 1
        phases, reached, last, count = [], (set(range(rows)), set(range(rows))), (-1, -1), 0
        while True:
            moves, now, fresh = [], [-1, -1], (set(), set())
            for side in (0, 1):
                pairs = [(p, i) for i, p in partner[side].items() if p in reached[1 - side]]
                fresh[side].update(i for _, i in pairs)
                if pairs:
                    moves.append((last[1 - side], pairs))
                    now[side] = count
                    count += 1
            if not moves:
                break
            phases.append(moves)
            reached, last = fresh, tuple(now)
    arrivals = [[] for _ in range(rows)]
    blocks = []
    for moves in phases:
        for source, pairs in moves:
            got = {b: a if source < 0 else blocks[source][a] for a, b in pairs}
            blocks.append(got)
            for i, block in got.items():
                arrivals[i].append((len(blocks) - 1, block))
    return phases, arrivals


def on_device(amplitudes, amp_mask, integrals, int_tiles, pair_dest):
    rows = lax.axis_size("row")
    cols = lax.axis_size("col")
    extra = cols // 8
    pair_rows, amp_cols = amplitudes.shape
    int_rows, int_cols = integrals.shape
    capacity = 2 * pair_rows // cols
    every = [(e, a, b, c) for e in range(extra) for a in range(2) for b in range(2) for c in range(2)]
    chips = [(e, a, b) for e in range(extra) for a in range(2) for b in range(2)]
    hops = [(de, turn) for de in range(extra) for turn in (0, 1)]
    turns = [(de, da, db) for de in range(extra) for da, db in ((0, 0), (1, 0), (0, 1))]
    phases, order = line_schedule(rows)

    def permute(value, moved_to):
        return lax.ppermute(value, "col", [(col_index(*at), col_index(*moved_to(*at))) for at in every])

    def along(e, a, b, c):
        return e, a ^ (c == 1), b ^ (c == 0), c

    def other(e, a, b, c):
        return e, a ^ (c == 0), b ^ (c == 1), c

    def across(e, a, b, c):
        return e, a, b, 1 - c

    consts = Scalars(rows, cols)
    core_at = consts.add(lambda z, e, a, b, c: c)
    wanted_at = len(consts.columns)
    for flip in (1, 0):
        for de, da, db in turns:
            consts.add(lambda z, e, a, b, c: col_index((e + de) % extra, a ^ da, b ^ db, c ^ flip))
    slot_rows = [lambda z: z] + [functools.partial(lambda j, z: order[z][j][1], j) for j in range(rows - 1)]
    rows_at = {
        q: [consts.add(lambda z, e, a, b, c: q * rows + row(z)) for row in slot_rows] for q in range(4)
    }
    gathered = [(de, p, q) for de in range(extra) for q in (0, 1) for p in (0, 1)]

    def arrival(chip, e, a, b, c):
        ce, ca, cb = chips[chip]
        p, q = (cb ^ b, ca ^ a) if c == 0 else (ca ^ a, cb ^ b)
        return gathered.index(((ce - e) % extra, p, q))

    mine_at = [consts.add(lambda z, e, a, b, c: arrival(row(z), e, a, b, c)) for row in slot_rows]
    theirs_at = [consts.add(lambda z, e, a, b, c: arrival(row(z), e, a, b, 1 - c)) for row in slot_rows]
    picks_at, place_at, arrive_at = {}, {}, {}
    for q in range(4):
        flip, second = int(q >= 2), q % 2
        picks_at[q] = [
            consts.add(lambda z, e, a, b, c: 3 * de + turn * (1 + (c ^ flip))) for de, turn in hops
        ]

        def block(e, a, b, kind, turn):
            return col_index(e, a ^ (second if kind else turn), b ^ (turn if kind else second), kind)

        place_at[q] = consts.add(lambda z, e, a, b, c: block(e, a, b, c ^ flip, 0))
        arrive_at[q] = [
            consts.add(lambda z, e, a, b, c: block((e - de) % extra, a, b, c ^ flip, turn)) for de, turn in hops[1:]
        ]
    flags_at = {}
    for j in range(rows - 1):
        kinds = sorted({order[i][j][0] for i in range(rows)})
        for kind in kinds[:-1]:
            flags_at[j, kind] = consts.add(lambda z, e, a, b, c: order[z][j][0] == kind)
    scalars = consts.of_device(lax.axis_index("row"), lax.axis_index("col"), cols)

    own_lists = int_tiles[:, 0, :]
    row = lax.axis_index("row").astype(jnp.int32).reshape(1)
    packed, packed_again, amp_used = pack(row, own_lists, amp_mask, integrals, amplitudes)

    moved = []

    def line_phase(moves, own):
        return [lax.ppermute(own if source < 0 else moved[source], "row", pairs) for source, pairs in moves]

    fresh = line_phase(phases[0], packed)
    amp_next = permute(amp_used, along)
    amp_other = permute(amp_used, other)
    amps = [amp_used, amp_next, amp_other, permute(amp_next, other)]
    for de in range(1, extra):
        amps += [permute(amp, lambda e, a, b, c: ((e - de) % extra, a, b, c)) for amp in amps[:4]]

    count = own_lists.shape[1]
    tiles = (int_rows // TILE) * (int_cols // TILE)
    found = own_lists[:, None, :] == jnp.arange(tiles, dtype=jnp.int32)[None, :, None]
    own_table = jnp.min(jnp.where(found, jnp.arange(count, dtype=jnp.int32), count), axis=2)

    col_ids = jnp.arange(cols, dtype=jnp.int32)
    onehot = (pair_dest[:, None] == col_ids[None, :]).astype(jnp.int32)
    before = jnp.cumsum(onehot, axis=0) - onehot
    target = pair_dest * capacity + jnp.sum(before * onehot, axis=1)

    table_next = permute(own_table, along)
    pair_tables = permute(jnp.concatenate([own_table, table_next], axis=0), across)
    sums = None
    slots, nexts, theirs_of, theirs_next = [packed], [permute(packed, along)], [permute(packed, across)], []
    width = own_table.shape[1]
    tail = jnp.pad(scalars, (0, -scalars.shape[0] % width)).reshape(-1, width)
    numbers = jnp.concatenate([own_table, table_next, pair_tables, tail], axis=0)
    target = tie(target, numbers)
    mine, for_them = pick_rows(scalars, wanted_at, len(turns), target, amps, capacity)
    for at, moves in enumerate(phases):
        if at > 0:
            fresh = line_phase(moves, packed_again)
        if at == 0:
            waited = (mine, nexts[0], theirs_of[0])
            fresh[0] = tie(fresh[0], mine, fresh[1])
        elif at == 1:
            theirs = permute(for_them, across)
            waited = (theirs, nexts[-1])
        else:
            waited = (*nexts[-1:], *theirs_of[-1:])
            while len(theirs_next) < len(nexts) - 1:
                theirs_next.append(permute(nexts[len(theirs_next)], across))
                waited = (*waited, theirs_next[-1])
        if at == len(phases) - 1:
            parts = (core_at, picks_at[0], *(places[: rows - 1] for places in (rows_at[0], mine_at, theirs_at)), tiles, 4 * rows)
            (sums,) = product(numbers, mine, theirs, slots, int_cols, parts)
            waited = (*waited, sums)
            for j in range(len(theirs_next), len(nexts) - 1):
                nexts[j] = tie(nexts[j], sums)
                theirs_next.append(permute(nexts[j], across))
                waited = (*waited, theirs_next[j])
        tied = []
        for i, value in enumerate(fresh):
            if at > 0 or i > 0:
                value = tie(value, *waited, *fresh[i + 1 :], *(tied[:1] if at > 0 else ()))
            tied.append(value)
        moved += tied
        if at == 0:
            packed_again = tie(packed_again, fresh[1])
        while len(slots) < rows and all(order[i][len(slots) - 1][0] < len(moved) for i in range(rows)):
            j = len(slots) - 1
            kinds = sorted({order[i][j][0] for i in range(rows)})
            slot = moved[kinds[-1]]
            for kind in kinds[:-1]:
                slot = choose(scalars, flags_at[j, kind], moved[kind], slot)
            slots.append(slot)
            nexts.append(permute(slot, along))
            theirs_of.append(permute(slot, across))

    out = None
    arrived = []
    for turn_at, q in enumerate((0, 2, 1, 3)):
        if turn_at == 3:
            out = put(arrived[0], out, scalars, arrive_at[0])
            theirs_next[-1] = tie(theirs_next[-1], *arrived[1], out)
        places = (rows_at[q], mine_at, theirs_at)
        blocks = (slots, nexts, theirs_of, theirs_next)[q]
        if q == 0 and rows > 1:
            blocks, places = blocks[-1:], [place[-1:] for place in places]
        call = functools.partial(product, numbers, mine, theirs, blocks, int_cols)
        own = dict(whole_cols=cols * int_cols, whole=out, place_at=place_at[q])
        if turn_at < 3:
            out, *pieces = call(
                (core_at, picks_at[q], *places, tiles, 4 * rows), acc=sums if q == 0 else None, **own
            )
        else:
            pieces = call((core_at, picks_at[q][1:], *places, tiles, 4 * rows), pieces_only=True)
        arrived.append([])
        for (de, turn), piece in zip(hops[1:], pieces):
            def sent_to(e, a, b, c):
                kind = c ^ int(q >= 2)
                return (e + de) % extra, a ^ (0 if kind else turn), b ^ (turn if kind else 0), c

            arrived[-1].append(permute(piece, sent_to))
        if q in (0, 2):
            while len(theirs_next) < rows - (q == 0):
                nexts[len(theirs_next)] = tie(nexts[len(theirs_next)], pieces[0])
                theirs_next.append(permute(nexts[len(theirs_next)], across))
    own["whole"] = tie(out, pieces[0])
    (out,) = call((core_at, picks_at[q][:1], *places, tiles, 4 * rows), **own)
    out = put(arrived[1] + arrived[2], out, scalars, arrive_at[2] + arrive_at[1])
    out = put(arrived[3], out, scalars, arrive_at[3])
    return out


def solution(mesh):
    in_specs = (P("row", "col"), P("row", "col"), P("row", "col"), P(None, "col", None), P("row"))
    out_specs = P(("row", "col"), None)
    return jax.shard_map(
        on_device, mesh=mesh, in_specs=in_specs, out_specs=out_specs, check_vma=False
    )
```
